32 devices in a mesh: section: 2 (over core), dp: 4 (over z), expert: 4 (over y, x).
Axes of the slice: x: 2, y: 2, z: 4, core: 2. Of those that a mesh axis runs over, the one named last changes fastest.
Arguments:
- edge_in: bfloat16 [2, 2, 4, 512, 1536], P('section', None, 'expert', 'dp'), may hold values from -6 to 6
- seg_lengths: int32 [2, 4, 13], P(None, 'expert'), may hold values from 1 to 204, 512 in all within a row
- routes: int32 [2, 2, 4, 512, 4], P('section', None, 'expert', 'dp'), may hold values from 0 to 31, all different within a row
- turns: int32 [2, 2, 4, 4, 128], P('section', None, 'expert', 'dp'), may hold values from 0 to 127, each once within a row
- attn_gain: float32 [2, 1536], P('section'), may hold values from 0.5 to 1.5
- w_query: bfloat16 [2, 1536, 1536], P('section'), may hold values from -0.3125 to 0.3125
- w_key: bfloat16 [2, 1536, 256], P('section'), may hold values from -0.15625 to 0.15625
- w_value: bfloat16 [2, 1536, 256], P('section'), may hold values from -0.15625 to 0.15625
- w_out: bfloat16 [2, 1536, 1536], P('section'), may hold values from -1.25 to 1.25
- ffn_gain: float32 [2, 1536], P('section'), may hold values from 0.5 to 1.5
- w_router: bfloat16 [2, 1536, 32], P('section'), may hold values from -0.078125 to 0.078125
- w_gate: bfloat16 [2, 32, 1536, 768], P('section', 'expert', 'dp'), may hold values from -0.15625 to 0.15625
- w_up: bfloat16 [2, 32, 1536, 768], P('section', 'expert', 'dp'), may hold values from -0.15625 to 0.15625
- w_down: bfloat16 [2, 32, 768, 1536], P('section', 'expert', 'dp'), may hold values from -0.4375 to 0.4375
Outputs:
- edge_out: float32 [2, 2, 4, 512, 1536], P('section', None, 'expert', 'dp')
- grad_attn_gain: float32 [2, 1536], P('section')
- grad_query: float32 [2, 1536, 1536], P('section')
- grad_key: float32 [2, 1536, 256], P('section')
- grad_value: float32 [2, 1536, 256], P('section')
- grad_out: float32 [2, 1536, 1536], P('section')
- grad_ffn_gain: float32 [2, 1536], P('section')
- grad_router: float32 [2, 1536, 32], P('section')
- grad_gate: float32 [2, 32, 1536, 768], P('section', 'expert', 'dp')
- grad_up: float32 [2, 32, 1536, 768], P('section', 'expert', 'dp')
- grad_down: float32 [2, 32, 768, 1536], P('section', 'expert', 'dp')
The draws below stay inside these ranges and needn't reach their ends.
Inputs may be any that keep to these rules, and one draw needn't show every extreme that they name: `seg_lengths`: each row gives the lengths of a tree's 13 segments in depth-first order: the trunk, then for each of four branches the branch followed by its two leaves; a row sums to 512. `routes`: each row names 4 different experts. `turns`: the 128 numbers of one block form a permutation.
All inputs are finite; a program needn't handle non-finite values.
Results may differ from the reference program's by a relative error of at most 0.03.
Values may be sent and summed in bfloat16 or wider, within the bound.
No kernel may reach another device: no remote copies, remote signals or barrier semaphores. Data moves between devices by JAX's collectives and lax.ppermute only.
A program may use at most 384 MiB of HBM per device.

```python
import math
import jax
import jax.numpy as jnp
import numpy as np
from jax import lax

D = 1536
QUERY_HEADS = 12
KEY_VALUE_HEADS = 2
HEAD_SIZE = 128
FFE = 768
TOPK = 4
MICRO = 2
SEGS = 13
TOK_DEV = 128
EXPERTS = 32
TREE = 512
BLOCKS = 4
GROUPS = 4
LAYERS = 2
CAP = 16
QW = 1536
KW = 256


def shard_levels(stream_key, shape, shards, low, high):
    factor_of, own = 1.0, jax.random.fold_in(stream_key, 6)
    for axis_at, shards_of in shards:
        draws = jnp.exp(jax.random.uniform(jax.random.fold_in(own, axis_at), (shards_of,), jnp.float32, low / len(shards), high / len(shards)))
        factor_of = factor_of * jnp.repeat(draws, shape[axis_at] // shards_of).reshape([-1 if axis == axis_at else 1 for axis in range(len(shape))])
    return factor_of


def different_ones(stream_key, rows, amount, top, lift):
    order = jax.random.permutation(jax.random.fold_in(stream_key, 1), amount)
    favour = order
    for power in range(3):
        favour = favour * favour // amount
    favour = favour * lift // amount
    lots = jax.random.randint(jax.random.fold_in(stream_key, 2), (rows, amount), 0, 4096) + favour
    sure = jax.random.permutation(jax.random.fold_in(stream_key, 3), rows)[jnp.arange(amount) % rows]
    lots = jnp.where(jnp.arange(rows)[:, None] == sure[None, :], 1 << 14, lots)
    merit = lots * amount + jnp.arange(amount)
    return lax.top_k(merit.astype(jnp.int32), top)[1].astype(jnp.int32)


def profile(count, total, reach, skew):
    weights = [(1 << 20) // math.isqrt(standing ** skew) + 1 for standing in range(2, count + 1)]
    surplus, given = total - reach - (count - 1), [1] * (count - 1)
    while surplus > 0:
        movable = [i for i in range(count - 1) if given[i] < reach]
        whole, remaining = sum([weights[i] for i in movable]), surplus
        for i in movable:
            more = min(reach - given[i], max(1, remaining * weights[i] // whole), surplus)
            given[i] = given[i] + more
            surplus = surplus - more
    return np.array([reach] + given)


def uneven(stream_key, count, total, limit, skew):
    if count == 2:
        one = jax.random.randint(stream_key, (), max(1, total - limit), min(limit, total - 1) + 1)
        return jnp.stack([one, total - one])
    lengths = jnp.asarray(profile(count, total, limit, skew), jnp.int32)
    pairs = (count - 1) // 2
    giver, receiver = lengths[1:1 + 2 * pairs:2], lengths[2:2 + 2 * pairs:2]
    slack = jnp.minimum(giver - 1, limit - receiver)
    shifted = jax.random.randint(jax.random.fold_in(stream_key, 1), (pairs,), 0, 1 << 20) % (slack + 1)
    lengths = lengths.at[1:1 + 2 * pairs:2].set(giver - shifted).at[2:2 + 2 * pairs:2].set(receiver + shifted)
    return lengths[jax.random.permutation(jax.random.fold_in(stream_key, 2), count)]


def noise(stream_key, extent, deviation, reach, split=(), held_as=jnp.bfloat16):
    drawn = jax.random.normal(stream_key, extent, jnp.float32) * deviation
    if len(split) > 0:
        drawn = shard_levels(stream_key, extent, split, -0.22, 0.18) * drawn
    return jnp.clip(drawn, min=-reach, max=reach).astype(held_as)


def setup_inputs(seed: int = 0) -> dict:
    keys = jax.random.split(jax.random.key(seed), 15)
    edge_in = noise(keys[0], (LAYERS, MICRO, GROUPS, TREE, D), 1.0, 6.0, ((0, 2), (2, 4), (3, 4)))
    seg_lengths = jax.vmap(lambda own: uneven(own, SEGS, TREE, TREE * 2 // 5, 2))(jax.random.split(keys[1], MICRO * GROUPS)).reshape((MICRO, GROUPS, SEGS)).astype(jnp.int32)
    routes = different_ones(keys[2], LAYERS * MICRO * GROUPS * TREE, EXPERTS, TOPK, 1024).reshape((LAYERS, MICRO, GROUPS, TREE, TOPK))
    turns = jax.vmap(lambda own: jax.random.permutation(own, TOK_DEV))(jax.random.split(keys[3], LAYERS * MICRO * GROUPS * BLOCKS)).reshape((LAYERS, MICRO, GROUPS, BLOCKS, TOK_DEV)).astype(jnp.int32)
    attn_gain = jnp.clip(1.0 + 0.1 * jax.random.normal(keys[4], (LAYERS, D), jnp.float32), 0.5, 1.5)
    w_query = noise(keys[5], (LAYERS, D, QW), (D // 4) ** -0.5, 0.3125, ((0, 2),))
    w_key = noise(keys[6], (LAYERS, D, KW), D ** -0.5, 0.15625, ((0, 2),))
    w_value = noise(keys[7], (LAYERS, D, KW), D ** -0.5, 0.15625, ((0, 2),))
    w_out = noise(keys[8], (LAYERS, QW, D), (QW // 64) ** -0.5, 1.25, ((0, 2),))
    ffn_gain = jnp.clip(1.0 + 0.1 * jax.random.normal(keys[9], (LAYERS, D), jnp.float32), 0.5, 1.5)
    w_router = noise(keys[10], (LAYERS, D, EXPERTS), (4 * D) ** -0.5, 0.078125, ((0, 2),))
    w_gate = noise(keys[11], (LAYERS, EXPERTS, D, FFE), D ** -0.5, 0.15625, ((0, 2), (1, 4), (2, 4)))
    w_up = noise(keys[12], (LAYERS, EXPERTS, D, FFE), D ** -0.5, 0.15625, ((0, 2), (1, 4), (2, 4)))
    w_down = noise(keys[13], (LAYERS, EXPERTS, FFE, D), (FFE // 4) ** -0.5, 0.4375, ((0, 2), (1, 4), (2, 4)))
    return dict(edge_in=edge_in, seg_lengths=seg_lengths, routes=routes, turns=turns, attn_gain=attn_gain, w_query=w_query, w_key=w_key, w_value=w_value, w_out=w_out, ffn_gain=ffn_gain, w_router=w_router, w_gate=w_gate, w_up=w_up, w_down=w_down)


epsilon = 1e-06
masked_score = -1e+30

@jax.custom_vjp
def low(v):
    return lax.optimization_barrier(v.astype(jnp.bfloat16)).astype(jnp.float32)

@jax.custom_vjp
def low_back(v):
    return v

def low_keep(v):
    return (low(v), None)

def low_pass(kept, grad):
    return (grad,)

def back_keep(v):
    return (v, None)

def back_low(kept, grad):
    return (low(grad),)
low.defvjp(low_keep, low_pass)
low_back.defvjp(back_keep, back_low)

def ancestry():
    parents = [-1]
    for branch_index in range(4):
        parents += [0, 1 + 3 * branch_index, 1 + 3 * branch_index]
    lineage = np.zeros((13, 13), np.float32)
    for segment in range(13):
        current = segment
        while current >= 0:
            lineage[current, segment] = 1.0
            current = parents[current]
    return lineage

def product(left, right):
    return jnp.dot(left, right, precision=lax.Precision.HIGHEST)

def norm(values, gain_vec):
    return values * lax.rsqrt(lax.optimization_barrier(jnp.mean(values * values, -1, keepdims=True)) + epsilon) * gain_vec

def attention(queries, key_row_block, value_row_block, lengths_row):
    tree_length = queries.shape[0]
    seg_ends = jnp.cumsum(lengths_row)
    spots = jnp.arange(tree_length, dtype=jnp.int32)
    seg_index = lax.optimization_barrier(jnp.sum((spots[:, None] >= seg_ends[None, :]).astype(jnp.int32), 1))
    seg_hot = (seg_index[:, None] == jnp.arange(13, dtype=jnp.int32)[None, :]).astype(jnp.float32)
    allowed = product(seg_hot, jnp.asarray(ancestry()))
    query_tile_block = math.gcd(tree_length, 512)
    key_per_head = key_row_block.reshape(tree_length, KEY_VALUE_HEADS, HEAD_SIZE)
    value_per_head = value_row_block.reshape(tree_length, KEY_VALUE_HEADS, HEAD_SIZE)

    def one_block(block_items):
        query_row_block, allowed_rows, query_spots = block_items
        linked = product(allowed_rows, seg_hot.T) > 0.5
        visible = linked & (spots[None, :] <= query_spots[:, None])
        grouped_query = query_row_block.reshape(query_tile_block, KEY_VALUE_HEADS, QUERY_HEADS // KEY_VALUE_HEADS, HEAD_SIZE)
        raw = jnp.einsum('tkgd,skd->kgts', grouped_query, key_per_head, precision=lax.Precision.HIGHEST) * HEAD_SIZE ** (-0.5)
        scores = jnp.where(visible[None, None], low_back(raw), masked_score)
        attn_prob = low(jnp.exp(scores - jax.nn.logsumexp(scores, -1, keepdims=True)))
        attn_mix = jnp.einsum('kgts,skd->tkgd', attn_prob, value_per_head, precision=lax.Precision.HIGHEST)
        return low(low_back(attn_mix.reshape(query_tile_block, QUERY_HEADS * HEAD_SIZE)))
    mixed_blocks = lax.map(jax.checkpoint(one_block), (queries.reshape(-1, query_tile_block, QUERY_HEADS * HEAD_SIZE), allowed.reshape(-1, query_tile_block, 13), spots.reshape(-1, query_tile_block)))
    return mixed_blocks.reshape(tree_length, QUERY_HEADS * HEAD_SIZE)

def mixture(hidden_two, route_rows, turn_rows, w_router, w_gate, w_up, w_down):
    logits = low_back(product(hidden_two, w_router))
    chosen_hot = (route_rows[:, :, None] == jnp.arange(EXPERTS, dtype=jnp.int32)[None, None, :]).astype(jnp.float32)
    chosen = lax.optimization_barrier(jnp.sum(chosen_hot * logits[:, None, :], -1))
    gate_share = jax.nn.softmax(chosen, -1)
    hot_blocks = chosen_hot.reshape(BLOCKS, TOK_DEV, TOPK, EXPERTS)
    assigned = lax.optimization_barrier(jnp.sum(hot_blocks, 2))
    earlier = (turn_rows[:, None, :] < turn_rows[:, :, None]).astype(jnp.float32)
    places = jnp.einsum('bst,bte->bse', earlier, assigned, precision=lax.Precision.HIGHEST)
    slot_of = lax.optimization_barrier(jnp.sum(hot_blocks * places[:, :, None, :], -1))
    kept_pick = (slot_of < CAP).astype(jnp.float32)
    target = route_rows.reshape(BLOCKS, TOK_DEV, TOPK).astype(jnp.float32) * CAP + slot_of
    slot_ids = jnp.arange(EXPERTS * CAP, dtype=jnp.float32)
    selector = kept_pick[..., None] * (target[..., None] == slot_ids).astype(jnp.float32)
    block_rows = hidden_two.reshape(BLOCKS, TOK_DEV, D)
    buffers = jnp.einsum('btkj,btd->bjd', selector, block_rows, precision=lax.Precision.HIGHEST)
    buffers = low_back(buffers.reshape(BLOCKS, EXPERTS, CAP, D))
    gate_pre = low_back(jnp.einsum('becd,edf->becf', buffers, w_gate, precision=lax.Precision.HIGHEST))
    up_pre = low_back(jnp.einsum('becd,edf->becf', buffers, w_up, precision=lax.Precision.HIGHEST))
    inner_act = low(jax.nn.silu(gate_pre) * up_pre)
    produced = low(low_back(jnp.einsum('becf,efd->becd', inner_act, w_down, precision=lax.Precision.HIGHEST)))
    pulled = jnp.einsum('btkj,bjd->btkd', selector, produced.reshape(BLOCKS, EXPERTS * CAP, D), precision=lax.Precision.HIGHEST)
    weighting = gate_share.reshape(BLOCKS, TOK_DEV, TOPK) * kept_pick
    return lax.optimization_barrier(jnp.sum(weighting[..., None] * pulled, 2)).reshape(-1, D)

def layer(layer_in, lengths_row, route_rows, turn_rows, weights):
    attn_gain, w_query, w_key, w_value, w_out, ffn_gain, w_router, w_gate, w_up, w_down = weights
    hidden_one = low(norm(layer_in, attn_gain))
    queries = low(low_back(product(hidden_one, w_query)))
    key_row_block = low(low_back(product(hidden_one, w_key)))
    value_row_block = low(low_back(product(hidden_one, w_value)))
    attn_mix = attention(queries, key_row_block, value_row_block, lengths_row)
    middle = layer_in + low_back(product(attn_mix, w_out))
    hidden_two = low(norm(middle, ffn_gain))
    return middle + mixture(hidden_two, route_rows, turn_rows, w_router, w_gate, w_up, w_down)

def reference(edge_in, seg_lengths, routes, turns, attn_gain, w_query, w_key, w_value, w_out, ffn_gain, w_router, w_gate, w_up, w_down):
    weights = tuple((weight_arg.astype(jnp.float32) for weight_arg in (attn_gain, w_query, w_key, w_value, w_out, ffn_gain, w_router, w_gate, w_up, w_down)))
    starts = edge_in[0].astype(jnp.float32).reshape(MICRO * GROUPS, TREE, D)
    cotangent = edge_in[1].astype(jnp.float32).reshape(MICRO * GROUPS, TREE, D)
    lengths_flat = seg_lengths.reshape(MICRO * GROUPS, SEGS)
    routes_flat = jnp.moveaxis(routes, 0, 2).reshape(MICRO * GROUPS, LAYERS, TREE, TOPK)
    turns_flat = jnp.moveaxis(turns, 0, 2).reshape(MICRO * GROUPS, LAYERS, BLOCKS, TOK_DEV)

    def forward(starts, weights):

        def one_tree(tree_items):
            state, lengths_row, route_rows, turn_rows = tree_items
            for layer_index in range(LAYERS):
                layer_weights = tuple((piece[layer_index] for piece in weights))
                state = layer(state, lengths_row, route_rows[layer_index], turn_rows[layer_index], layer_weights)
                if layer_index + 1 < LAYERS:
                    state = low(low_back(state))
            return state
        return lax.map(jax.checkpoint(one_tree), (starts, lengths_flat, routes_flat, turns_flat))
    outputs, pullback = jax.vjp(forward, starts, weights)
    grad_starts, grad_weights = pullback(cotangent)
    edge_out = jnp.stack([grad_starts, outputs]).reshape(LAYERS, MICRO, GROUPS, TREE, D)
    return (edge_out,) + tuple(grad_weights)
```

```python
import jax
import jax.numpy as jnp
import numpy as np
from jax import lax
from jax.sharding import PartitionSpec as P

HEAD_SIZE = 128
SCALE = HEAD_SIZE ** (-0.5)
epsilon = 1e-06
masked_score = -1e30
BF = jnp.bfloat16
F32 = jnp.float32

SWAP = [(0, 1), (1, 0)]
UP = [(0, 1)]
DOWN = [(1, 0)]
OWNERS = ("expert", "dp", "section")
LINE = ("dp", "section")
REPLICAS = ("dp", "expert")


def ancestry():
    parents = [-1]
    for branch_index in range(4):
        parents += [0, 1 + 3 * branch_index, 1 + 3 * branch_index]
    lineage = np.zeros((13, 13), np.float32)
    for segment in range(13):
        current = segment
        while current >= 0:
            lineage[current, segment] = 1.0
            current = parents[current]
    return lineage


def dot(left, right):
    return jnp.dot(left, right, preferred_element_type=F32)


def dot_t(left, right):
    return lax.dot_general(left, right, (((1,), (1,)), ((), ())), preferred_element_type=F32)


def t_dot(left, right):
    return lax.dot_general(left, right, (((0,), (0,)), ((), ())), preferred_element_type=F32)


def normalize(values, gain_vec):
    factor = lax.rsqrt(jnp.mean(values * values, -1, keepdims=True) + epsilon)
    return (values * factor * gain_vec, factor)


def norm_back(values, factor, gain_vec, upstream):
    scaled = upstream * gain_vec
    grad_gain = jnp.sum(upstream * values * factor, 0)
    inner_mean = jnp.mean(scaled * values, -1, keepdims=True)
    return (scaled * factor - values * factor * factor * factor * inner_mean, grad_gain)


def tree_mask(lengths_row, first_row, local_len, tree_length):
    seg_ends = jnp.cumsum(lengths_row)
    key_spots = jnp.arange(tree_length, dtype=jnp.int32)
    query_spots = first_row + jnp.arange(local_len, dtype=jnp.int32)
    seg_ids = jnp.arange(13, dtype=jnp.int32)
    key_seg = jnp.sum((key_spots[:, None] >= seg_ends[None, :]).astype(jnp.int32), 1)
    query_seg = jnp.sum((query_spots[:, None] >= seg_ends[None, :]).astype(jnp.int32), 1)
    key_hot = (key_seg[:, None] == seg_ids[None, :]).astype(BF)
    query_hot = (query_seg[:, None] == seg_ids[None, :]).astype(BF)
    allowed = dot(query_hot, jnp.asarray(ancestry(), BF)).astype(BF)
    linked = dot_t(allowed, key_hot) > 0.5
    return linked & (key_spots[None, :] <= query_spots[:, None])


def exchange(shard, axes):
    return lax.all_to_all(shard, axes, split_axis=0, concat_axis=0, tiled=True)


def swapped(shard):
    return lax.ppermute(shard, "section", SWAP)


def gather_rows(shard):
    size = lax.axis_size("dp")
    copies = jnp.broadcast_to(shard[None], (size,) + shard.shape)
    return exchange(copies, "dp").reshape((-1,) + shard.shape[1:])


def sum_to_owner(partial):
    size = lax.axis_size("dp")
    blocks = exchange(partial.reshape((size, -1) + partial.shape[1:]), "dp")
    return jnp.sum(blocks.astype(F32), 0)


def layer_forward(layer_in, visible, route_rows, turn_row, dense_set, expert_set):
    attn_gain, w_query, w_key, w_value, w_out, ffn_gain, w_router = dense_set
    w_gate, w_up, w_down = expert_set
    local_len, width = layer_in.shape
    heads_kv = w_key.shape[1] // HEAD_SIZE
    experts_all = w_router.shape[1]
    pick_count = route_rows.shape[1]
    capacity = local_len * pick_count // experts_all
    slots = experts_all * capacity
    normed, factor_one = normalize(layer_in, attn_gain)
    hidden_one = normed.astype(BF)
    queries = dot(hidden_one, w_query).astype(BF)
    key_rows = dot(hidden_one, w_key).astype(BF)
    value_rows = dot(hidden_one, w_value).astype(BF)
    kv_all = gather_rows(jnp.concatenate([key_rows, value_rows], 1))
    key_width = w_key.shape[1]
    key_all = kv_all[:, :key_width].reshape(-1, heads_kv, HEAD_SIZE)
    value_all = kv_all[:, key_width:].reshape(-1, heads_kv, HEAD_SIZE)
    grouped_query = queries.reshape(local_len, heads_kv, -1, HEAD_SIZE)
    raw = jnp.einsum("tkgd,skd->kgts", grouped_query, key_all, preferred_element_type=F32) * SCALE
    scores = jnp.where(visible[None, None], raw, masked_score)
    log_total = jax.nn.logsumexp(scores, -1, keepdims=True)
    attn_prob = jnp.exp(scores - log_total)
    attn_mix = jnp.einsum(
        "kgts,skd->tkgd", attn_prob.astype(BF), value_all, preferred_element_type=F32
    )
    attn_mix = attn_mix.reshape(local_len, -1).astype(BF)
    middle = layer_in + dot(attn_mix, w_out)
    normed_two, factor_two = normalize(middle, ffn_gain)
    hidden_two = normed_two.astype(BF)
    logits = dot(hidden_two, w_router)
    expert_ids = jnp.arange(experts_all, dtype=jnp.int32)
    chosen = jnp.any(route_rows[:, :, None] == expert_ids[None, None, :], 1)
    masked_logits = jnp.where(chosen, logits, masked_score)
    top = jnp.max(masked_logits, -1, keepdims=True)
    powers = jnp.where(chosen, jnp.exp(masked_logits - top), 0.0)
    gate_share = powers / jnp.sum(powers, -1, keepdims=True)
    earlier = (turn_row[None, :] < turn_row[:, None]).astype(BF)
    places = dot(earlier, chosen.astype(BF))
    place_of = jnp.where(chosen & (places < capacity), places, -1.0).astype(BF)
    slot_ids = jnp.arange(slots, dtype=jnp.int32)
    spread = (slot_ids[None, :] // capacity == expert_ids[:, None]).astype(BF)
    rank = (slot_ids % capacity).astype(F32)
    selected = dot(place_of, spread) == rank[None, :]
    selector = selected.astype(BF)
    weighting = jnp.where(selected, dot(gate_share.astype(BF), spread), 0.0).astype(BF)
    outgoing = t_dot(selector, hidden_two).astype(BF)
    arrived = send_out(outgoing, experts_all, capacity)
    gate_pre = dot(arrived, w_gate)
    up_pre = dot(arrived, w_up)
    inner_act = (jax.nn.silu(gate_pre) * up_pre).astype(BF)
    produced = dot(inner_act, w_down).astype(BF)
    returned = send_back(produced, experts_all, capacity)
    result = middle + dot(weighting, returned)
    stored = {
        "layer_in": layer_in,
        "factor_one": factor_one,
        "hidden_one": hidden_one,
        "queries": queries,
        "key_all": key_all,
        "value_all": value_all,
        "attn_prob": attn_prob,
        "attn_mix": attn_mix,
        "middle": middle,
        "factor_two": factor_two,
        "hidden_two": hidden_two,
        "gate_share": gate_share,
        "selected": selected,
        "spread": spread,
        "weighting": weighting,
        "arrived": arrived,
        "gate_pre": gate_pre,
        "up_pre": up_pre,
        "inner_act": inner_act,
        "returned": returned,
    }
    return (result, stored)


def copies_of_expert(experts_all):
    owners = lax.axis_size("expert") * lax.axis_size("dp") * lax.axis_size("section")
    return owners // experts_all


def send_out(slot_rows, experts_all, capacity):
    width = slot_rows.shape[-1]
    copies = copies_of_expert(experts_all)
    rows = slot_rows.reshape(experts_all, capacity, width)
    if copies > 1:
        mine = jnp.arange(copies) == lax.axis_index("dp") % copies
        rows = jnp.where(mine[None, :, None, None], rows[:, None], 0).reshape(-1, capacity, width)
    return exchange(rows, OWNERS).reshape(-1, width)


def send_back(rows, experts_all, capacity):
    width = rows.shape[-1]
    copies = copies_of_expert(experts_all)
    rows = exchange(rows.reshape(-1, capacity, width), OWNERS)
    if copies > 1:
        mine = lax.axis_index("dp") % copies
        rows = lax.dynamic_index_in_dim(
            rows.reshape(experts_all, copies, capacity, width), mine, 1, False
        )
    return rows.reshape(-1, width)


def layer_backward(stored, grad_top, dense_set, expert_set):
    attn_gain, w_query, w_key, w_value, w_out, ffn_gain, w_router = dense_set
    w_gate, w_up, w_down = expert_set
    local_len = grad_top.shape[0]
    experts_all = w_router.shape[1]
    slots = stored["selected"].shape[1]
    capacity = slots // experts_all
    gate_share = stored["gate_share"]
    slot_grads = t_dot(stored["weighting"], grad_top).astype(BF)
    slot_owed = send_out(slot_grads, experts_all, capacity)
    match = jnp.where(stored["selected"], dot_t(grad_top, stored["returned"]), 0.0)
    grad_weighting = lax.dot_general(
        match,
        stored["spread"].astype(F32),
        (((1,), (1,)), ((), ())),
        precision=lax.Precision.HIGHEST,
        preferred_element_type=F32,
    )
    grad_logits = (
        gate_share * (grad_weighting - jnp.sum(gate_share * grad_weighting, -1, keepdims=True))
    ).astype(BF)
    grad_router = t_dot(stored["hidden_two"], grad_logits)
    grad_hidden = dot_t(grad_logits, w_router)
    gate_pre = stored["gate_pre"]
    up_pre = stored["up_pre"]
    grad_inner = dot_t(slot_owed, w_down)
    sigmoid_a = jax.nn.sigmoid(gate_pre)
    grad_gate_pre = (grad_inner * up_pre * sigmoid_a * (1.0 + gate_pre * (1.0 - sigmoid_a))).astype(
        BF
    )
    grad_up_pre = (grad_inner * gate_pre * sigmoid_a).astype(BF)
    grad_arrived = (dot_t(grad_gate_pre, w_gate) + dot_t(grad_up_pre, w_up)).astype(BF)
    sent_back = send_back(grad_arrived, experts_all, capacity)
    arrived = stored["arrived"]
    grad_down = t_dot(stored["inner_act"], slot_owed)
    grad_gate = t_dot(arrived, grad_gate_pre)
    grad_up = t_dot(arrived, grad_up_pre)
    grad_hidden = grad_hidden + dot(stored["selected"].astype(BF), sent_back)
    grad_normed_two, grad_ffn_gain = norm_back(
        stored["middle"], stored["factor_two"], ffn_gain, grad_hidden
    )
    grad_middle = grad_top.astype(F32) + grad_normed_two
    grad_branch = grad_middle.astype(BF)
    grad_w_out = t_dot(stored["attn_mix"], grad_branch)
    grad_mix = dot_t(grad_branch, w_out).astype(BF)
    key_all = stored["key_all"]
    value_all = stored["value_all"]
    heads_kv = key_all.shape[1]
    attn_prob = stored["attn_prob"]
    grouped_grad = grad_mix.reshape(local_len, heads_kv, -1, HEAD_SIZE)
    grad_prob = jnp.einsum("tkgd,skd->kgts", grouped_grad, value_all, preferred_element_type=F32)
    centre = jnp.sum(attn_prob * grad_prob, -1, keepdims=True)
    grad_scores = (attn_prob * (grad_prob - centre)).astype(BF)
    grad_queries = (
        jnp.einsum("kgts,skd->tkgd", grad_scores, key_all, preferred_element_type=F32) * SCALE
    )
    grad_queries = grad_queries.reshape(local_len, -1).astype(BF)
    grouped_query = stored["queries"].reshape(local_len, heads_kv, -1, HEAD_SIZE)
    grad_keys_all = (
        jnp.einsum("kgts,tkgd->skd", grad_scores, grouped_query, preferred_element_type=F32) * SCALE
    )
    grad_values_all = jnp.einsum(
        "kgts,tkgd->skd", attn_prob.astype(BF), grouped_grad, preferred_element_type=F32
    )
    tree_length = key_all.shape[0]
    grad_kv = sum_to_owner(
        jnp.concatenate(
            [grad_keys_all.reshape(tree_length, -1), grad_values_all.reshape(tree_length, -1)], 1
        ).astype(BF)
    ).astype(BF)
    key_width = w_key.shape[1]
    grad_keys, grad_values = grad_kv[:, :key_width], grad_kv[:, key_width:]
    hidden_one = stored["hidden_one"]
    grad_query_w = t_dot(hidden_one, grad_queries)
    grad_key_w = t_dot(hidden_one, grad_keys)
    grad_value_w = t_dot(hidden_one, grad_values)
    grad_hidden_one = dot_t(grad_queries, w_query)
    grad_hidden_one = grad_hidden_one + dot_t(grad_keys, w_key)
    grad_hidden_one = grad_hidden_one + dot_t(grad_values, w_value)
    grad_normed_one, grad_attn_gain = norm_back(
        stored["layer_in"], stored["factor_one"], attn_gain, grad_hidden_one
    )
    grad_input = grad_middle + grad_normed_one
    dense_grads = (
        grad_attn_gain,
        grad_query_w,
        grad_key_w,
        grad_value_w,
        grad_w_out,
        grad_ffn_gain,
        grad_router,
    )
    return (grad_input, dense_grads, (grad_gate, grad_up, grad_down))


def experts_in(own, is_first):
    experts, rows, columns = own.shape
    copies = lax.axis_size("dp") * lax.axis_size("section") // experts
    half = rows // 2
    low_half, high_half = own[:, :half], own[:, half:]
    kept = jnp.where(is_first, low_half, high_half)
    received = swapped(jnp.where(is_first, high_half, low_half))
    layers = (jnp.where(is_first, kept, received), jnp.where(is_first, received, kept))
    whole = []
    for piece in layers:
        if copies > 1:
            piece = jnp.repeat(piece, copies, 0)
        whole.append(exchange(piece, LINE).reshape(-1, columns))
    return whole


def experts_out(grad, experts):
    size = lax.axis_size("dp") * lax.axis_size("section")
    columns = grad.shape[1]
    pieces = exchange(grad.astype(BF).reshape(size, -1, columns), LINE)
    copies = size // experts
    if copies > 1:
        pieces = jnp.sum(
            pieces.reshape(experts, copies, -1, columns).astype(F32), 1
        ).astype(BF)
    return pieces


def dense_total(grads, shift):
    attn_gain, query, key, value, out, ffn_gain, router = grads
    small = jnp.concatenate([router, attn_gain[:, None], ffn_gain[:, None]], 1)
    widths = [a.shape[1] for a in (query, key, value, out, small)]
    packed = jnp.concatenate([a.astype(BF) for a in (query, key, value, out, small)], 1)
    rows = packed.shape[0]
    other = lax.ppermute(packed, "section", shift)
    both = (packed.astype(F32) + other.astype(F32)).astype(BF)
    part = lax.psum_scatter(both, REPLICAS, scatter_dimension=0, tiled=True)
    total = lax.all_gather(part, REPLICAS, axis=0, tiled=True).astype(F32)
    offsets = np.cumsum(widths)[:-1]
    query, key, value, out, small = jnp.split(total, offsets, 1)
    experts = small.shape[1] - 2
    return (small[:, experts], query, key, value, out, small[:, experts + 1], small[:, :experts])


def local(
    edge_in,
    seg_lengths,
    routes,
    turns,
    attn_gain,
    w_query,
    w_key,
    w_value,
    w_out,
    ffn_gain,
    w_router,
    w_gate,
    w_up,
    w_down,
):
    edge_rows = edge_in[0, :, 0]
    local_len = edge_rows.shape[1]
    lengths_all = seg_lengths[:, 0]
    route_all = routes[0, :, 0]
    turn_all = turns[0, :, 0, 0]
    tree_length = local_len * lax.axis_size("dp")
    first_row = lax.axis_index("dp") * local_len
    section_index = lax.axis_index("section")
    is_first = section_index == 0

    def both_layers(own, received):
        return (jnp.where(is_first, own, received), jnp.where(is_first, received, own))

    def of_micro(pair):
        mine = jnp.where(is_first, pair[0], pair[1])
        others = jnp.where(is_first, pair[1], pair[0])
        return both_layers(mine, swapped(others))

    layer_rows, cotangent = of_micro(edge_rows)
    route_pair = of_micro(route_all)
    turn_pair = of_micro(turn_all)
    lengths_row = jnp.where(is_first, lengths_all[0], lengths_all[1])
    dense_own = (attn_gain[0], w_query[0], w_key[0], w_value[0], w_out[0], ffn_gain[0], w_router[0])
    dense_pairs = [both_layers(a, swapped(a)) for a in dense_own]
    expert_own = (w_gate[0], w_up[0], w_down[0])
    expert_pairs = [experts_in(a, is_first) for a in expert_own]
    dense_sets = [tuple(p[i] for p in dense_pairs) for i in range(2)]
    expert_sets = [tuple(p[i] for p in expert_pairs) for i in range(2)]
    visible = tree_mask(lengths_row, first_row, local_len, tree_length)

    stored = []
    state = layer_rows
    for layer in range(2):
        state, kept = layer_forward(
            state.astype(F32),
            visible,
            route_pair[layer],
            turn_pair[layer],
            dense_sets[layer],
            expert_sets[layer],
        )
        stored.append(kept)
        if layer == 0:
            state = state.astype(BF)
    top = state
    top_other = lax.ppermute(top, "section", UP)

    grad = cotangent
    dense_totals = [None, None]
    expert_halves = [None, None]
    for layer in (1, 0):
        grad, dense_grads, expert_grads = layer_backward(
            stored[layer], grad, dense_sets[layer], expert_sets[layer]
        )
        expert_halves[layer] = [experts_out(g, w_gate.shape[1]) for g in expert_grads]
        dense_totals[layer] = dense_total(dense_grads, SWAP)
        if layer == 1:
            grad = grad.astype(BF)
    grad_other = lax.ppermute(grad, "section", DOWN)
    edge_out = jnp.where(
        is_first, jnp.stack([grad, grad_other]), jnp.stack([top_other, top])
    )[None, :, None]
    expert_total = []
    for first, second in zip(*expert_halves, strict=True):
        low_half = jnp.where(is_first, first, lax.ppermute(second, "section", UP))
        high_half = jnp.where(is_first, lax.ppermute(first, "section", DOWN), second)
        expert_total.append(jnp.concatenate([low_half, high_half], 1).astype(F32))
    dense_out = [jnp.where(is_first, a, b) for a, b in zip(*dense_totals, strict=True)]
    return (
        (edge_out,)
        + tuple((piece[None] for piece in dense_out))
        + tuple((piece[None] for piece in expert_total))
    )


def solution(mesh):
    placed = (
        P("section", None, "expert", "dp", None),
        P(None, "expert", None),
        P("section", None, "expert", "dp", None),
        P("section", None, "expert", "dp", None),
        P("section", None),
        P("section", None, None),
        P("section", None, None),
        P("section", None, None),
        P("section", None, None),
        P("section", None),
        P("section", None, None),
        P("section", "expert", "dp", None),
        P("section", "expert", "dp", None),
        P("section", "expert", "dp", None),
    )
    return jax.shard_map(
        local,
        mesh=mesh,
        in_specs=placed,
        out_specs=(
            P("section", None, "expert", "dp", None),
            P("section", None),
            P("section", None, None),
            P("section", None, None),
            P("section", None, None),
            P("section", None, None),
            P("section", None),
            P("section", None, None),
            P("section", "expert", "dp", None),
            P("section", "expert", "dp", None),
            P("section", "expert", "dp", None),
        ),
        check_vma=False,
    )
```

```python
import jax
import jax.numpy as jnp
import numpy as np
from jax import lax
from jax.sharding import PartitionSpec as P

HEAD_SIZE = 128
SCALE = HEAD_SIZE ** (-0.5)
epsilon = 1e-06
masked_score = -1e30
BF = jnp.bfloat16
F32 = jnp.float32

SWAP = [(0, 1), (1, 0)]
UP = [(0, 1)]
DOWN = [(1, 0)]
OWNERS = ("expert", "dp", "section")
LINE = ("dp", "section")
REPLICAS = ("dp", "expert")


def ancestry():
    parents = [-1]
    for branch_index in range(4):
        parents += [0, 1 + 3 * branch_index, 1 + 3 * branch_index]
    lineage = np.zeros((13, 13), np.float32)
    for segment in range(13):
        current = segment
        while current >= 0:
            lineage[current, segment] = 1.0
            current = parents[current]
    return lineage


def dot(left, right):
    return jnp.dot(left, right, preferred_element_type=F32)


def dot_t(left, right):
    return lax.dot_general(left, right, (((1,), (1,)), ((), ())), preferred_element_type=F32)


def t_dot(left, right):
    return lax.dot_general(left, right, (((0,), (0,)), ((), ())), preferred_element_type=F32)


def normalize(values, gain_vec):
    factor = lax.rsqrt(jnp.mean(values * values, -1, keepdims=True) + epsilon)
    return (values * factor * gain_vec, factor)


def norm_back(values, factor, gain_vec, upstream):
    scaled = upstream * gain_vec
    grad_gain = jnp.sum(upstream * values * factor, 0)
    inner_mean = jnp.mean(scaled * values, -1, keepdims=True)
    return (scaled * factor - values * factor * factor * factor * inner_mean, grad_gain)


def tree_mask(lengths_row, local_len):
    size = lax.axis_size("dp")
    own = lax.axis_index("dp")
    first_row = own * local_len
    seg_ends = jnp.cumsum(lengths_row)
    blocks = (own - jnp.arange(size, dtype=jnp.int32)) % size
    key_spots = (
        blocks[:, None] * local_len + jnp.arange(local_len, dtype=jnp.int32)[None, :]
    ).reshape(-1)
    query_spots = first_row + jnp.arange(local_len, dtype=jnp.int32)
    seg_ids = jnp.arange(13, dtype=jnp.int32)
    key_seg = jnp.sum((key_spots[:, None] >= seg_ends[None, :]).astype(jnp.int32), 1)
    query_seg = jnp.sum((query_spots[:, None] >= seg_ends[None, :]).astype(jnp.int32), 1)
    key_hot = (key_seg[:, None] == seg_ids[None, :]).astype(BF)
    query_hot = (query_seg[:, None] == seg_ids[None, :]).astype(BF)
    allowed = dot(query_hot, jnp.asarray(ancestry(), BF)).astype(BF)
    linked = dot_t(allowed, key_hot) > 0.5
    return linked & (key_spots[None, :] <= query_spots[:, None])


def exchange(shard, axes):
    return lax.all_to_all(shard, axes, split_axis=0, concat_axis=0, tiled=True)


def swapped(shard):
    return lax.ppermute(shard, "section", SWAP)


def gather_rows(shard):
    size = lax.axis_size("dp")
    blocks = [shard]
    for step in range(1, size):
        blocks.append(lax.ppermute(shard, "dp", [(i, (i + step) % size) for i in range(size)]))
    return jnp.concatenate(blocks, 0)


def sum_to_owner(partial):
    size = lax.axis_size("dp")
    blocks = jnp.split(partial, size, 0)
    total = blocks[0].astype(F32)
    for step in range(1, size):
        back = [((i + step) % size, i) for i in range(size)]
        total = total + lax.ppermute(blocks[step], "dp", back).astype(F32)
    return total


def layer_forward(layer_in, visible, route_rows, turn_row, dense_set, expert_set):
    attn_gain, w_query, w_key, w_value, w_out, ffn_gain, w_router = dense_set
    w_gate, w_up, w_down = expert_set
    local_len, width = layer_in.shape
    heads_kv = w_key.shape[1] // HEAD_SIZE
    experts_all = w_router.shape[1]
    pick_count = route_rows.shape[1]
    capacity = local_len * pick_count // experts_all
    slots = experts_all * capacity
    normed, factor_one = normalize(layer_in, attn_gain)
    hidden_one = normed.astype(BF)
    queries = dot(hidden_one, w_query).astype(BF)
    key_rows = dot(hidden_one, w_key).astype(BF)
    value_rows = dot(hidden_one, w_value).astype(BF)
    kv_all = gather_rows(jnp.concatenate([key_rows, value_rows], 1))
    key_width = w_key.shape[1]
    key_all = kv_all[:, :key_width].reshape(-1, heads_kv, HEAD_SIZE)
    value_all = kv_all[:, key_width:].reshape(-1, heads_kv, HEAD_SIZE)
    grouped_query = queries.reshape(local_len, heads_kv, -1, HEAD_SIZE)
    raw = jnp.einsum("tkgd,skd->kgts", grouped_query, key_all, preferred_element_type=F32) * SCALE
    scores = jnp.where(visible[None, None], raw, masked_score)
    log_total = jax.nn.logsumexp(scores, -1, keepdims=True)
    attn_prob = jnp.exp(scores - log_total)
    attn_mix = jnp.einsum(
        "kgts,skd->tkgd", attn_prob.astype(BF), value_all, preferred_element_type=F32
    )
    attn_mix = attn_mix.reshape(local_len, -1).astype(BF)
    middle = layer_in + dot(attn_mix, w_out)
    normed_two, factor_two = normalize(middle, ffn_gain)
    hidden_two = normed_two.astype(BF)
    logits = dot(hidden_two, w_router)
    expert_ids = jnp.arange(experts_all, dtype=jnp.int32)
    chosen = jnp.any(route_rows[:, :, None] == expert_ids[None, None, :], 1)
    masked_logits = jnp.where(chosen, logits, masked_score)
    top = jnp.max(masked_logits, -1, keepdims=True)
    powers = jnp.where(chosen, jnp.exp(masked_logits - top), 0.0)
    gate_share = powers / jnp.sum(powers, -1, keepdims=True)
    earlier = (turn_row[None, :] < turn_row[:, None]).astype(BF)
    places = dot(earlier, chosen.astype(BF))
    place_of = jnp.where(chosen & (places < capacity), places, -1.0).astype(BF)
    slot_ids = jnp.arange(slots, dtype=jnp.int32)
    spread = (slot_ids[None, :] // capacity == expert_ids[:, None]).astype(BF)
    rank = (slot_ids % capacity).astype(F32)
    selected = dot(place_of, spread) == rank[None, :]
    selector = selected.astype(BF)
    weighting = jnp.where(selected, dot(gate_share.astype(BF), spread), 0.0).astype(BF)
    outgoing = t_dot(selector, hidden_two).astype(BF)
    arrived = send_out(outgoing, experts_all, capacity)
    gate_pre = dot(arrived, w_gate)
    up_pre = dot(arrived, w_up)
    inner_act = (jax.nn.silu(gate_pre) * up_pre).astype(BF)
    produced = dot(inner_act, w_down).astype(BF)
    returned = send_back(produced, experts_all, capacity)
    result = middle + dot(weighting, returned)
    stored = {
        "layer_in": layer_in,
        "factor_one": factor_one,
        "hidden_one": hidden_one,
        "queries": queries,
        "key_all": key_all,
        "value_all": value_all,
        "attn_prob": attn_prob,
        "attn_mix": attn_mix,
        "middle": middle,
        "factor_two": factor_two,
        "hidden_two": hidden_two,
        "gate_share": gate_share,
        "selected": selected,
        "spread": spread,
        "weighting": weighting,
        "arrived": arrived,
        "gate_pre": gate_pre,
        "up_pre": up_pre,
        "inner_act": inner_act,
        "returned": returned,
        "early_hidden": early_operand(hidden_one),
        "early_mix": early_operand(attn_mix),
    }
    return (result, stored)


def copies_of_expert(experts_all):
    owners = lax.axis_size("expert") * lax.axis_size("dp") * lax.axis_size("section")
    return owners // experts_all


def send_out(slot_rows, experts_all, capacity):
    width = slot_rows.shape[-1]
    copies = copies_of_expert(experts_all)
    rows = slot_rows.reshape(experts_all, capacity, width)
    if copies > 1:
        mine = jnp.arange(copies) == lax.axis_index("dp") % copies
        rows = jnp.where(mine[None, :, None, None], rows[:, None], 0).reshape(-1, capacity, width)
    return exchange(rows, OWNERS).reshape(-1, width)


def send_back(rows, experts_all, capacity):
    width = rows.shape[-1]
    copies = copies_of_expert(experts_all)
    rows = exchange(rows.reshape(-1, capacity, width), OWNERS)
    if copies > 1:
        mine = lax.axis_index("dp") % copies
        rows = lax.dynamic_index_in_dim(
            rows.reshape(experts_all, copies, capacity, width), mine, 1, False
        )
    return rows.reshape(-1, width)


def layer_backward(stored, grad_top, dense_set, expert_set):
    attn_gain, w_query, w_key, w_value, w_out, ffn_gain, w_router = dense_set
    w_gate, w_up, w_down = expert_set
    local_len = grad_top.shape[0]
    experts_all = w_router.shape[1]
    slots = stored["selected"].shape[1]
    capacity = slots // experts_all
    gate_share = stored["gate_share"]
    slot_grads = t_dot(stored["weighting"], grad_top).astype(BF)
    slot_owed = send_out(slot_grads, experts_all, capacity)
    match = jnp.where(stored["selected"], dot_t(grad_top, stored["returned"]), 0.0)
    grad_weighting = lax.dot_general(
        match,
        stored["spread"].astype(F32),
        (((1,), (1,)), ((), ())),
        precision=lax.Precision.HIGHEST,
        preferred_element_type=F32,
    )
    grad_logits = (
        gate_share * (grad_weighting - jnp.sum(gate_share * grad_weighting, -1, keepdims=True))
    ).astype(BF)
    grad_router = t_dot(grad_logits, stored["hidden_two"])
    grad_hidden = dot_t(grad_logits, w_router)
    gate_pre = stored["gate_pre"]
    up_pre = stored["up_pre"]
    grad_inner = dot_t(slot_owed, w_down)
    sigmoid_a = jax.nn.sigmoid(gate_pre)
    grad_gate_pre = (grad_inner * up_pre * sigmoid_a * (1.0 + gate_pre * (1.0 - sigmoid_a))).astype(
        BF
    )
    grad_up_pre = (grad_inner * gate_pre * sigmoid_a).astype(BF)
    grad_arrived = (dot_t(grad_gate_pre, w_gate) + dot_t(grad_up_pre, w_up)).astype(BF)
    sent_back = send_back(grad_arrived, experts_all, capacity)
    arrived = stored["arrived"]
    grad_down = t_dot(stored["inner_act"], slot_owed)
    grad_gate = t_dot(arrived, grad_gate_pre)
    grad_up = t_dot(arrived, grad_up_pre)
    grad_hidden = grad_hidden + dot(stored["selected"].astype(BF), sent_back)
    grad_normed_two, grad_ffn_gain = norm_back(
        stored["middle"], stored["factor_two"], ffn_gain, grad_hidden
    )
    grad_middle = grad_top.astype(F32) + grad_normed_two
    grad_branch = grad_middle.astype(BF)
    grad_w_out = dense_total(stored["early_mix"], late_operand(grad_branch))
    grad_mix = dot_t(grad_branch, w_out).astype(BF)
    key_all = stored["key_all"]
    value_all = stored["value_all"]
    heads_kv = key_all.shape[1]
    attn_prob = stored["attn_prob"]
    grouped_grad = grad_mix.reshape(local_len, heads_kv, -1, HEAD_SIZE)
    grad_prob = jnp.einsum("tkgd,skd->kgts", grouped_grad, value_all, preferred_element_type=F32)
    centre = jnp.sum(attn_prob * grad_prob, -1, keepdims=True)
    grad_scores = (attn_prob * (grad_prob - centre)).astype(BF)
    grad_queries = (
        jnp.einsum("kgts,skd->tkgd", grad_scores, key_all, preferred_element_type=F32) * SCALE
    )
    grad_queries = grad_queries.reshape(local_len, -1).astype(BF)
    grouped_query = stored["queries"].reshape(local_len, heads_kv, -1, HEAD_SIZE)
    grad_keys_all = (
        jnp.einsum("kgts,tkgd->skd", grad_scores, grouped_query, preferred_element_type=F32) * SCALE
    )
    grad_values_all = jnp.einsum(
        "kgts,tkgd->skd", attn_prob.astype(BF), grouped_grad, preferred_element_type=F32
    )
    tree_length = key_all.shape[0]
    grad_kv = sum_to_owner(
        jnp.concatenate(
            [grad_keys_all.reshape(tree_length, -1), grad_values_all.reshape(tree_length, -1)], 1
        ).astype(BF)
    ).astype(BF)
    key_width = w_key.shape[1]
    grad_keys, grad_values = grad_kv[:, :key_width], grad_kv[:, key_width:]
    grad_qkv_w = dense_total(
        stored["early_hidden"], late_operand(jnp.concatenate([grad_queries, grad_kv], 1))
    )
    grad_hidden_one = dot_t(grad_queries, w_query)
    grad_hidden_one = grad_hidden_one + dot_t(grad_keys, w_key)
    grad_hidden_one = grad_hidden_one + dot_t(grad_values, w_value)
    grad_normed_one, grad_attn_gain = norm_back(
        stored["layer_in"], stored["factor_one"], attn_gain, grad_hidden_one
    )
    grad_input = grad_middle + grad_normed_one
    small = jnp.concatenate([grad_router, grad_attn_gain[None], grad_ffn_gain[None]], 0)
    small = small_total(jnp.pad(small, ((0, -small.shape[0] % 16), (0, 0))))
    dense_grads = (grad_w_out, grad_qkv_w, small)
    return (grad_input, dense_grads, (grad_gate, grad_up, grad_down))


def experts_in(own, is_first):
    experts, rows, columns = own.shape
    copies = lax.axis_size("dp") * lax.axis_size("section") // experts
    half = rows // 2
    low_half, high_half = own[:, :half], own[:, half:]
    kept = jnp.where(is_first, low_half, high_half)
    received = swapped(jnp.where(is_first, high_half, low_half))
    layers = (jnp.where(is_first, kept, received), jnp.where(is_first, received, kept))
    whole = []
    for piece in layers:
        if copies > 1:
            piece = jnp.repeat(piece, copies, 0)
        whole.append(exchange(piece, LINE).reshape(-1, columns))
    return whole


def experts_out(grad, experts):
    size = lax.axis_size("dp") * lax.axis_size("section")
    columns = grad.shape[1]
    pieces = exchange(grad.astype(BF).reshape(size, -1, columns), LINE)
    copies = size // experts
    if copies > 1:
        pieces = jnp.sum(
            pieces.reshape(experts, copies, -1, columns).astype(F32), 1
        ).astype(BF)
    return pieces


def ring(axis, step):
    size = lax.axis_size(axis)
    return [(i, (i + step) % size) for i in range(size)]


def partners(axis, flip):
    return [(i, i ^ flip) for i in range(lax.axis_size(axis))]


def early_operand(rows):
    half = rows.shape[1] // 2
    section = lax.axis_index("section")
    mine = lax.dynamic_slice_in_dim(rows, section * half, half, 1)
    others = lax.dynamic_slice_in_dim(rows, (1 - section) * half, half, 1)
    gathered = jnp.stack([mine, swapped(others)])
    flip = 1
    while flip < lax.axis_size("expert"):
        others = lax.ppermute(gathered, "expert", partners("expert", flip))
        gathered = jnp.concatenate([gathered, others], 1)
        flip *= 2
    return gathered.reshape(-1, half)


def late_operand(rows):
    groups = lax.axis_size("expert")
    own = lax.axis_index("expert")
    share = rows.shape[1] // groups
    blocks = []
    for flip in range(groups):
        block = lax.dynamic_slice_in_dim(rows, (own ^ flip) * share, share, 1)
        if flip > 0:
            block = lax.ppermute(block, "expert", partners("expert", flip))
        blocks.append(block)
    gathered = jnp.concatenate(blocks, 0)
    return jnp.concatenate([gathered, swapped(gathered)], 0)


def rows_of(array, index, count):
    return lax.dynamic_slice_in_dim(array, index * count, count, 0)


def dense_total(early, late):
    partial = t_dot(early, late)
    size = lax.axis_size("dp")
    own = lax.axis_index("dp")
    count = partial.shape[0] // size
    total = rows_of(partial, own, count)
    rounded = partial.astype(BF)
    for step in range(1, size):
        block = rows_of(rounded, (own + step) % size, count)
        total = total + lax.ppermute(block, "dp", ring("dp", step)).astype(F32)
    total = total.astype(BF)
    blocks = [total] + [lax.ppermute(total, "dp", ring("dp", -step)) for step in range(1, size)]
    total = jnp.concatenate(blocks + blocks[:-1], 0)
    total = lax.dynamic_slice_in_dim(total, ((size - own) % size) * count, size * count, 0)
    group = lax.axis_index("expert")
    flip = 1
    while flip < lax.axis_size("expert"):
        others = lax.ppermute(total, "expert", partners("expert", flip))
        first = (group & flip) == 0
        total = jnp.concatenate(
            [jnp.where(first, total, others), jnp.where(first, others, total)], 1
        )
        flip *= 2
    return total


def small_total(partial):
    total = partial + swapped(partial.astype(BF)).astype(F32)
    flip = 1
    while flip < lax.axis_size("expert"):
        total = total + lax.ppermute(
            total.astype(BF), "expert", partners("expert", flip)
        ).astype(F32)
        flip *= 2
    rounded = total.astype(BF)
    for step in range(1, lax.axis_size("dp")):
        total = total + lax.ppermute(rounded, "dp", ring("dp", step)).astype(F32)
    return total


def at_home(first, second, is_first, axis):
    low_half = jnp.where(is_first, first, lax.ppermute(second, "section", UP))
    high_half = jnp.where(is_first, lax.ppermute(first, "section", DOWN), second)
    return jnp.concatenate([low_half, high_half], axis).astype(F32)


def local(
    edge_in,
    seg_lengths,
    routes,
    turns,
    attn_gain,
    w_query,
    w_key,
    w_value,
    w_out,
    ffn_gain,
    w_router,
    w_gate,
    w_up,
    w_down,
):
    edge_rows = edge_in[0, :, 0]
    local_len = edge_rows.shape[1]
    lengths_all = seg_lengths[:, 0]
    route_all = routes[0, :, 0]
    turn_all = turns[0, :, 0, 0]
    section_index = lax.axis_index("section")
    is_first = section_index == 0

    def both_layers(own, received):
        return (jnp.where(is_first, own, received), jnp.where(is_first, received, own))

    def of_micro(pair):
        mine = jnp.where(is_first, pair[0], pair[1])
        others = jnp.where(is_first, pair[1], pair[0])
        return both_layers(mine, swapped(others))

    layer_rows, cotangent = of_micro(edge_rows)
    route_pair = of_micro(route_all)
    turn_pair = of_micro(turn_all)
    lengths_row = jnp.where(is_first, lengths_all[0], lengths_all[1])
    dense_own = (attn_gain[0], w_query[0], w_key[0], w_value[0], w_out[0], ffn_gain[0], w_router[0])
    dense_pairs = [both_layers(a, swapped(a)) for a in dense_own]
    expert_own = (w_gate[0], w_up[0], w_down[0])
    expert_pairs = [experts_in(a, is_first) for a in expert_own]
    dense_sets = [tuple(p[i] for p in dense_pairs) for i in range(2)]
    expert_sets = [tuple(p[i] for p in expert_pairs) for i in range(2)]
    visible = tree_mask(lengths_row, local_len)

    stored = []
    state = layer_rows
    for layer in range(2):
        state, kept = layer_forward(
            state.astype(F32),
            visible,
            route_pair[layer],
            turn_pair[layer],
            dense_sets[layer],
            expert_sets[layer],
        )
        stored.append(kept)
        if layer == 0:
            state = state.astype(BF)
    top = state
    top_other = lax.ppermute(top, "section", UP)

    grad = cotangent
    dense_totals = [None, None]
    expert_halves = [None, None]
    for layer in (1, 0):
        grad, dense_grads, expert_grads = layer_backward(
            stored[layer], grad, dense_sets[layer], expert_sets[layer]
        )
        expert_halves[layer] = [experts_out(g, w_gate.shape[1]) for g in expert_grads]
        dense_totals[layer] = dense_grads
        if layer == 1:
            grad = grad.astype(BF)
            grad, expert_halves[1] = lax.optimization_barrier((grad, expert_halves[1]))
    grad_other = lax.ppermute(grad, "section", DOWN)
    edge_out = jnp.where(
        is_first, jnp.stack([grad, grad_other]), jnp.stack([top_other, top])
    )[None, :, None]
    expert_total = [at_home(*pair, is_first, 1) for pair in zip(*expert_halves, strict=True)]
    out, qkv = [at_home(a, b, is_first, 0) for a, b in list(zip(*dense_totals, strict=True))[:2]]
    small = jnp.where(is_first, dense_totals[0][2], dense_totals[1][2])
    query_width, key_width = w_query.shape[2], w_key.shape[2]
    query, key, value = jnp.split(qkv, [query_width, query_width + key_width], 1)
    experts_all = w_router.shape[2]
    dense_out = (
        small[experts_all],
        query,
        key,
        value,
        out,
        small[experts_all + 1],
        small[:experts_all].T,
    )
    return (
        (edge_out,)
        + tuple((piece[None] for piece in dense_out))
        + tuple((piece[None] for piece in expert_total))
    )


def solution(mesh):
    placed = (
        P("section", None, "expert", "dp", None),
        P(None, "expert", None),
        P("section", None, "expert", "dp", None),
        P("section", None, "expert", "dp", None),
        P("section", None),
        P("section", None, None),
        P("section", None, None),
        P("section", None, None),
        P("section", None, None),
        P("section", None),
        P("section", None, None),
        P("section", "expert", "dp", None),
        P("section", "expert", "dp", None),
        P("section", "expert", "dp", None),
    )
    return jax.shard_map(
        local,
        mesh=mesh,
        in_specs=placed,
        out_specs=(
            P("section", None, "expert", "dp", None),
            P("section", None),
            P("section", None, None),
            P("section", None, None),
            P("section", None, None),
            P("section", None, None),
            P("section", None),
            P("section", None, None),
            P("section", "expert", "dp", None),
            P("section", "expert", "dp", None),
            P("section", "expert", "dp", None),
        ),
        check_vma=False,
    )
```

```python
import jax
import jax.numpy as jnp
import numpy as np
from jax import lax
from jax.experimental import pallas as pl
from jax.experimental.pallas import tpu as pltpu
from jax.sharding import PartitionSpec as P

HEAD_SIZE = 128
SCALE = HEAD_SIZE ** (-0.5)
epsilon = 1e-06
masked_score = -1e30
BF = jnp.bfloat16
F32 = jnp.float32

SWAP = [(0, 1), (1, 0)]
UP = [(0, 1)]
DOWN = [(1, 0)]
OWNERS = ("expert", "dp", "section")
LINE = ("dp", "section")


def ancestry():
    parents = [-1]
    for branch_index in range(4):
        parents += [0, 1 + 3 * branch_index, 1 + 3 * branch_index]
    lineage = np.zeros((13, 13), np.float32)
    for segment in range(13):
        current = segment
        while current >= 0:
            lineage[current, segment] = 1.0
            current = parents[current]
    return lineage


def dot(left, right):
    return jnp.dot(left, right, preferred_element_type=F32)


def dot_t(left, right):
    return lax.dot_general(left, right, (((1,), (1,)), ((), ())), preferred_element_type=F32)


def t_dot(left, right):
    return lax.dot_general(left, right, (((0,), (0,)), ((), ())), preferred_element_type=F32)


def t_dot_t(left, right):
    return lax.dot_general(left, right, (((0,), (1,)), ((), ())), preferred_element_type=F32)


def normalize(values, gain_vec):
    factor = lax.rsqrt(jnp.mean(values * values, -1, keepdims=True) + epsilon)
    return (values * factor * gain_vec, factor)


def norm_back(values, factor, gain_vec, upstream):
    scaled = upstream * gain_vec
    grad_gain = jnp.sum(upstream * values * factor, 0)
    inner_mean = jnp.mean(scaled * values, -1, keepdims=True)
    return (scaled * factor - values * factor * factor * factor * inner_mean, grad_gain)


def tree_mask(lengths_row, local_len):
    own = lax.axis_index("dp")
    first_row = own * local_len
    seg_ends = jnp.cumsum(lengths_row)
    blocks = own ^ jnp.asarray(block_order(), jnp.int32)
    key_spots = (
        blocks[:, None] * local_len + jnp.arange(local_len, dtype=jnp.int32)[None, :]
    ).reshape(-1)
    query_spots = first_row + jnp.arange(local_len, dtype=jnp.int32)
    seg_ids = jnp.arange(13, dtype=jnp.int32)
    key_seg = jnp.sum((key_spots[:, None] >= seg_ends[None, :]).astype(jnp.int32), 1)
    query_seg = jnp.sum((query_spots[:, None] >= seg_ends[None, :]).astype(jnp.int32), 1)
    key_hot = (key_seg[:, None] == seg_ids[None, :]).astype(BF)
    query_hot = (query_seg[:, None] == seg_ids[None, :]).astype(BF)
    allowed = dot(query_hot, jnp.asarray(ancestry(), BF)).astype(BF)
    linked = dot_t(allowed, key_hot) > 0.5
    return linked & (key_spots[None, :] <= query_spots[:, None])


def tie(*values):
    return lax.optimization_barrier(values)


def swapped(shard):
    return lax.ppermute(shard, "section", SWAP)


def partners(axis, flip):
    return [(i, i ^ flip) for i in range(lax.axis_size(axis))]


def flips(axis):
    found = [1]
    while 2 * found[-1] < lax.axis_size(axis):
        found.append(2 * found[-1])
    return found


def block_order():
    order = [0]
    for flip in reversed(flips("dp")):
        order = order + [k ^ flip for k in order]
    return order


def gathered(shard, axis, over="dp"):
    for flip in reversed(flips(over)):
        shard = jnp.concatenate([shard, lax.ppermute(shard, over, partners(over, flip))], axis)
    return shard


def sum_to_owner(partial, axis):
    sent_as = partial.dtype
    for flip in flips("dp"):
        kept, sent = jnp.split(partial, 2, axis)
        sent = lax.ppermute(sent.astype(sent_as), "dp", partners("dp", flip))
        partial = kept.astype(F32) + sent.astype(F32)
    return partial


def pick_blocks(sources, blocks, pick, count, kernel, out_shapes, out_blocks):
    where = jnp.stack([lax.axis_index(axis) for axis in ("section", "dp")]).astype(jnp.int32)

    def spec(at):
        def index(k, where):
            return pick(k, where)[at]

        return pl.BlockSpec(blocks[at], index)

    def body(where, *refs):
        kernel(pl.program_id(0), where, refs[: len(sources)], refs[len(sources) :])

    return pl.pallas_call(
        body,
        grid_spec=pltpu.PrefetchScalarGridSpec(
            num_scalar_prefetch=1,
            grid=(count,),
            in_specs=[spec(at) for at in range(len(sources))],
            out_specs=[
                pl.BlockSpec(shape, lambda k, where: (k,) + (0,) * (len(shape) - 1))
                for shape in out_blocks
            ],
        ),
        out_shape=[jax.ShapeDtypeStruct(shape, F32) for shape in out_shapes],
        compiler_params=pltpu.CompilerParams(vmem_limit_bytes=48 * 1024 * 1024),
    )(where, *sources)


def two_homes(first, second):
    return (
        first,
        second,
        lax.ppermute(first, "section", DOWN),
        lax.ppermute(second, "section", UP),
    )


def source_of(section, core):
    return jnp.where(core == section, section, 2 + section)


def dense_home(homes, out_widths):
    parts, groups, rows, width = homes[0].shape
    block = rows // 2

    def pick(k, where):
        used = source_of(where[0], k // (2 * parts))
        return [
            (jnp.where(used == source, k // 2 % parts, 0), 0, jnp.where(used == source, k % 2, 0), 0)
            for source in range(4)
        ]

    def kernel(k, where, sources, outs):
        used = source_of(where[0], k // (2 * parts))
        for source in range(4):

            @pl.when(used == source)
            def _():
                out, at = 0, 0
                for group in range(groups):
                    start = 0
                    while start < width:
                        piece = min(width - start, out_widths[out] - at)
                        outs[out][:, at : at + piece] = sources[source][
                            0, group, :, start : start + piece
                        ].astype(F32)
                        start, at = start + piece, at + piece
                        if at == out_widths[out]:
                            out, at = out + 1, 0

    count = 4 * parts
    shapes = [(count * block, w) for w in out_widths]
    blocks = [(1, groups, block, width)] * 4
    return pick_blocks(
        homes, blocks, pick, count, kernel, shapes, [(block, w) for w in out_widths]
    )


def two_parts(array, index, axis=0):
    half = array.shape[axis] // 2
    return (
        lax.dynamic_slice_in_dim(array, index * half, half, axis),
        lax.dynamic_slice_in_dim(array, (1 - index) * half, half, axis),
    )


def in_order(mine, others, index, axis):
    first = index == 0
    return jnp.concatenate(
        [jnp.where(first, mine, others), jnp.where(first, others, mine)], axis
    )


def early_operand(rows):
    mine, others = two_parts(rows, lax.axis_index("section"), 1)
    half = mine.shape[1]
    joined = jnp.stack([mine.reshape(2, -1, half), swapped(others).reshape(2, -1, half)], 1)
    return gathered(joined[:, None], 1, "expert").reshape(2, -1, half)


def late_operands(operands):
    groups = lax.axis_size("expert")
    own = lax.axis_index("expert")
    blocks = []
    order = [0]
    for flip in reversed(flips("expert")):
        order = order + [k ^ flip for k in order]
    for flip in order:
        shares = []
        for rows in operands:
            share = rows.shape[1] // groups
            shares.append(lax.dynamic_slice_in_dim(rows, (own ^ flip) * share, share, 1))
        block = jnp.concatenate(shares, 1)
        if flip > 0:
            block = lax.ppermute(block, "expert", partners("expert", flip))
        blocks.append(block)
    joined = jnp.stack(blocks)
    joined = jnp.stack([joined, swapped(joined)], 1)
    joined = joined.reshape(-1, joined.shape[-1])
    return jnp.split(joined, np.cumsum([a.shape[1] // groups for a in operands])[:-1], 1)


def dense_partial(early, late):
    return jnp.concatenate([t_dot(e, p) for e, p in zip(early, late, strict=True)], 1)


def dense_rows(partial):
    own = lax.axis_index("dp")
    for flip in flips("dp"):
        kept, sent = two_parts(partial, jnp.where((own & flip) == 0, 0, 1))
        sent = lax.ppermute(sent.astype(BF), "dp", partners("dp", flip))
        partial = kept.astype(F32) + sent.astype(F32)
    return partial.astype(BF)


def dense_line(total):
    own = lax.axis_index("dp")
    for flip in reversed(flips("dp")):
        others = lax.ppermute(total, "dp", partners("dp", flip))
        total = in_order(total, others, own & flip, 0)
    return total


def dense_groups(total):
    own = lax.axis_index("expert")
    order = flips("expert")
    parts = []
    for part, way in zip(jnp.split(total, 2, 0), (order, order[::-1]), strict=True):
        part = part.reshape((1,) * len(order) + part.shape)
        for flip in way:
            others = lax.ppermute(part, "expert", partners("expert", flip))
            part = in_order(part, others, own & flip, len(order) - 1 - order.index(flip))
        parts.append(part.reshape((-1,) + part.shape[-2:]))
    return jnp.stack(parts)


def small_total(partial):
    for axis in ("section", "expert", "dp"):
        for flip in flips(axis):
            others = lax.ppermute(partial.astype(BF), axis, partners(axis, flip))
            partial = partial + others.astype(F32)
    return partial


def exchange(rows, axes):
    return lax.all_to_all(rows, axes, split_axis=0, concat_axis=0, tiled=True)


def copies_of_expert(experts_all):
    owners = lax.axis_size("expert") * lax.axis_size("dp") * lax.axis_size("section")
    return owners // experts_all


def send_out(slot_rows, experts_all):
    width = slot_rows.shape[-1]
    copies = copies_of_expert(experts_all)
    rows = slot_rows.reshape(experts_all, -1, width)
    if copies > 1:
        mine = jnp.arange(copies) == lax.axis_index("dp") % copies
        rows = jnp.where(mine[None, :, None, None], rows[:, None], 0)
        rows = rows.reshape(experts_all * copies, -1, width)
    return exchange(rows, OWNERS).reshape(-1, width)


def send_back(rows, experts_all):
    width = rows.shape[-1]
    copies = copies_of_expert(experts_all)
    rows = exchange(rows.reshape(experts_all * copies, -1, width), OWNERS)
    if copies > 1:
        rows = rows.reshape(experts_all, copies, -1, width)
        rows = lax.dynamic_index_in_dim(rows, lax.axis_index("dp") % copies, 1, False)
    return rows.reshape(-1, width)


def row_halves(own, is_first):
    half = own.shape[1] // 2
    low_half, high_half = own[:, :half], own[:, half:]
    kept = jnp.where(is_first, low_half, high_half)
    received = swapped(jnp.where(is_first, high_half, low_half))
    return (jnp.where(is_first, kept, received), jnp.where(is_first, received, kept))


def expert_in(rows):
    copies = lax.axis_size("dp") * lax.axis_size("section") // rows.shape[0]
    if copies > 1:
        rows = jnp.repeat(rows, copies, 0)
    return exchange(rows, LINE).reshape(-1, rows.shape[-1])


def expert_out(grad, experts):
    size = lax.axis_size("dp") * lax.axis_size("section")
    columns = grad.shape[1]
    pieces = exchange(grad.reshape(size, -1, columns), LINE)
    copies = size // experts
    if copies > 1:
        pieces = pieces.reshape(experts, copies, -1, columns).astype(F32)
        pieces = jnp.sum(pieces, 1).astype(BF)
    return pieces


def expert_home(homes):
    experts, rows, columns = homes[0].shape

    def pick(k, where):
        section = where[0]
        used = [section, 2 + section]
        return [
            (jnp.where((used[0] == source) | (used[1] == source), k, 0), 0, 0)
            for source in range(4)
        ]

    def kernel(k, where, sources, outs):
        for core in range(2):
            used = source_of(where[0], core)
            for source in range(4):

                @pl.when(used == source)
                def _():
                    outs[0][0, core * rows : (core + 1) * rows] = sources[source][0].astype(F32)

    shape = (experts, 2 * rows, columns)
    blocks = [(1, rows, columns)] * 4
    return pick_blocks(homes, blocks, pick, experts, kernel, [shape], [(1,) + shape[1:]])[0]


def routing(route_rows, turn_row, experts_all, capacity):
    expert_ids = jnp.arange(experts_all, dtype=jnp.int32)
    chosen = jnp.any(route_rows[:, :, None] == expert_ids[None, None, :], 1)
    earlier = (turn_row[None, :] < turn_row[:, None]).astype(BF)
    places = dot(earlier, chosen.astype(BF))
    place_of = jnp.where(chosen & (places < capacity), places, -1.0).astype(BF)
    slot_ids = jnp.arange(experts_all * capacity, dtype=jnp.int32)
    spread = (slot_ids[None, :] // capacity == expert_ids[:, None]).astype(BF)
    selected = dot(place_of, spread) == (slot_ids % capacity).astype(F32)[None, :]
    return chosen, selected, spread


def attention_forward(layer_in, visible, routed, dense_set, hook):
    attn_gain, w_query, w_key, w_value, w_out, ffn_gain, w_router = dense_set
    local_len = layer_in.shape[0]
    heads_kv = w_key.shape[1] // HEAD_SIZE
    normed, factor_one = normalize(layer_in, attn_gain)
    hidden_one = normed.astype(BF)
    key_rows = dot(hidden_one, w_key).astype(BF)
    value_rows = dot(hidden_one, w_value).astype(BF)
    kv_all = hook(gathered(jnp.concatenate([key_rows, value_rows], 1), 0))
    queries = dot(hidden_one, w_query).astype(BF)
    key_width = w_key.shape[1]
    key_all = kv_all[:, :key_width].reshape(-1, heads_kv, HEAD_SIZE)
    value_all = kv_all[:, key_width:].reshape(-1, heads_kv, HEAD_SIZE)
    grouped_query = queries.reshape(local_len, heads_kv, -1, HEAD_SIZE)
    raw = jnp.einsum("tkgd,skd->kgts", grouped_query, key_all, preferred_element_type=F32) * SCALE
    scores = jnp.where(visible[None, None], raw, masked_score)
    log_total = jax.nn.logsumexp(scores, -1, keepdims=True)
    attn_prob = jnp.exp(scores - log_total)
    attn_mix = jnp.einsum(
        "kgts,skd->tkgd", attn_prob.astype(BF), value_all, preferred_element_type=F32
    )
    attn_mix = attn_mix.reshape(local_len, -1).astype(BF)
    middle = layer_in + dot(attn_mix, w_out)
    normed_two, factor_two = normalize(middle, ffn_gain)
    hidden_two = normed_two.astype(BF)
    chosen, selected, spread = routed
    logits = dot(hidden_two, w_router)
    masked_logits = jnp.where(chosen, logits, masked_score)
    top = jnp.max(masked_logits, -1, keepdims=True)
    powers = jnp.where(chosen, jnp.exp(masked_logits - top), 0.0)
    gate_share = powers / jnp.sum(powers, -1, keepdims=True)
    weighting = jnp.where(selected, dot(gate_share.astype(BF), spread), 0.0).astype(BF)
    return {
        "layer_in": layer_in,
        "factor_one": factor_one,
        "hidden_one": hidden_one,
        "queries": queries,
        "key_all": key_all,
        "value_all": value_all,
        "attn_prob": attn_prob,
        "attn_mix": attn_mix,
        "middle": middle,
        "factor_two": factor_two,
        "hidden_two": hidden_two,
        "gate_share": gate_share,
        "selected": selected,
        "selector": selected.astype(BF),
        "spread": spread,
        "weighting": weighting,
    }


def expert_forward(arrived, w_gate, w_up):
    gate_pre = dot(arrived, w_gate)
    up_pre = dot(arrived, w_up)
    return gate_pre, up_pre, (jax.nn.silu(gate_pre) * up_pre).astype(BF)


def expert_backward(owed, gate_pre, up_pre, w_down):
    grad_inner = dot_t(owed, w_down)
    sigmoid_a = jax.nn.sigmoid(gate_pre)
    grad_gate_pre = grad_inner * up_pre * sigmoid_a * (1.0 + gate_pre * (1.0 - sigmoid_a))
    return grad_gate_pre.astype(BF), (grad_inner * gate_pre * sigmoid_a).astype(BF)


def router_backward(stored, grad_top, returned, w_router):
    match = jnp.where(stored["selected"], dot_t(grad_top, returned), 0.0)
    grad_weighting = lax.dot_general(
        match,
        stored["spread"].astype(F32),
        (((1,), (1,)), ((), ())),
        precision=lax.Precision.HIGHEST,
        preferred_element_type=F32,
    )
    gate_share = stored["gate_share"]
    grad_logits = (
        gate_share * (grad_weighting - jnp.sum(gate_share * grad_weighting, -1, keepdims=True))
    ).astype(BF)
    return t_dot(grad_logits, stored["hidden_two"]), dot_t(grad_logits, w_router)


def attention_backward(stored, grad_top, grad_router, grad_hidden, dense_set, hook):
    attn_gain, w_query, w_key, w_value, w_out, ffn_gain, w_router = dense_set
    local_len = grad_top.shape[0]
    grad_normed_two, grad_ffn_gain = norm_back(
        stored["middle"], stored["factor_two"], ffn_gain, grad_hidden
    )
    grad_middle = grad_top.astype(F32) + grad_normed_two
    grad_branch = hook("branch", grad_middle.astype(BF))
    grad_mix = dot_t(grad_branch, w_out).astype(BF)
    key_all = stored["key_all"]
    value_all = stored["value_all"]
    heads_kv = key_all.shape[1]
    attn_prob = stored["attn_prob"]
    grouped_grad = grad_mix.reshape(local_len, heads_kv, -1, HEAD_SIZE)
    grad_prob = jnp.einsum("tkgd,skd->kgts", grouped_grad, value_all, preferred_element_type=F32)
    centre = jnp.sum(attn_prob * grad_prob, -1, keepdims=True)
    grad_scores = (attn_prob * (grad_prob - centre)).astype(BF)
    grouped_query = stored["queries"].reshape(local_len, heads_kv, -1, HEAD_SIZE)
    grad_keys_all = (
        jnp.einsum("kgts,tkgd->skd", grad_scores, grouped_query, preferred_element_type=F32) * SCALE
    )
    grad_values_all = jnp.einsum(
        "kgts,tkgd->skd", attn_prob.astype(BF), grouped_grad, preferred_element_type=F32
    )
    tree_length = key_all.shape[0]
    grad_kv_all = jnp.concatenate(
        [grad_keys_all.reshape(tree_length, -1), grad_values_all.reshape(tree_length, -1)], 1
    ).astype(BF)
    grad_kv_all = hook("kv_all", grad_kv_all)
    grad_kv = sum_to_owner(grad_kv_all, 0).astype(BF)
    grad_queries = (
        jnp.einsum("kgts,skd->tkgd", grad_scores, key_all, preferred_element_type=F32) * SCALE
    )
    grad_queries = grad_queries.reshape(local_len, -1).astype(BF)
    key_width = w_key.shape[1]
    grad_keys, grad_values = grad_kv[:, :key_width], grad_kv[:, key_width:]
    grad_hidden_one = dot_t(grad_queries, w_query)
    grad_hidden_one = grad_hidden_one + dot_t(grad_keys, w_key)
    grad_hidden_one = grad_hidden_one + dot_t(grad_values, w_value)
    grad_normed_one, grad_attn_gain = norm_back(
        stored["layer_in"], stored["factor_one"], attn_gain, grad_hidden_one
    )
    grad_input = grad_middle + grad_normed_one
    small = jnp.concatenate([grad_router, grad_attn_gain[None], grad_ffn_gain[None]], 0)
    return {
        "input": grad_input,
        "branch": grad_branch,
        "qkv": jnp.concatenate([grad_queries, grad_kv], 1),
        "small": jnp.pad(small, ((0, -small.shape[0] % 16), (0, 0))),
    }


def local(
    edge_in,
    seg_lengths,
    routes,
    turns,
    attn_gain,
    w_query,
    w_key,
    w_value,
    w_out,
    ffn_gain,
    w_router,
    w_gate,
    w_up,
    w_down,
):
    edge_rows = edge_in[0, :, 0]
    local_len = edge_rows.shape[1]
    lengths_all = seg_lengths[:, 0]
    is_first = lax.axis_index("section") == 0

    def both_layers(own, received):
        return (jnp.where(is_first, own, received), jnp.where(is_first, received, own))

    def of_micro(pair):
        mine = jnp.where(is_first, pair[0], pair[1])
        others = jnp.where(is_first, pair[1], pair[0])
        return both_layers(mine, swapped(others))

    layer_rows, cotangent = of_micro(edge_rows)
    dense_own = (attn_gain[0], w_query[0], w_key[0], w_value[0], w_out[0], ffn_gain[0], w_router[0])
    dense_pairs = [both_layers(a, swapped(a)) for a in dense_own]
    dense_sets = [tuple(p[i] for p in dense_pairs) for i in range(2)]
    lengths_row = jnp.where(is_first, lengths_all[0], lengths_all[1])
    visible = tree_mask(lengths_row, local_len)
    experts_all, experts = w_router.shape[2], w_gate.shape[1]
    picks = routes.shape[4]
    capacity = local_len * picks // experts_all
    orders = of_micro(
        jnp.concatenate([jnp.swapaxes(routes[0, :, 0], 1, 2), turns[0, :, 0]], 1)
    )
    routed = [routing(o[:picks].T, o[picks], experts_all, capacity) for o in orders]
    gates, ups, downs = (row_halves(a[0], is_first) for a in (w_gate, w_up, w_down))

    gate_first, up_first = expert_in(gates[0]), expert_in(ups[0])
    first = attention_forward(
        layer_rows.astype(F32), visible, routed[0], dense_sets[0], lambda value: value
    )
    outgoing = t_dot(first["selector"], first["hidden_two"]).astype(BF)
    arrived_first = send_out(outgoing, experts_all)
    down_first = expert_in(downs[0])
    gate_pre, up_pre, inner_first = expert_forward(arrived_first, gate_first, up_first)
    pres_first = (gate_pre, up_pre)
    returned_first = send_back(dot(inner_first, down_first).astype(BF), experts_all)
    early = jnp.concatenate([first["hidden_one"], first["attn_mix"]], 0)
    early, returned_first = tie(early, returned_first)
    kept = {"early": early_operand(early)}

    def end(name, value):
        kept[name], value = tie(kept[name], value)
        return value

    state = (first["middle"] + dot(first["weighting"], returned_first)).astype(BF)

    gate_second, up_second = expert_in(gates[1]), expert_in(ups[1])
    second = attention_forward(
        state.astype(F32), visible, routed[1], dense_sets[1], lambda value: end("early", value)
    )
    outgoing = t_dot(second["selector"], second["hidden_two"]).astype(BF)
    early_first = kept["early"]
    arrived_second = send_out(outgoing, experts_all)
    early = jnp.concatenate([second["hidden_one"], second["attn_mix"]], 0)
    early, arrived_second = tie(early, arrived_second)
    early_second = early_operand(early)
    owed_second = send_out(t_dot(second["weighting"], cotangent).astype(BF), experts_all)
    down_second = expert_in(downs[1])
    gate_pre, up_pre, inner_second = expert_forward(arrived_second, gate_second, up_second)
    grad_gate_pre, grad_up_pre = expert_backward(owed_second, gate_pre, up_pre, down_second)
    grad_arrived = (dot_t(grad_gate_pre, gate_second) + dot_t(grad_up_pre, up_second)).astype(BF)
    early_second, grad_arrived = tie(early_second, grad_arrived)
    returned_second = send_back(dot(inner_second, down_second).astype(BF), experts_all)
    sent_second = send_back(grad_arrived, experts_all)
    top = second["middle"] + dot(second["weighting"], returned_second)
    top_other = lax.ppermute(top, "section", UP)
    expert_grads = [t_dot(arrived_second, g).astype(BF) for g in (grad_gate_pre, grad_up_pre)]
    expert_grads.append(t_dot(inner_second, owed_second).astype(BF))
    sent_second, expert_grads = tie(sent_second, expert_grads)

    kept["gate"] = expert_out(expert_grads[0], experts)
    grad_router, grad_hidden = router_backward(
        second, cotangent, returned_second, dense_sets[1][6]
    )
    grad_hidden = grad_hidden + dot(second["selector"], sent_second)

    def later_hook(name, value):
        return end("gate", value) if name == "kv_all" else value

    later = attention_backward(
        second, cotangent, grad_router, grad_hidden, dense_sets[1], later_hook
    )
    grad = later["input"].astype(BF)
    branch, qkv, grad = tie(later["branch"], later["qkv"], grad)
    late = late_operands([branch, qkv])
    width = late[0].shape[1]
    outgoing = t_dot(first["weighting"], grad).astype(BF)
    owed_first = send_out(outgoing, experts_all)
    late, owed_first, up_grad = tie(late, owed_first, expert_grads[1])
    kept["up"] = expert_out(up_grad, experts)
    hidden_early, mix_early = early_second
    kept["dense"] = dense_rows(dense_partial([mix_early, hidden_early], late))
    grad_gate_pre, grad_up_pre = expert_backward(owed_first, *pres_first, down_first)
    grad_arrived = (dot_t(grad_gate_pre, gate_first) + dot_t(grad_up_pre, up_first)).astype(BF)
    first_grads = [t_dot(arrived_first, g).astype(BF) for g in (grad_gate_pre, grad_up_pre)]
    first_grads.append(t_dot(inner_first, owed_first).astype(BF))
    grad_arrived, first_grads = tie(grad_arrived, first_grads)
    sent_first = send_back(end("dense", end("up", grad_arrived)), experts_all)
    down_grad, sent_first = tie(expert_grads[2], sent_first)
    kept["down"] = expert_out(down_grad, experts)
    kept["dense"], sent_first = tie(kept["dense"], sent_first)
    kept["dense"] = dense_line(kept["dense"])
    grad_router, grad_hidden = router_backward(first, grad, returned_first, dense_sets[0][6])
    grad_hidden = grad_hidden + dot(first["selector"], sent_first)

    def hook(name, value):
        if name == "branch":
            kept["late"] = late_operands([value])
        if name == "kv_all":
            value = end("dense", end("down", end("late", value)))
            kept["dense"] = dense_groups(kept["dense"])
            kept["out"] = dense_partial([early_first[1]], kept["late"])
            return end("out", value)
        return value

    earlier = attention_backward(
        first, grad, grad_router, grad_hidden, dense_sets[0], hook
    )
    out_second = [kept[name] for name in ("gate", "up", "down")]
    ending, gate_grad = tie(earlier["qkv"], first_grads[0])
    gate_part = expert_out(gate_grad, experts)
    out_total = dense_line(dense_rows(kept["out"]))
    qkv_total = dense_partial([early_first[0]], late_operands([ending]))
    smalls = small_total(jnp.concatenate([earlier["small"], later["small"]], 0))
    gate_part, qkv_total, out_total, smalls = tie(gate_part, qkv_total, out_total, smalls)
    out_total = dense_groups(out_total)
    qkv_total = dense_line(dense_rows(qkv_total))
    qkv_total, up_grad, second_total = tie(qkv_total, first_grads[1], kept["dense"])
    up_part = expert_out(up_grad, experts)
    qkv_total = dense_groups(qkv_total)
    gate_total = expert_home(two_homes(gate_part, out_second[0]))
    out = dense_home(two_homes(out_total, second_total[..., :width]), [w_out.shape[2]])[0]
    up_part, down_grad, gate_total, out, qkv_total, smalls = tie(
        up_part, first_grads[2], gate_total, out, qkv_total, smalls
    )
    down_part = expert_out(down_grad, experts)
    up_total = expert_home(two_homes(up_part, out_second[1]))
    query, key, value = dense_home(
        two_homes(qkv_total, second_total[..., width:]),
        [w_query.shape[2], w_key.shape[2], w_value.shape[2]],
    )
    small = jnp.where(is_first, *jnp.split(smalls, 2, 0))
    grad = earlier["input"]
    grad_other = lax.ppermute(grad, "section", DOWN)
    edge_out = jnp.where(
        is_first, jnp.stack([grad, grad_other]), jnp.stack([top_other, top])
    )[None, :, None]
    down_part, up_total, query, key, value, edge_out = tie(
        down_part, up_total, query, key, value, edge_out
    )
    expert_total = [gate_total, up_total, expert_home(two_homes(down_part, out_second[2]))]
    dense_out = (
        small[experts_all],
        query,
        key,
        value,
        out,
        small[experts_all + 1],
        small[:experts_all].T,
    )
    return (
        (edge_out,)
        + tuple((piece[None] for piece in dense_out))
        + tuple((piece[None] for piece in expert_total))
    )


def solution(mesh):
    placed = (
        P("section", None, "expert", "dp", None),
        P(None, "expert", None),
        P("section", None, "expert", "dp", None),
        P("section", None, "expert", "dp", None),
        P("section", None),
        P("section", None, None),
        P("section", None, None),
        P("section", None, None),
        P("section", None, None),
        P("section", None),
        P("section", None, None),
        P("section", "expert", "dp", None),
        P("section", "expert", "dp", None),
        P("section", "expert", "dp", None),
    )
    return jax.shard_map(
        local,
        mesh=mesh,
        in_specs=placed,
        out_specs=(
            P("section", None, "expert", "dp", None),
            P("section", None),
            P("section", None, None),
            P("section", None, None),
            P("section", None, None),
            P("section", None, None),
            P("section", None),
            P("section", None, None),
            P("section", "expert", "dp", None),
            P("section", "expert", "dp", None),
            P("section", "expert", "dp", None),
        ),
        check_vma=False,
    )
```

```python
from types import SimpleNamespace

import jax
import jax.numpy as jnp
import numpy as np
from jax import lax
from jax.experimental import pallas as pl
from jax.experimental.pallas import tpu as pltpu
from jax.sharding import PartitionSpec as P

HEAD_SIZE = 128
SCALE = HEAD_SIZE ** (-0.5)
epsilon = 1e-06
masked_score = -1e30
BF = jnp.bfloat16
F32 = jnp.float32

SWAP = [(0, 1), (1, 0)]
UP = [(0, 1)]
DOWN = [(1, 0)]
OWNERS = ("expert", "dp", "section")
LINE = ("dp", "section")


def ancestry():
    parents = [-1]
    for branch_index in range(4):
        parents += [0, 1 + 3 * branch_index, 1 + 3 * branch_index]
    lineage = np.zeros((13, 13), np.float32)
    for segment in range(13):
        current = segment
        while current >= 0:
            lineage[current, segment] = 1.0
            current = parents[current]
    return lineage


def dot(left, right):
    return jnp.dot(left, right, preferred_element_type=F32)


def dot_t(left, right):
    return lax.dot_general(left, right, (((1,), (1,)), ((), ())), preferred_element_type=F32)


def t_dot(left, right):
    return lax.dot_general(left, right, (((0,), (0,)), ((), ())), preferred_element_type=F32)


def t_dot_t(left, right):
    return lax.dot_general(left, right, (((0,), (1,)), ((), ())), preferred_element_type=F32)


def normalize(values, gain_vec):
    factor = lax.rsqrt(jnp.mean(values * values, -1, keepdims=True) + epsilon)
    return (values * factor * gain_vec, factor)


def norm_back(values, factor, gain_vec, upstream):
    scaled = upstream * gain_vec
    grad_gain = jnp.sum(upstream * values * factor, 0)
    inner_mean = jnp.mean(scaled * values, -1, keepdims=True)
    return (scaled * factor - values * factor * factor * factor * inner_mean, grad_gain)


def tree_mask(lengths_row, local_len):
    own = lax.axis_index("dp")
    first_row = own * local_len
    seg_ends = jnp.cumsum(lengths_row)
    blocks = own ^ jnp.asarray(block_order(), jnp.int32)
    key_spots = (
        blocks[:, None] * local_len + jnp.arange(local_len, dtype=jnp.int32)[None, :]
    ).reshape(-1)
    query_spots = first_row + jnp.arange(local_len, dtype=jnp.int32)
    seg_ids = jnp.arange(13, dtype=jnp.int32)
    key_seg = jnp.sum((key_spots[:, None] >= seg_ends[None, :]).astype(jnp.int32), 1)
    query_seg = jnp.sum((query_spots[:, None] >= seg_ends[None, :]).astype(jnp.int32), 1)
    key_hot = (key_seg[:, None] == seg_ids[None, :]).astype(BF)
    query_hot = (query_seg[:, None] == seg_ids[None, :]).astype(BF)
    allowed = dot(query_hot, jnp.asarray(ancestry(), BF)).astype(BF)
    linked = dot_t(allowed, key_hot) > 0.5
    return linked & (key_spots[None, :] <= query_spots[:, None])


def tie(*values):
    return lax.optimization_barrier(values)


def swapped(shard):
    return lax.ppermute(shard, "section", SWAP)


def partners(axis, flip):
    return [(i, i ^ flip) for i in range(lax.axis_size(axis))]


def flips(axis):
    found = [1]
    while 2 * found[-1] < lax.axis_size(axis):
        found.append(2 * found[-1])
    return found


def block_order():
    order = [0]
    for flip in reversed(flips("dp")):
        order = order + [k ^ flip for k in order]
    return order


def gathered(shard, axis, over="dp"):
    for flip in reversed(flips(over)):
        shard = jnp.concatenate([shard, lax.ppermute(shard, over, partners(over, flip))], axis)
    return shard


def sum_to_owner(partial, axis):
    sent_as = partial.dtype
    for flip in flips("dp"):
        kept, sent = jnp.split(partial, 2, axis)
        sent = lax.ppermute(sent.astype(sent_as), "dp", partners("dp", flip))
        partial = kept.astype(F32) + sent.astype(F32)
    return partial


def pick_blocks(sources, blocks, pick, count, kernel, out_shapes, out_blocks):
    where = jnp.stack([lax.axis_index(axis) for axis in ("section", "dp")]).astype(jnp.int32)

    def spec(at):
        def index(k, where):
            return pick(k, where)[at]

        return pl.BlockSpec(blocks[at], index)

    def body(where, *refs):
        kernel(pl.program_id(0), where, refs[: len(sources)], refs[len(sources) :])

    return pl.pallas_call(
        body,
        grid_spec=pltpu.PrefetchScalarGridSpec(
            num_scalar_prefetch=1,
            grid=(count,),
            in_specs=[spec(at) for at in range(len(sources))],
            out_specs=[
                pl.BlockSpec(shape, lambda k, where: (k,) + (0,) * (len(shape) - 1))
                for shape in out_blocks
            ],
        ),
        out_shape=[jax.ShapeDtypeStruct(shape, F32) for shape in out_shapes],
        compiler_params=pltpu.CompilerParams(vmem_limit_bytes=48 * 1024 * 1024),
    )(where, *sources)


def two_homes(first, second):
    return (
        first,
        second,
        lax.ppermute(first, "section", DOWN),
        lax.ppermute(second, "section", UP),
    )


def source_of(section, core):
    return jnp.where(core == section, section, 2 + section)


def dense_home(homes, offsets, width, out_widths):
    parts, groups, rows, _ = homes[0].shape
    block = rows // 2

    def pick(k, where):
        used = source_of(where[0], k // (2 * parts))
        return [
            (jnp.where(used == source, k // 2 % parts, 0), 0, jnp.where(used == source, k % 2, 0), 0)
            for source in range(4)
        ]

    def kernel(k, where, sources, outs):
        used = source_of(where[0], k // (2 * parts))
        for source in range(4):

            @pl.when(used == source)
            def _():
                out, at = 0, 0
                for group in range(groups):
                    start = offsets[source]
                    stop = start + width
                    while start < stop:
                        piece = min(stop - start, out_widths[out] - at)
                        outs[out][:, at : at + piece] = sources[source][
                            0, group, :, start : start + piece
                        ].astype(F32)
                        start, at = start + piece, at + piece
                        if at == out_widths[out]:
                            out, at = out + 1, 0

    count = 4 * parts
    shapes = [(count * block, w) for w in out_widths]
    blocks = [(1, groups, block, home.shape[3]) for home in homes]
    return pick_blocks(
        homes, blocks, pick, count, kernel, shapes, [(block, w) for w in out_widths]
    )


def two_parts(array, index, axis=0):
    half = array.shape[axis] // 2
    return (
        lax.dynamic_slice_in_dim(array, index * half, half, axis),
        lax.dynamic_slice_in_dim(array, (1 - index) * half, half, axis),
    )


def in_order(mine, others, index, axis):
    first = index == 0
    return jnp.concatenate(
        [jnp.where(first, mine, others), jnp.where(first, others, mine)], axis
    )


def early_operand(rows):
    mine, others = two_parts(rows, lax.axis_index("section"), 1)
    half = mine.shape[1]
    joined = jnp.stack([mine.reshape(2, -1, half), swapped(others).reshape(2, -1, half)], 1)
    return gathered(joined[:, None], 1, "expert").reshape(2, -1, half)


def late_operands(operands):
    groups = lax.axis_size("expert")
    own = lax.axis_index("expert")
    blocks = []
    order = [0]
    for flip in reversed(flips("expert")):
        order = order + [k ^ flip for k in order]
    for flip in order:
        shares = []
        for rows in operands:
            share = rows.shape[1] // groups
            shares.append(lax.dynamic_slice_in_dim(rows, (own ^ flip) * share, share, 1))
        block = jnp.concatenate(shares, 1)
        if flip > 0:
            block = lax.ppermute(block, "expert", partners("expert", flip))
        blocks.append(block)
    joined = jnp.stack(blocks)
    joined = jnp.stack([joined, swapped(joined)], 1)
    joined = joined.reshape(-1, joined.shape[-1])
    return jnp.split(joined, np.cumsum([a.shape[1] // groups for a in operands])[:-1], 1)


def dense_partial(early, late):
    return jnp.concatenate([t_dot(e, p) for e, p in zip(early, late, strict=True)], 1)


def dense_rows(partial):
    for flip in flips("dp"):
        partial = dense_rows_step(partial, flip)
    return partial.astype(BF)


def dense_rows_step(partial, flip):
    own = lax.axis_index("dp")
    kept, sent = two_parts(partial, jnp.where((own & flip) == 0, 0, 1))
    sent = lax.ppermute(sent.astype(BF), "dp", partners("dp", flip))
    return kept.astype(F32) + sent.astype(F32)


def dense_line(total):
    own = lax.axis_index("dp")
    for flip in reversed(flips("dp")):
        others = lax.ppermute(total, "dp", partners("dp", flip))
        total = in_order(total, others, own & flip, 0)
    return total


def group_parts(total):
    axes = (1,) * len(flips("expert"))
    return [part.reshape(axes + part.shape) for part in jnp.split(total, 2, 0)]


def group_step(parts, index):
    own = lax.axis_index("expert")
    order = flips("expert")
    stepped = []
    for part, way in zip(parts, (order, order[::-1]), strict=True):
        flip = way[index]
        others = lax.ppermute(part, "expert", partners("expert", flip))
        axis = len(order) - 1 - order.index(flip)
        stepped.append(in_order(part, others, own & flip, axis))
    return stepped


def group_join(parts):
    return jnp.stack([part.reshape((-1,) + part.shape[-2:]) for part in parts])


def dense_groups(total):
    parts = group_parts(total)
    for index in range(len(flips("expert"))):
        parts = group_step(parts, index)
    return group_join(parts)


def small_step(partial, axis, flip):
    return partial + lax.ppermute(partial.astype(BF), axis, partners(axis, flip)).astype(F32)


def exchange(rows, axes):
    return lax.all_to_all(rows, axes, split_axis=0, concat_axis=0, tiled=True)


def copies_of_expert(experts_all):
    owners = lax.axis_size("expert") * lax.axis_size("dp") * lax.axis_size("section")
    return owners // experts_all


def send_out(slot_rows, experts_all):
    width = slot_rows.shape[-1]
    copies = copies_of_expert(experts_all)
    rows = slot_rows.reshape(experts_all, -1, width)
    if copies > 1:
        mine = jnp.arange(copies) == lax.axis_index("dp") % copies
        rows = jnp.where(mine[None, :, None, None], rows[:, None], 0)
        rows = rows.reshape(experts_all * copies, -1, width)
    return exchange(rows, OWNERS).reshape(-1, width)


def send_back(rows, experts_all):
    width = rows.shape[-1]
    copies = copies_of_expert(experts_all)
    rows = exchange(rows.reshape(experts_all * copies, -1, width), OWNERS)
    if copies > 1:
        rows = rows.reshape(experts_all, copies, -1, width)
        rows = lax.dynamic_index_in_dim(rows, lax.axis_index("dp") % copies, 1, False)
    return rows.reshape(-1, width)


def row_halves(own, is_first):
    half = own.shape[1] // 2
    received = swapped(two_parts(own, lax.axis_index("section"), 1)[1])
    return (
        jnp.where(is_first, own[:, :half], received),
        jnp.where(is_first, received, own[:, half:]),
    )


def expert_in(rows):
    copies = lax.axis_size("dp") * lax.axis_size("section") // rows.shape[0]
    if copies > 1:
        rows = jnp.repeat(rows, copies, 0)
    return exchange(rows, LINE).reshape(-1, rows.shape[-1])


def expert_out(grad, experts):
    size = lax.axis_size("dp") * lax.axis_size("section")
    columns = grad.shape[1]
    pieces = exchange(grad.reshape(size, -1, columns), LINE)
    copies = size // experts
    if copies > 1:
        pieces = pieces.reshape(experts, copies, -1, columns).astype(F32)
        pieces = jnp.sum(pieces, 1).astype(BF)
    return pieces


def expert_home(homes, count=1):
    experts, rows, width = homes[0].shape
    columns = width // count

    def pick(k, where):
        section = where[0]
        used = [section, 2 + section]
        return [
            (jnp.where((used[0] == source) | (used[1] == source), k, 0), 0, 0)
            for source in range(4)
        ]

    def kernel(k, where, sources, outs):
        for core in range(2):
            used = source_of(where[0], core)
            for source in range(4):

                @pl.when(used == source)
                def _():
                    for part, out in enumerate(outs):
                        out[0, core * rows : (core + 1) * rows] = sources[source][
                            0, :, part * columns : (part + 1) * columns
                        ].astype(F32)

    shape = (experts, 2 * rows, columns)
    blocks = [(1, rows, width)] * 4
    return list(
        pick_blocks(homes, blocks, pick, experts, kernel, [shape] * count, [(1,) + shape[1:]] * count)
    )


def routing(route_rows, turn_row, experts_all, capacity):
    expert_ids = jnp.arange(experts_all, dtype=jnp.int32)
    chosen = jnp.any(route_rows[:, :, None] == expert_ids[None, None, :], 1)
    earlier = (turn_row[None, :] < turn_row[:, None]).astype(BF)
    places = dot(earlier, chosen.astype(BF))
    place_of = jnp.where(chosen & (places < capacity), places, -1.0).astype(BF)
    slot_ids = jnp.arange(experts_all * capacity, dtype=jnp.int32)
    spread = (slot_ids[None, :] // capacity == expert_ids[:, None]).astype(BF)
    selected = dot(place_of, spread) == (slot_ids % capacity).astype(F32)[None, :]
    return chosen, selected, spread


def attention_forward(layer_in, visible, routed, dense_set, hook):
    attn_gain, w_query, w_key, w_value, w_out, ffn_gain, w_router = dense_set
    local_len = layer_in.shape[0]
    heads_kv = w_key.shape[1] // HEAD_SIZE
    normed, factor_one = normalize(layer_in, attn_gain)
    hidden_one = normed.astype(BF)
    key_rows = dot(hidden_one, w_key).astype(BF)
    value_rows = dot(hidden_one, w_value).astype(BF)
    kv_all = hook(gathered(jnp.concatenate([key_rows, value_rows], 1), 0))
    queries = dot(hidden_one, w_query).astype(BF)
    key_width = w_key.shape[1]
    key_all = kv_all[:, :key_width].reshape(-1, heads_kv, HEAD_SIZE)
    value_all = kv_all[:, key_width:].reshape(-1, heads_kv, HEAD_SIZE)
    grouped_query = queries.reshape(local_len, heads_kv, -1, HEAD_SIZE)
    raw = jnp.einsum("tkgd,skd->kgts", grouped_query, key_all, preferred_element_type=F32) * SCALE
    scores = jnp.where(visible[None, None], raw, masked_score)
    log_total = jax.nn.logsumexp(scores, -1, keepdims=True)
    attn_prob = jnp.exp(scores - log_total)
    attn_mix = jnp.einsum(
        "kgts,skd->tkgd", attn_prob.astype(BF), value_all, preferred_element_type=F32
    )
    attn_mix = attn_mix.reshape(local_len, -1).astype(BF)
    middle = layer_in + dot(attn_mix, w_out)
    normed_two, factor_two = normalize(middle, ffn_gain)
    hidden_two = normed_two.astype(BF)
    chosen, selected, spread = routed
    logits = dot(hidden_two, w_router)
    masked_logits = jnp.where(chosen, logits, masked_score)
    top = jnp.max(masked_logits, -1, keepdims=True)
    powers = jnp.where(chosen, jnp.exp(masked_logits - top), 0.0)
    gate_share = powers / jnp.sum(powers, -1, keepdims=True)
    weighting = jnp.where(selected, dot(gate_share.astype(BF), spread), 0.0).astype(BF)
    return SimpleNamespace(
        layer_in=layer_in,
        factor_one=factor_one,
        hidden_one=hidden_one,
        queries=queries,
        key_all=key_all,
        value_all=value_all,
        attn_prob=attn_prob,
        attn_mix=attn_mix,
        middle=middle,
        factor_two=factor_two,
        hidden_two=hidden_two,
        gate_share=gate_share,
        selected=selected,
        selector=selected.astype(BF),
        spread=spread,
        weighting=weighting,
    )


def expert_forward(arrived, w_gate, w_up):
    gate_pre = dot(arrived, w_gate)
    up_pre = dot(arrived, w_up)
    return gate_pre, up_pre, (jax.nn.silu(gate_pre) * up_pre).astype(BF)


def expert_backward(owed, gate_pre, up_pre, w_down):
    grad_inner = dot_t(owed, w_down)
    sigmoid_a = jax.nn.sigmoid(gate_pre)
    grad_gate_pre = grad_inner * up_pre * sigmoid_a * (1.0 + gate_pre * (1.0 - sigmoid_a))
    return jnp.concatenate([grad_gate_pre, grad_inner * gate_pre * sigmoid_a], 1).astype(BF)


def expert_input(grad_pre, w_gate, w_up):
    width = w_gate.shape[1]
    return dot_t(grad_pre[:, :width], w_gate) + dot_t(grad_pre[:, width:], w_up)


def router_backward(stored, grad_top, returned, w_router):
    match = jnp.where(stored.selected, dot_t(grad_top, returned), 0.0)
    grad_weighting = lax.dot_general(
        match,
        stored.spread.astype(F32),
        (((1,), (1,)), ((), ())),
        precision=lax.Precision.HIGHEST,
        preferred_element_type=F32,
    )
    gate_share = stored.gate_share
    grad_logits = (
        gate_share * (grad_weighting - jnp.sum(gate_share * grad_weighting, -1, keepdims=True))
    ).astype(BF)
    return t_dot(grad_logits, stored.hidden_two), dot_t(grad_logits, w_router)


def attention_backward(stored, grad_top, grad_router, grad_hidden, dense_set, hook):
    attn_gain, w_query, w_key, w_value, w_out, ffn_gain, w_router = dense_set
    local_len = grad_top.shape[0]
    grad_normed_two, grad_ffn_gain = norm_back(
        stored.middle, stored.factor_two, ffn_gain, grad_hidden
    )
    grad_middle = grad_top.astype(F32) + grad_normed_two
    grad_branch = hook("branch", grad_middle.astype(BF))
    grad_mix = dot_t(grad_branch, w_out).astype(BF)
    key_all = stored.key_all
    value_all = stored.value_all
    heads_kv = key_all.shape[1]
    attn_prob = stored.attn_prob
    grouped_grad = grad_mix.reshape(local_len, heads_kv, -1, HEAD_SIZE)
    grad_prob = jnp.einsum("tkgd,skd->kgts", grouped_grad, value_all, preferred_element_type=F32)
    centre = jnp.sum(attn_prob * grad_prob, -1, keepdims=True)
    grad_scores = (attn_prob * (grad_prob - centre)).astype(BF)
    grouped_query = stored.queries.reshape(local_len, heads_kv, -1, HEAD_SIZE)
    grad_keys_all = (
        jnp.einsum("kgts,tkgd->skd", grad_scores, grouped_query, preferred_element_type=F32) * SCALE
    )
    grad_values_all = jnp.einsum(
        "kgts,tkgd->skd", attn_prob.astype(BF), grouped_grad, preferred_element_type=F32
    )
    tree_length = key_all.shape[0]
    grad_kv_all = jnp.concatenate(
        [grad_keys_all.reshape(tree_length, -1), grad_values_all.reshape(tree_length, -1)], 1
    ).astype(BF)
    grad_kv_all = hook("kv_all", grad_kv_all)
    grad_kv = hook("kv", sum_to_owner(grad_kv_all, 0).astype(BF))
    grad_queries = (
        jnp.einsum("kgts,skd->tkgd", grad_scores, key_all, preferred_element_type=F32) * SCALE
    )
    grad_queries = grad_queries.reshape(local_len, -1).astype(BF)
    key_width = w_key.shape[1]
    grad_keys, grad_values = grad_kv[:, :key_width], grad_kv[:, key_width:]
    grad_hidden_one = dot_t(grad_queries, w_query)
    grad_hidden_one = grad_hidden_one + dot_t(grad_keys, w_key)
    grad_hidden_one = grad_hidden_one + dot_t(grad_values, w_value)
    grad_normed_one, grad_attn_gain = norm_back(
        stored.layer_in, stored.factor_one, attn_gain, grad_hidden_one
    )
    grad_input = grad_middle + grad_normed_one
    small = jnp.concatenate([grad_router, grad_attn_gain[None], grad_ffn_gain[None]], 0)
    return SimpleNamespace(
        input=grad_input,
        branch=grad_branch,
        qkv=jnp.concatenate([grad_queries, grad_kv], 1),
        small=jnp.pad(small, ((0, -small.shape[0] % 16), (0, 0))),
    )


def local(
    edge_in,
    seg_lengths,
    routes,
    turns,
    attn_gain,
    w_query,
    w_key,
    w_value,
    w_out,
    ffn_gain,
    w_router,
    w_gate,
    w_up,
    w_down,
):
    edge_rows = edge_in[0, :, 0]
    local_len = edge_rows.shape[1]
    lengths_all = seg_lengths[:, 0]
    is_first = lax.axis_index("section") == 0

    def both_layers(own, received):
        return (jnp.where(is_first, own, received), jnp.where(is_first, received, own))

    def of_micro(pair):
        mine = jnp.where(is_first, pair[0], pair[1])
        others = jnp.where(is_first, pair[1], pair[0])
        return both_layers(mine, swapped(others))

    layer_rows, cotangent = of_micro(edge_rows)
    dense_own = (attn_gain[0], w_query[0], w_key[0], w_value[0], w_out[0], ffn_gain[0], w_router[0])
    dense_pairs = [both_layers(a, swapped(a)) for a in dense_own]
    dense_sets = [tuple(p[i] for p in dense_pairs) for i in range(2)]
    lengths_row = jnp.where(is_first, lengths_all[0], lengths_all[1])
    visible = tree_mask(lengths_row, local_len)
    experts_all, experts = w_router.shape[2], w_gate.shape[1]
    picks = routes.shape[4]
    capacity = local_len * picks // experts_all
    orders = of_micro(
        jnp.concatenate([jnp.swapaxes(routes[0, :, 0], 1, 2), turns[0, :, 0]], 1)
    )
    routed = [routing(o[:picks].T, o[picks], experts_all, capacity) for o in orders]
    gates, ups, downs = (row_halves(a[0], is_first) for a in (w_gate, w_up, w_down))

    gate_first, up_first = expert_in(gates[0]), expert_in(ups[0])
    first = attention_forward(
        layer_rows.astype(F32), visible, routed[0], dense_sets[0], lambda value: value
    )
    outgoing = t_dot(first.selector, first.hidden_two).astype(BF)
    arrived_first = send_out(outgoing, experts_all)
    down_first = expert_in(downs[0])
    gate_pre, up_pre, inner_first = expert_forward(arrived_first, gate_first, up_first)
    pres_first = (gate_pre, up_pre)
    returned_first = send_back(dot(inner_first, down_first).astype(BF), experts_all)
    early = jnp.concatenate([first.hidden_one, first.attn_mix], 0)
    early, returned_first = tie(early, returned_first)
    kept = SimpleNamespace(early=early_operand(early))

    def end(name, value):
        got, value = tie(getattr(kept, name), value)
        setattr(kept, name, got)
        return value

    state = (first.middle + dot(first.weighting, returned_first)).astype(BF)
    gate_second, up_second = expert_in(gates[1]), expert_in(ups[1])
    second = attention_forward(
        state.astype(F32), visible, routed[1], dense_sets[1], lambda value: end("early", value)
    )
    early_first = kept.early
    outgoing = jnp.concatenate(
        [t_dot(second.selector, second.hidden_two), t_dot(second.weighting, cotangent)], 1
    ).astype(BF)
    outgoing = send_out(outgoing, experts_all)
    early = jnp.concatenate([second.hidden_one, second.attn_mix], 0)
    early, outgoing = tie(early, outgoing)
    early_second = early_operand(early)
    arrived_second, owed_second = jnp.split(outgoing, 2, 1)
    down_second = expert_in(downs[1])
    gate_pre, up_pre, inner_second = expert_forward(arrived_second, gate_second, up_second)
    grad_pre = expert_backward(owed_second, gate_pre, up_pre, down_second)
    early_second, grad_pre = tie(early_second, grad_pre)
    produced = jnp.concatenate(
        [dot(inner_second, down_second), expert_input(grad_pre, gate_second, up_second)], 1
    ).astype(BF)
    produced = send_back(produced, experts_all)
    gate_up_grad = t_dot(arrived_second, grad_pre).astype(BF)
    down_grad = t_dot(inner_second, owed_second).astype(BF)
    produced, gate_up_grad, down_grad = tie(produced, gate_up_grad, down_grad)
    kept.down1 = expert_out(down_grad, experts)
    returned_second, sent_second = jnp.split(produced, 2, 1)
    top = second.middle + dot(second.weighting, returned_second)
    top_other = lax.ppermute(top, "section", UP)

    grad_router, grad_hidden = router_backward(
        second, cotangent, returned_second, dense_sets[1][6]
    )
    grad_hidden = grad_hidden + dot(second.selector, sent_second)
    later = attention_backward(
        second,
        cotangent,
        grad_router,
        grad_hidden,
        dense_sets[1],
        lambda name, value: end("down1", value) if name == "kv_all" else value,
    )
    grad = later.input.astype(BF)
    branch, qkv, grad = tie(later.branch, later.qkv, grad)
    late = late_operands([branch, qkv])
    width = late[0].shape[1]
    owed_first = send_out(t_dot(first.weighting, grad).astype(BF), experts_all)
    late, owed_first = tie(late, owed_first)
    hidden_early, mix_early = early_second
    kept.dense = dense_rows(dense_partial([mix_early, hidden_early], late))
    grad_pre = expert_backward(owed_first, *pres_first, down_first)
    grad_arrived = expert_input(grad_pre, gate_first, up_first).astype(BF)
    first_grads = [t_dot(arrived_first, grad_pre).astype(BF)]
    first_grads.append(t_dot(inner_first, owed_first).astype(BF))
    sent_first = send_back(end("dense", grad_arrived), experts_all)
    kept.dense, sent_first = tie(kept.dense, sent_first)
    kept.dense, gate_up_grad = tie(dense_line(kept.dense), gate_up_grad)
    kept.gate_up1 = expert_out(gate_up_grad, experts)
    grad_router, grad_hidden = router_backward(first, grad, returned_first, dense_sets[0][6])
    grad_hidden = grad_hidden + dot(first.selector, sent_first)

    def hook(name, value):
        if name == "branch":
            kept.late = late_operands([value])
        if name == "kv_all":
            value = end("late", value)
            kept.out = dense_partial([early_first[1]], kept.late)
            kept.dense = dense_groups(kept.dense)
            value = end("dense", end("out", end("gate_up1", value)))
        if name == "kv":
            down_grad, value, kept.out = tie(first_grads[1], value, kept.out)
            kept.down0 = expert_out(down_grad, experts)
        return value

    earlier = attention_backward(
        first, grad, grad_router, grad_hidden, dense_sets[0], hook
    )
    smalls = jnp.concatenate([earlier.small, later.small], 0)
    for axis in ("section", "expert"):
        for flip in flips(axis):
            smalls = small_step(smalls, axis, flip)
    qkv_total = dense_partial([early_first[0]], late_operands([earlier.qkv]))
    qkv_total, smalls, down_part, out_total = tie(qkv_total, smalls, kept.down0, kept.out)
    for flip in flips("dp"):
        qkv_total = dense_rows_step(qkv_total, flip)
        out_total = dense_rows_step(out_total, flip)
        smalls = small_step(smalls, "dp", flip)
        qkv_total, out_total, smalls = tie(qkv_total, out_total, smalls)
    qkv_total, out_total = dense_line(qkv_total.astype(BF)), dense_line(out_total.astype(BF))
    qkv_total, out_total, gate_up_grad = tie(qkv_total, out_total, first_grads[0])
    gate_up_part = expert_out(gate_up_grad, experts)
    second_total = kept.dense
    second_other = lax.ppermute(second_total, "section", UP)
    down_total = expert_home(two_homes(down_part, kept.down1))
    out_total = dense_groups(out_total)
    out_other = lax.ppermute(out_total, "section", DOWN)
    homes = (out_total, second_total, out_other, second_other)
    out = dense_home(homes, [0] * 4, width, [w_out.shape[2]])[0]
    qkv_total = dense_groups(qkv_total)
    qkv_other = lax.ppermute(qkv_total, "section", DOWN)
    homes = (qkv_total, second_total, qkv_other, second_other)
    query, key, value = dense_home(
        homes,
        [0, width, 0, width],
        qkv_total.shape[3],
        [w_query.shape[2], w_key.shape[2], w_value.shape[2]],
    )
    small = jnp.where(is_first, *jnp.split(smalls, 2, 0))
    grad = earlier.input
    grad_other = lax.ppermute(grad, "section", DOWN)
    edge_out = jnp.where(
        is_first, jnp.stack([grad, grad_other]), jnp.stack([top_other, top])
    )[None, :, None]
    gate_up_part, down_total, out, query, key, value, edge_out = tie(
        gate_up_part, down_total, out, query, key, value, edge_out
    )
    expert_total = expert_home(two_homes(gate_up_part, kept.gate_up1), 2) + down_total
    dense_out = (
        small[experts_all],
        query,
        key,
        value,
        out,
        small[experts_all + 1],
        small[:experts_all].T,
    )
    return (
        (edge_out,)
        + tuple((piece[None] for piece in dense_out))
        + tuple((piece[None] for piece in expert_total))
    )


def solution(mesh):
    section, expert, dp = "section", "expert", "dp"
    tokens = P(section, None, expert, dp, None)
    vector, matrix = P(section, None), P(section, None, None)
    rows = P(section, expert, dp, None)
    dense = (vector, matrix, matrix, matrix, matrix, vector, matrix)
    return jax.shard_map(
        local,
        mesh=mesh,
        in_specs=(tokens, P(None, expert, None), tokens, tokens) + dense + (rows, rows, rows),
        out_specs=(tokens,) + dense + (rows, rows, rows),
        check_vma=False,
    )
```

```python
from types import SimpleNamespace

import jax
import jax.numpy as jnp
import numpy as np
from jax import lax
from jax.experimental import pallas as pl
from jax.experimental.pallas import tpu as pltpu
from jax.sharding import PartitionSpec as P

HEAD_SIZE = 128
SCALE = HEAD_SIZE ** (-0.5)
epsilon = 1e-06
masked_score = -1e30
BF = jnp.bfloat16
F32 = jnp.float32

SWAP = [(0, 1), (1, 0)]
UP = [(0, 1)]
DOWN = [(1, 0)]
OWNERS = ("expert", "dp", "section")
LINE = ("dp", "section")


def ancestry():
    parents = [-1]
    for branch_index in range(4):
        parents += [0, 1 + 3 * branch_index, 1 + 3 * branch_index]
    lineage = np.zeros((13, 13), np.float32)
    for segment in range(13):
        current = segment
        while current >= 0:
            lineage[current, segment] = 1.0
            current = parents[current]
    return lineage


def dot(left, right):
    return jnp.dot(left, right, preferred_element_type=F32)


def dot_t(left, right):
    return lax.dot_general(left, right, (((1,), (1,)), ((), ())), preferred_element_type=F32)


def t_dot(left, right):
    return lax.dot_general(left, right, (((0,), (0,)), ((), ())), preferred_element_type=F32)


def t_dot_t(left, right):
    return lax.dot_general(left, right, (((0,), (1,)), ((), ())), preferred_element_type=F32)


def normalize(values, gain_vec):
    factor = lax.rsqrt(jnp.mean(values * values, -1, keepdims=True) + epsilon)
    return (values * factor * gain_vec, factor)


def norm_back(values, factor, gain_vec, upstream):
    scaled = upstream * gain_vec
    grad_gain = jnp.sum(upstream * values * factor, 0)
    inner_mean = jnp.mean(scaled * values, -1, keepdims=True)
    return (scaled * factor - values * factor * factor * factor * inner_mean, grad_gain)


def tree_mask(lengths_row, local_len):
    own = lax.axis_index("dp")
    first_row = own * local_len
    seg_ends = jnp.cumsum(lengths_row)
    blocks = own ^ jnp.asarray(block_order(), jnp.int32)
    key_spots = (
        blocks[:, None] * local_len + jnp.arange(local_len, dtype=jnp.int32)[None, :]
    ).reshape(-1)
    query_spots = first_row + jnp.arange(local_len, dtype=jnp.int32)
    seg_ids = jnp.arange(13, dtype=jnp.int32)
    key_seg = jnp.sum((key_spots[:, None] >= seg_ends[None, :]).astype(jnp.int32), 1)
    query_seg = jnp.sum((query_spots[:, None] >= seg_ends[None, :]).astype(jnp.int32), 1)
    key_hot = (key_seg[:, None] == seg_ids[None, :]).astype(BF)
    query_hot = (query_seg[:, None] == seg_ids[None, :]).astype(BF)
    allowed = dot(query_hot, jnp.asarray(ancestry(), BF)).astype(BF)
    linked = dot_t(allowed, key_hot) > 0.5
    return linked & (key_spots[None, :] <= query_spots[:, None])


def tie(*values):
    return lax.optimization_barrier(values)


def swapped(shard):
    return lax.ppermute(shard, "section", SWAP)


def partners(axis, flip):
    return [(i, i ^ flip) for i in range(lax.axis_size(axis))]


def flips(axis):
    found = [1]
    while 2 * found[-1] < lax.axis_size(axis):
        found.append(2 * found[-1])
    return found


def block_order():
    order = [0]
    for flip in reversed(flips("dp")):
        order = order + [k ^ flip for k in order]
    return order


def gathered(shard, axis, over="dp"):
    for flip in reversed(flips(over)):
        shard = jnp.concatenate([shard, lax.ppermute(shard, over, partners(over, flip))], axis)
    return shard


def sum_to_owner(partial, axis):
    sent_as = partial.dtype
    for flip in flips("dp"):
        kept, sent = jnp.split(partial, 2, axis)
        sent = lax.ppermute(sent.astype(sent_as), "dp", partners("dp", flip))
        partial = kept.astype(F32) + sent.astype(F32)
    return partial


def pick_blocks(sources, blocks, pick, count, kernel, out_shapes, out_blocks):
    where = jnp.stack([lax.axis_index(axis) for axis in ("section", "dp")]).astype(jnp.int32)

    def spec(at):
        def index(k, where):
            return pick(k, where)[at]

        return pl.BlockSpec(blocks[at], index)

    def body(where, *refs):
        kernel(pl.program_id(0), where, refs[: len(sources)], refs[len(sources) :])

    return pl.pallas_call(
        body,
        grid_spec=pltpu.PrefetchScalarGridSpec(
            num_scalar_prefetch=1,
            grid=(count,),
            in_specs=[spec(at) for at in range(len(sources))],
            out_specs=[
                pl.BlockSpec(shape, lambda k, where: (k,) + (0,) * (len(shape) - 1))
                for shape in out_blocks
            ],
        ),
        out_shape=[jax.ShapeDtypeStruct(shape, F32) for shape in out_shapes],
        compiler_params=pltpu.CompilerParams(vmem_limit_bytes=48 * 1024 * 1024),
    )(where, *sources)


def two_homes(first, second):
    return (
        first,
        second,
        lax.ppermute(first, "section", DOWN),
        lax.ppermute(second, "section", UP),
    )


def source_of(section, core):
    return jnp.where(core == section, section, 2 + section)


def dense_home(homes, offsets, width, out_widths):
    parts, groups, rows, _ = homes[1].shape
    block = rows // 2

    def pick(k, where):
        used = source_of(where[0], k // (2 * parts))
        return [
            (jnp.where(used == source, k // 2 % parts, 0), 0, jnp.where(used == source, k % 2, 0), 0)
            for source in range(4)
        ]

    def kernel(k, where, sources, outs):
        used = source_of(where[0], k // (2 * parts))
        for source in range(4):

            @pl.when(used == source)
            def _():
                out, at = 0, 0
                for group in range(groups):
                    start = offsets[source]
                    stop = start + width
                    while start < stop:
                        piece = min(stop - start, out_widths[out] - at)
                        outs[out][:, at : at + piece] = sources[source][
                            0, group, :, start : start + piece
                        ].astype(F32)
                        start, at = start + piece, at + piece
                        if at == out_widths[out]:
                            out, at = out + 1, 0

    count = 4 * parts
    shapes = [(count * block, w) for w in out_widths]
    blocks = [(1, groups, block, home.shape[3]) for home in homes]
    return pick_blocks(
        homes, blocks, pick, count, kernel, shapes, [(block, w) for w in out_widths]
    )


def two_parts(array, index, axis=0):
    half = array.shape[axis] // 2
    return (
        lax.dynamic_slice_in_dim(array, index * half, half, axis),
        lax.dynamic_slice_in_dim(array, (1 - index) * half, half, axis),
    )


def in_order(mine, others, index, axis):
    first = index == 0
    return jnp.concatenate(
        [jnp.where(first, mine, others), jnp.where(first, others, mine)], axis
    )


def early_operand(rows):
    mine, others = two_parts(rows, lax.axis_index("section"), 1)
    half = mine.shape[1]
    joined = jnp.stack([mine.reshape(2, -1, half), swapped(others).reshape(2, -1, half)], 1)
    return gathered(joined[:, None], 1, "expert").reshape(2, -1, half)


def late_operands(operands):
    groups = lax.axis_size("expert")
    own = lax.axis_index("expert")
    blocks = []
    order = [0]
    for flip in reversed(flips("expert")):
        order = order + [k ^ flip for k in order]
    for flip in order:
        shares = []
        for rows in operands:
            share = rows.shape[1] // groups
            shares.append(lax.dynamic_slice_in_dim(rows, (own ^ flip) * share, share, 1))
        block = jnp.concatenate(shares, 1)
        if flip > 0:
            block = lax.ppermute(block, "expert", partners("expert", flip))
        blocks.append(block)
    joined = jnp.stack(blocks)
    joined = jnp.stack([joined, swapped(joined)], 1)
    joined = joined.reshape(-1, joined.shape[-1])
    return jnp.split(joined, np.cumsum([a.shape[1] // groups for a in operands])[:-1], 1)


def dense_partial(early, late):
    return jnp.concatenate([t_dot(e, p) for e, p in zip(early, late, strict=True)], 1)


def dense_rows(partial):
    for flip in flips("dp"):
        partial = dense_rows_step(partial, flip)
    return partial.astype(BF)


def dense_rows_step(partial, flip):
    own = lax.axis_index("dp")
    kept, sent = two_parts(partial, jnp.where((own & flip) == 0, 0, 1))
    sent = lax.ppermute(sent.astype(BF), "dp", partners("dp", flip))
    return kept.astype(F32) + sent.astype(F32)


def dense_line(total):
    own = lax.axis_index("dp")
    for flip in reversed(flips("dp")):
        others = lax.ppermute(total, "dp", partners("dp", flip))
        total = in_order(total, others, own & flip, 0)
    return total


def group_parts(total):
    axes = (1,) * len(flips("expert"))
    return [part.reshape(axes + part.shape) for part in jnp.split(total, 2, 0)]


def group_step(parts, index):
    own = lax.axis_index("expert")
    order = flips("expert")
    stepped = []
    for part, way in zip(parts, (order, order[::-1]), strict=True):
        flip = way[index]
        others = lax.ppermute(part, "expert", partners("expert", flip))
        axis = len(order) - 1 - order.index(flip)
        stepped.append(in_order(part, others, own & flip, axis))
    return stepped


def group_join(parts):
    return jnp.stack([part.reshape((-1,) + part.shape[-2:]) for part in parts])


def dense_groups(total):
    parts = group_parts(total)
    for index in range(len(flips("expert"))):
        parts = group_step(parts, index)
    return group_join(parts)


def small_sum(mine, others):
    total = mine + swapped(others.astype(BF)).astype(F32)
    for flip in flips("expert"):
        total = total + lax.ppermute(
            total.astype(BF), "expert", partners("expert", flip)
        ).astype(F32)
    return total


def with_small(partial, small):
    width = partial.shape[1]
    share = lax.dynamic_slice_in_dim(small, lax.axis_index("expert") * width, width, 1)
    share = jnp.pad(share, ((0, -small.shape[0] % 64), (0, 0)))
    halves = [jnp.split(a, 2, 0) for a in (partial, share)]
    return jnp.concatenate([a[k] for k in range(2) for a in halves], 0)


def small_of(total, rows):
    first = total.shape[2] - (rows + -rows % 64) // 2
    part = jnp.transpose(total[:, :, first:], (0, 2, 1, 3))
    return part.reshape(-1, part.shape[2] * part.shape[3])[:rows].astype(F32)


def exchange(rows, axes):
    return lax.all_to_all(rows, axes, split_axis=0, concat_axis=0, tiled=True)


def copies_of_expert(experts_all):
    owners = lax.axis_size("expert") * lax.axis_size("dp") * lax.axis_size("section")
    return owners // experts_all


def send_out(slot_rows, experts_all):
    width = slot_rows.shape[-1]
    copies = copies_of_expert(experts_all)
    rows = slot_rows.reshape(experts_all, -1, width)
    if copies > 1:
        mine = jnp.arange(copies) == lax.axis_index("dp") % copies
        rows = jnp.where(mine[None, :, None, None], rows[:, None], 0)
        rows = rows.reshape(experts_all * copies, -1, width)
    return exchange(rows, OWNERS).reshape(-1, width)


def send_back(rows, experts_all):
    width = rows.shape[-1]
    copies = copies_of_expert(experts_all)
    rows = exchange(rows.reshape(experts_all * copies, -1, width), OWNERS)
    if copies > 1:
        rows = rows.reshape(experts_all, copies, -1, width)
        rows = lax.dynamic_index_in_dim(rows, lax.axis_index("dp") % copies, 1, False)
    return rows.reshape(-1, width)


def row_halves(own, is_first):
    half = own.shape[1] // 2
    received = swapped(two_parts(own, lax.axis_index("section"), 1)[1])
    return (
        jnp.where(is_first, own[:, :half], received),
        jnp.where(is_first, received, own[:, half:]),
    )


def expert_in(rows):
    copies = lax.axis_size("dp") * lax.axis_size("section") // rows.shape[0]
    if copies > 1:
        rows = jnp.repeat(rows, copies, 0)
    return exchange(rows, LINE).reshape(-1, rows.shape[-1])


def expert_out(grad, experts):
    size = lax.axis_size("dp") * lax.axis_size("section")
    columns = grad.shape[1]
    pieces = exchange(grad.reshape(size, -1, columns), LINE)
    copies = size // experts
    if copies > 1:
        pieces = pieces.reshape(experts, copies, -1, columns).astype(F32)
        pieces = jnp.sum(pieces, 1).astype(BF)
    return pieces


def expert_home(homes, count=1):
    experts, rows, width = homes[0].shape
    columns = width // count

    def pick(k, where):
        section = where[0]
        used = [section, 2 + section]
        return [
            (jnp.where((used[0] == source) | (used[1] == source), k, 0), 0, 0)
            for source in range(4)
        ]

    def kernel(k, where, sources, outs):
        for core in range(2):
            used = source_of(where[0], core)
            for source in range(4):

                @pl.when(used == source)
                def _():
                    for part, out in enumerate(outs):
                        out[0, core * rows : (core + 1) * rows] = sources[source][
                            0, :, part * columns : (part + 1) * columns
                        ].astype(F32)

    shape = (experts, 2 * rows, columns)
    blocks = [(1, rows, width)] * 4
    return list(
        pick_blocks(homes, blocks, pick, experts, kernel, [shape] * count, [(1,) + shape[1:]] * count)
    )


def routing(route_rows, turn_row, experts_all, capacity):
    expert_ids = jnp.arange(experts_all, dtype=jnp.int32)
    chosen = jnp.any(route_rows[:, :, None] == expert_ids[None, None, :], 1)
    earlier = (turn_row[None, :] < turn_row[:, None]).astype(BF)
    places = dot(earlier, chosen.astype(BF))
    place_of = jnp.where(chosen & (places < capacity), places, -1.0).astype(BF)
    slot_ids = jnp.arange(experts_all * capacity, dtype=jnp.int32)
    spread = (slot_ids[None, :] // capacity == expert_ids[:, None]).astype(BF)
    selected = dot(place_of, spread) == (slot_ids % capacity).astype(F32)[None, :]
    return chosen, selected, spread


def attention_forward(layer_in, visible, routed, dense_set, hook):
    attn_gain, w_query, w_key, w_value, w_out, ffn_gain, w_router = dense_set
    local_len = layer_in.shape[0]
    heads_kv = w_key.shape[1] // HEAD_SIZE
    normed, factor_one = normalize(layer_in, attn_gain)
    hidden_one = normed.astype(BF)
    key_rows = dot(hidden_one, w_key).astype(BF)
    value_rows = dot(hidden_one, w_value).astype(BF)
    kv_all = hook(gathered(jnp.concatenate([key_rows, value_rows], 1), 0))
    queries = dot(hidden_one, w_query).astype(BF)
    key_width = w_key.shape[1]
    key_all = kv_all[:, :key_width].reshape(-1, heads_kv, HEAD_SIZE)
    value_all = kv_all[:, key_width:].reshape(-1, heads_kv, HEAD_SIZE)
    grouped_query = queries.reshape(local_len, heads_kv, -1, HEAD_SIZE)
    raw = jnp.einsum("tkgd,skd->kgts", grouped_query, key_all, preferred_element_type=F32) * SCALE
    scores = jnp.where(visible[None, None], raw, masked_score)
    log_total = jax.nn.logsumexp(scores, -1, keepdims=True)
    attn_prob = jnp.exp(scores - log_total)
    attn_mix = jnp.einsum(
        "kgts,skd->tkgd", attn_prob.astype(BF), value_all, preferred_element_type=F32
    )
    attn_mix = attn_mix.reshape(local_len, -1).astype(BF)
    middle = layer_in + dot(attn_mix, w_out)
    normed_two, factor_two = normalize(middle, ffn_gain)
    hidden_two = normed_two.astype(BF)
    chosen, selected, spread = routed
    logits = dot(hidden_two, w_router)
    masked_logits = jnp.where(chosen, logits, masked_score)
    top = jnp.max(masked_logits, -1, keepdims=True)
    powers = jnp.where(chosen, jnp.exp(masked_logits - top), 0.0)
    gate_share = powers / jnp.sum(powers, -1, keepdims=True)
    weighting = jnp.where(selected, dot(gate_share.astype(BF), spread), 0.0).astype(BF)
    return SimpleNamespace(
        layer_in=layer_in,
        factor_one=factor_one,
        hidden_one=hidden_one,
        queries=queries,
        key_all=key_all,
        value_all=value_all,
        attn_prob=attn_prob,
        attn_mix=attn_mix,
        middle=middle,
        factor_two=factor_two,
        hidden_two=hidden_two,
        gate_share=gate_share,
        selected=selected,
        selector=selected.astype(BF),
        spread=spread,
        weighting=weighting,
    )


def expert_forward(arrived, w_gate, w_up):
    gate_pre = dot(arrived, w_gate)
    up_pre = dot(arrived, w_up)
    return gate_pre, up_pre, (jax.nn.silu(gate_pre) * up_pre).astype(BF)


def expert_backward(owed, gate_pre, up_pre, w_down):
    grad_inner = dot_t(owed, w_down)
    sigmoid_a = jax.nn.sigmoid(gate_pre)
    grad_gate_pre = grad_inner * up_pre * sigmoid_a * (1.0 + gate_pre * (1.0 - sigmoid_a))
    return jnp.concatenate([grad_gate_pre, grad_inner * gate_pre * sigmoid_a], 1).astype(BF)


def expert_input(grad_pre, w_gate, w_up):
    width = w_gate.shape[1]
    return dot_t(grad_pre[:, :width], w_gate) + dot_t(grad_pre[:, width:], w_up)


def router_backward(stored, grad_top, returned, w_router):
    match = jnp.where(stored.selected, dot_t(grad_top, returned), 0.0)
    grad_weighting = lax.dot_general(
        match,
        stored.spread.astype(F32),
        (((1,), (1,)), ((), ())),
        precision=lax.Precision.HIGHEST,
        preferred_element_type=F32,
    )
    gate_share = stored.gate_share
    grad_logits = (
        gate_share * (grad_weighting - jnp.sum(gate_share * grad_weighting, -1, keepdims=True))
    ).astype(BF)
    return t_dot(grad_logits, stored.hidden_two), dot_t(grad_logits, w_router)


def attention_backward(stored, grad_top, grad_router, grad_hidden, dense_set, hook):
    attn_gain, w_query, w_key, w_value, w_out, ffn_gain, w_router = dense_set
    local_len = grad_top.shape[0]
    grad_normed_two, grad_ffn_gain = norm_back(
        stored.middle, stored.factor_two, ffn_gain, grad_hidden
    )
    grad_middle = grad_top.astype(F32) + grad_normed_two
    grad_branch = hook("branch", grad_middle.astype(BF))
    grad_mix = dot_t(grad_branch, w_out).astype(BF)
    key_all = stored.key_all
    value_all = stored.value_all
    heads_kv = key_all.shape[1]
    attn_prob = stored.attn_prob
    grouped_grad = grad_mix.reshape(local_len, heads_kv, -1, HEAD_SIZE)
    grad_prob = jnp.einsum("tkgd,skd->kgts", grouped_grad, value_all, preferred_element_type=F32)
    centre = jnp.sum(attn_prob * grad_prob, -1, keepdims=True)
    grad_scores = (attn_prob * (grad_prob - centre)).astype(BF)
    grouped_query = stored.queries.reshape(local_len, heads_kv, -1, HEAD_SIZE)
    grad_keys_all = (
        jnp.einsum("kgts,tkgd->skd", grad_scores, grouped_query, preferred_element_type=F32) * SCALE
    )
    grad_values_all = jnp.einsum(
        "kgts,tkgd->skd", attn_prob.astype(BF), grouped_grad, preferred_element_type=F32
    )
    tree_length = key_all.shape[0]
    grad_kv_all = jnp.concatenate(
        [grad_keys_all.reshape(tree_length, -1), grad_values_all.reshape(tree_length, -1)], 1
    ).astype(BF)
    grad_kv_all = hook("kv_all", grad_kv_all)
    grad_kv = hook("kv", sum_to_owner(grad_kv_all, 0).astype(BF))
    grad_queries = (
        jnp.einsum("kgts,skd->tkgd", grad_scores, key_all, preferred_element_type=F32) * SCALE
    )
    grad_queries = grad_queries.reshape(local_len, -1).astype(BF)
    key_width = w_key.shape[1]
    grad_keys, grad_values = grad_kv[:, :key_width], grad_kv[:, key_width:]
    grad_hidden_one = dot_t(grad_queries, w_query)
    grad_hidden_one = grad_hidden_one + dot_t(grad_keys, w_key)
    grad_hidden_one = grad_hidden_one + dot_t(grad_values, w_value)
    grad_normed_one, grad_attn_gain = norm_back(
        stored.layer_in, stored.factor_one, attn_gain, grad_hidden_one
    )
    grad_input = grad_middle + grad_normed_one
    small = jnp.concatenate([grad_router, grad_attn_gain[None], grad_ffn_gain[None]], 0)
    return SimpleNamespace(
        input=grad_input,
        branch=grad_branch,
        qkv=jnp.concatenate([grad_queries, grad_kv], 1),
        small=jnp.pad(small, ((0, -small.shape[0] % 16), (0, 0))),
    )


def local(
    edge_in,
    seg_lengths,
    routes,
    turns,
    attn_gain,
    w_query,
    w_key,
    w_value,
    w_out,
    ffn_gain,
    w_router,
    w_gate,
    w_up,
    w_down,
):
    edge_rows = edge_in[0, :, 0]
    local_len = edge_rows.shape[1]
    lengths_all = seg_lengths[:, 0]
    is_first = lax.axis_index("section") == 0

    def both_layers(own, received):
        return (jnp.where(is_first, own, received), jnp.where(is_first, received, own))

    def of_micro(pair):
        mine = jnp.where(is_first, pair[0], pair[1])
        others = jnp.where(is_first, pair[1], pair[0])
        return both_layers(mine, swapped(others))

    layer_rows, cotangent = of_micro(edge_rows)
    dense_own = (attn_gain[0], w_query[0], w_key[0], w_value[0], w_out[0], ffn_gain[0], w_router[0])
    dense_pairs = [both_layers(a, swapped(a)) for a in dense_own]
    dense_sets = [tuple(p[i] for p in dense_pairs) for i in range(2)]
    lengths_row = jnp.where(is_first, lengths_all[0], lengths_all[1])
    visible = tree_mask(lengths_row, local_len)
    experts_all, experts = w_router.shape[2], w_gate.shape[1]
    picks = routes.shape[4]
    capacity = local_len * picks // experts_all
    orders = of_micro(
        jnp.concatenate([jnp.swapaxes(routes[0, :, 0], 1, 2), turns[0, :, 0]], 1)
    )
    routed = [routing(o[:picks].T, o[picks], experts_all, capacity) for o in orders]
    gates, ups, downs = (row_halves(a[0], is_first) for a in (w_gate, w_up, w_down))

    gate_first, up_first = expert_in(gates[0]), expert_in(ups[0])
    first = attention_forward(
        layer_rows.astype(F32), visible, routed[0], dense_sets[0], lambda value: value
    )
    outgoing = t_dot(first.selector, first.hidden_two).astype(BF)
    arrived_first = send_out(outgoing, experts_all)
    down_first = expert_in(downs[0])
    gate_pre, up_pre, inner_first = expert_forward(arrived_first, gate_first, up_first)
    pres_first = (gate_pre, up_pre)
    returned_first = send_back(dot(inner_first, down_first).astype(BF), experts_all)
    early = jnp.concatenate([first.hidden_one, first.attn_mix], 0)
    early, returned_first = tie(early, returned_first)
    kept = SimpleNamespace(early=early_operand(early))

    def end(name, value):
        got, value = tie(getattr(kept, name), value)
        setattr(kept, name, got)
        return value

    state = (first.middle + dot(first.weighting, returned_first)).astype(BF)
    gate_second, up_second = expert_in(gates[1]), expert_in(ups[1])
    second = attention_forward(
        state.astype(F32), visible, routed[1], dense_sets[1], lambda value: end("early", value)
    )
    early_first = kept.early
    outgoing = jnp.concatenate(
        [t_dot(second.selector, second.hidden_two), t_dot(second.weighting, cotangent)], 1
    ).astype(BF)
    outgoing = send_out(outgoing, experts_all)
    early = jnp.concatenate([second.hidden_one, second.attn_mix], 0)
    early, outgoing = tie(early, outgoing)
    early_second = early_operand(early)
    arrived_second, owed_second = jnp.split(outgoing, 2, 1)
    down_second = expert_in(downs[1])
    gate_pre, up_pre, inner_second = expert_forward(arrived_second, gate_second, up_second)
    grad_pre = expert_backward(owed_second, gate_pre, up_pre, down_second)
    early_second, grad_pre = tie(early_second, grad_pre)
    produced = jnp.concatenate(
        [dot(inner_second, down_second), expert_input(grad_pre, gate_second, up_second)], 1
    ).astype(BF)
    produced = send_back(produced, experts_all)
    gate_up_grad = t_dot(arrived_second, grad_pre).astype(BF)
    down_grad = t_dot(inner_second, owed_second).astype(BF)
    produced, gate_up_grad, down_grad = tie(produced, gate_up_grad, down_grad)
    kept.down1 = expert_out(down_grad, experts)
    returned_second, sent_second = jnp.split(produced, 2, 1)
    top = second.middle + dot(second.weighting, returned_second)
    top_other = lax.ppermute(top, "section", UP)

    grad_router, grad_hidden = router_backward(
        second, cotangent, returned_second, dense_sets[1][6]
    )
    grad_hidden = grad_hidden + dot(second.selector, sent_second)
    later = attention_backward(
        second,
        cotangent,
        grad_router,
        grad_hidden,
        dense_sets[1],
        lambda name, value: end("down1", value) if name == "kv_all" else value,
    )
    grad = later.input.astype(BF)
    branch, qkv, grad = tie(later.branch, later.qkv, grad)
    late = late_operands([branch, qkv])
    width = late[0].shape[1]
    owed_first = send_out(t_dot(first.weighting, grad).astype(BF), experts_all)
    late, owed_first = tie(late, owed_first)
    hidden_early, mix_early = early_second
    kept.dense = dense_rows(dense_partial([mix_early, hidden_early], late))
    grad_pre = expert_backward(owed_first, *pres_first, down_first)
    grad_arrived = expert_input(grad_pre, gate_first, up_first).astype(BF)
    first_grads = [t_dot(arrived_first, grad_pre).astype(BF)]
    first_grads.append(t_dot(inner_first, owed_first).astype(BF))
    sent_first = send_back(end("dense", grad_arrived), experts_all)
    kept.dense, sent_first = tie(kept.dense, sent_first)
    kept.dense, gate_up_grad = tie(dense_line(kept.dense), gate_up_grad)
    kept.gate_up1 = expert_out(gate_up_grad, experts)
    grad_router, grad_hidden = router_backward(first, grad, returned_first, dense_sets[0][6])
    grad_hidden = grad_hidden + dot(first.selector, sent_first)

    def hook(name, value):
        if name == "branch":
            kept.late = late_operands([value])
        if name == "kv_all":
            value = end("late", value)
            kept.out = dense_partial([early_first[1]], kept.late)
            kept.dense = dense_groups(kept.dense)
            value = end("dense", end("out", end("gate_up1", value)))
        if name == "kv":
            down_grad, value, kept.out = tie(first_grads[1], value, kept.out)
            kept.down0 = expert_out(down_grad, experts)
        return value

    earlier = attention_backward(
        first, grad, grad_router, grad_hidden, dense_sets[0], hook
    )
    smalls = small_sum(
        jnp.where(is_first, earlier.small, later.small),
        jnp.where(is_first, later.small, earlier.small),
    )
    qkv_total = dense_partial([early_first[0]], late_operands([earlier.qkv]))
    qkv_total, smalls, down_part, out_total = tie(qkv_total, smalls, kept.down0, kept.out)
    small_rows = smalls.shape[0]
    out_total = with_small(out_total, smalls)
    for flip in flips("dp"):
        qkv_total = dense_rows_step(qkv_total, flip)
        out_total = dense_rows_step(out_total, flip)
        qkv_total, out_total = tie(qkv_total, out_total)
    qkv_total, out_total = dense_line(qkv_total.astype(BF)), dense_line(out_total.astype(BF))
    qkv_total, out_total, gate_up_grad = tie(qkv_total, out_total, first_grads[0])
    gate_up_part = expert_out(gate_up_grad, experts)
    second_total = kept.dense
    second_other = lax.ppermute(second_total, "section", UP)
    down_total = expert_home(two_homes(down_part, kept.down1))
    out_total = dense_groups(out_total)
    small = small_of(out_total, small_rows)
    out_other = lax.ppermute(out_total, "section", DOWN)
    homes = (out_total, second_total, out_other, second_other)
    out = dense_home(homes, [0] * 4, width, [w_out.shape[2]])[0]
    qkv_total = dense_groups(qkv_total)
    qkv_other = lax.ppermute(qkv_total, "section", DOWN)
    homes = (qkv_total, second_total, qkv_other, second_other)
    query, key, value = dense_home(
        homes,
        [0, width, 0, width],
        qkv_total.shape[3],
        [w_query.shape[2], w_key.shape[2], w_value.shape[2]],
    )
    grad = earlier.input
    grad_other = lax.ppermute(grad, "section", DOWN)
    edge_out = jnp.where(
        is_first, jnp.stack([grad, grad_other]), jnp.stack([top_other, top])
    )[None, :, None]
    gate_up_part, down_total, out, query, key, value, edge_out, small = tie(
        gate_up_part, down_total, out, query, key, value, edge_out, small
    )
    expert_total = expert_home(two_homes(gate_up_part, kept.gate_up1), 2) + down_total
    dense_out = (
        small[experts_all],
        query,
        key,
        value,
        out,
        small[experts_all + 1],
        small[:experts_all].T,
    )
    return (
        (edge_out,)
        + tuple((piece[None] for piece in dense_out))
        + tuple((piece[None] for piece in expert_total))
    )


def solution(mesh):
    section, expert, dp = "section", "expert", "dp"
    tokens = P(section, None, expert, dp, None)
    vector, matrix = P(section, None), P(section, None, None)
    rows = P(section, expert, dp, None)
    dense = (vector, matrix, matrix, matrix, matrix, vector, matrix)
    return jax.shard_map(
        local,
        mesh=mesh,
        in_specs=(tokens, P(None, expert, None), tokens, tokens) + dense + (rows, rows, rows),
        out_specs=(tokens,) + dense + (rows, rows, rows),
        check_vma=False,
    )
```

```python
from types import SimpleNamespace

import jax
import jax.numpy as jnp
import numpy as np
from jax import lax
from jax.experimental import pallas as pl
from jax.experimental.pallas import tpu as pltpu
from jax.sharding import PartitionSpec as P

HEAD_SIZE = 128
SCALE = HEAD_SIZE ** (-0.5)
epsilon = 1e-06
masked_score = -1e30
BF = jnp.bfloat16
F32 = jnp.float32

SWAP = [(0, 1), (1, 0)]
UP = [(0, 1)]
DOWN = [(1, 0)]
OWNERS = ("expert", "dp", "section")
LINE = ("dp", "section")


def ancestry():
    parents = [-1]
    for branch_index in range(4):
        parents += [0, 1 + 3 * branch_index, 1 + 3 * branch_index]
    lineage = np.zeros((13, 13), np.float32)
    for segment in range(13):
        current = segment
        while current >= 0:
            lineage[current, segment] = 1.0
            current = parents[current]
    return lineage


def dot(left, right):
    return jnp.dot(left, right, preferred_element_type=F32)


def dot_t(left, right):
    return lax.dot_general(left, right, (((1,), (1,)), ((), ())), preferred_element_type=F32)


def t_dot(left, right):
    return lax.dot_general(left, right, (((0,), (0,)), ((), ())), preferred_element_type=F32)


def t_dot_t(left, right):
    return lax.dot_general(left, right, (((0,), (1,)), ((), ())), preferred_element_type=F32)


def normalize(values, gain_vec):
    factor = lax.rsqrt(jnp.mean(values * values, -1, keepdims=True) + epsilon)
    return (values * factor * gain_vec, factor)


def norm_back(values, factor, gain_vec, upstream):
    scaled = upstream * gain_vec
    grad_gain = jnp.sum(upstream * values * factor, 0)
    inner_mean = jnp.mean(scaled * values, -1, keepdims=True)
    return (scaled * factor - values * factor * factor * factor * inner_mean, grad_gain)


def tree_mask(lengths_row, local_len):
    own = lax.axis_index("dp")
    first_row = own * local_len
    seg_ends = jnp.cumsum(lengths_row)
    blocks = own ^ jnp.asarray(block_order(), jnp.int32)
    key_spots = (
        blocks[:, None] * local_len + jnp.arange(local_len, dtype=jnp.int32)[None, :]
    ).reshape(-1)
    query_spots = first_row + jnp.arange(local_len, dtype=jnp.int32)
    seg_ids = jnp.arange(13, dtype=jnp.int32)
    key_seg = jnp.sum((key_spots[:, None] >= seg_ends[None, :]).astype(jnp.int32), 1)
    query_seg = jnp.sum((query_spots[:, None] >= seg_ends[None, :]).astype(jnp.int32), 1)
    key_hot = (key_seg[:, None] == seg_ids[None, :]).astype(BF)
    query_hot = (query_seg[:, None] == seg_ids[None, :]).astype(BF)
    allowed = dot(query_hot, jnp.asarray(ancestry(), BF)).astype(BF)
    linked = dot_t(allowed, key_hot) > 0.5
    return linked & (key_spots[None, :] <= query_spots[:, None])


def tie(*values):
    return lax.optimization_barrier(values)


def swapped(shard):
    return lax.ppermute(shard, "section", SWAP)


def partners(axis, flip):
    return [(i, i ^ flip) for i in range(lax.axis_size(axis))]


def flips(axis):
    found = [1]
    while 2 * found[-1] < lax.axis_size(axis):
        found.append(2 * found[-1])
    return found


def block_order():
    order = [0]
    for flip in reversed(flips("dp")):
        order = order + [k ^ flip for k in order]
    return order


def gathered(shard, axis, over="dp"):
    for flip in reversed(flips(over)):
        shard = jnp.concatenate([shard, lax.ppermute(shard, over, partners(over, flip))], axis)
    return shard


def sum_to_owner(partial, axis):
    sent_as = partial.dtype
    for flip in flips("dp"):
        kept, sent = jnp.split(partial, 2, axis)
        sent = lax.ppermute(sent.astype(sent_as), "dp", partners("dp", flip))
        partial = kept.astype(F32) + sent.astype(F32)
    return partial


def pick_blocks(sources, blocks, pick, count, kernel, out_shapes, out_blocks, place=None, into=()):
    where = jnp.stack([lax.axis_index(axis) for axis in ("section", "dp")]).astype(jnp.int32)

    def spec(at):
        def index(k, where):
            return pick(k, where)[at]

        return pl.BlockSpec(blocks[at], index)

    def body(where, *refs):
        kernel(pl.program_id(0), where, refs[: len(sources)], refs[len(sources) + len(into) :])

    return pl.pallas_call(
        body,
        grid_spec=pltpu.PrefetchScalarGridSpec(
            num_scalar_prefetch=1,
            grid=(count,),
            in_specs=[spec(at) for at in range(len(sources))]
            + [pl.BlockSpec(memory_space=pl.ANY)] * len(into),
            out_specs=[
                pl.BlockSpec(shape, place or (lambda k, where: (k,) + (0,) * (len(shape) - 1)))
                for shape in out_blocks
            ],
        ),
        out_shape=[jax.ShapeDtypeStruct(shape, F32) for shape in out_shapes],
        input_output_aliases={1 + len(sources) + at: at for at in range(len(into))},
        compiler_params=pltpu.CompilerParams(vmem_limit_bytes=48 * 1024 * 1024),
    )(where, *sources, *into)


def two_homes(first, second):
    return (
        first,
        second,
        lax.ppermute(first, "section", DOWN),
        lax.ppermute(second, "section", UP),
    )


def source_of(section, core):
    return jnp.where(core == section, section, 2 + section)


def dense_home(homes, offsets, width, out_widths):
    parts, groups, rows, _ = homes[1].shape
    block = rows // 2

    def pick(k, where):
        used = source_of(where[0], k // (2 * parts))
        return [
            (jnp.where(used == source, k // 2 % parts, 0), 0, jnp.where(used == source, k % 2, 0), 0)
            for source in range(4)
        ]

    def kernel(k, where, sources, outs):
        used = source_of(where[0], k // (2 * parts))
        for source in range(4):

            @pl.when(used == source)
            def _():
                out, at = 0, 0
                for group in range(groups):
                    start = offsets[source]
                    stop = start + width
                    while start < stop:
                        piece = min(stop - start, out_widths[out] - at)
                        outs[out][:, at : at + piece] = sources[source][
                            0, group, :, start : start + piece
                        ].astype(F32)
                        start, at = start + piece, at + piece
                        if at == out_widths[out]:
                            out, at = out + 1, 0

    count = 4 * parts
    shapes = [(count * block, w) for w in out_widths]
    blocks = [(1, groups, block, home.shape[3]) for home in homes]
    return pick_blocks(
        homes, blocks, pick, count, kernel, shapes, [(block, w) for w in out_widths]
    )


def two_parts(array, index, axis=0):
    half = array.shape[axis] // 2
    return (
        lax.dynamic_slice_in_dim(array, index * half, half, axis),
        lax.dynamic_slice_in_dim(array, (1 - index) * half, half, axis),
    )


def in_order(mine, others, index, axis):
    first = index == 0
    return jnp.concatenate(
        [jnp.where(first, mine, others), jnp.where(first, others, mine)], axis
    )


def early_operand(rows):
    mine, others = two_parts(rows, lax.axis_index("section"), 1)
    half = mine.shape[1]
    joined = jnp.stack([mine.reshape(2, -1, half), swapped(others).reshape(2, -1, half)], 1)
    return gathered(joined[:, None], 1, "expert").reshape(2, -1, half)


def late_operands(operands):
    groups = lax.axis_size("expert")
    own = lax.axis_index("expert")
    blocks = []
    order = [0]
    for flip in reversed(flips("expert")):
        order = order + [k ^ flip for k in order]
    for flip in order:
        shares = []
        for rows in operands:
            share = rows.shape[1] // groups
            shares.append(lax.dynamic_slice_in_dim(rows, (own ^ flip) * share, share, 1))
        block = jnp.concatenate(shares, 1)
        if flip > 0:
            block = lax.ppermute(block, "expert", partners("expert", flip))
        blocks.append(block)
    joined = jnp.stack(blocks)
    joined = jnp.stack([joined, swapped(joined)], 1)
    joined = joined.reshape(-1, joined.shape[-1])
    return jnp.split(joined, np.cumsum([a.shape[1] // groups for a in operands])[:-1], 1)


def dense_partial(early, late):
    return jnp.concatenate([t_dot(e, p) for e, p in zip(early, late, strict=True)], 1)


def dense_rows(partial):
    for flip in flips("dp"):
        partial = dense_rows_step(partial, flip)
    return partial.astype(BF)


def dense_rows_step(partial, flip):
    own = lax.axis_index("dp")
    kept, sent = two_parts(partial, jnp.where((own & flip) == 0, 0, 1))
    sent = lax.ppermute(sent.astype(BF), "dp", partners("dp", flip))
    return kept.astype(F32) + sent.astype(F32)


def dense_line(total):
    for flip in reversed(flips("dp")):
        total = dense_line_step(total, flip)
    return total


def dense_line_step(total, flip):
    others = lax.ppermute(total, "dp", partners("dp", flip))
    return in_order(total, others, lax.axis_index("dp") & flip, 0)


def group_parts(total):
    axes = (1,) * len(flips("expert"))
    return [part.reshape(axes + part.shape) for part in jnp.split(total, 2, 0)]


def group_step(parts, index):
    own = lax.axis_index("expert")
    order = flips("expert")
    stepped = []
    for part, way in zip(parts, (order, order[::-1]), strict=True):
        flip = way[index]
        others = lax.ppermute(part, "expert", partners("expert", flip))
        axis = len(order) - 1 - order.index(flip)
        stepped.append(in_order(part, others, own & flip, axis))
    return stepped


def group_join(parts):
    return jnp.stack([part.reshape((-1,) + part.shape[-2:]) for part in parts])


def dense_groups(total):
    parts = group_parts(total)
    for index in range(len(flips("expert"))):
        parts = group_step(parts, index)
    return group_join(parts)


def small_sum(mine, others):
    total = mine + swapped(others.astype(BF)).astype(F32)
    for flip in flips("expert"):
        total = total + lax.ppermute(
            total.astype(BF), "expert", partners("expert", flip)
        ).astype(F32)
    return total


def with_small(partial, small):
    width = small.shape[1] // lax.axis_size("expert")
    share = lax.dynamic_slice_in_dim(small, lax.axis_index("expert") * width, width, 1)
    share = jnp.pad(share, ((0, -small.shape[0] % 64), (0, partial.shape[1] - width)))
    halves = [jnp.split(a, 2, 0) for a in (partial, share)]
    return jnp.concatenate([a[k] for k in range(2) for a in halves], 0)


def small_of(total, rows, columns):
    first = total.shape[2] - (rows + -rows % 64) // 2
    part = jnp.transpose(total[:, :, first:, : columns // total.shape[1]], (0, 2, 1, 3))
    return part.reshape(-1, part.shape[2] * part.shape[3])[:rows].astype(F32)


def exchange(rows, axes):
    return lax.all_to_all(rows, axes, split_axis=0, concat_axis=0, tiled=True)


def copies_of_expert(experts_all):
    owners = lax.axis_size("expert") * lax.axis_size("dp") * lax.axis_size("section")
    return owners // experts_all


def send_out(slot_rows, experts_all):
    width = slot_rows.shape[-1]
    copies = copies_of_expert(experts_all)
    rows = slot_rows.reshape(experts_all, -1, width)
    if copies > 1:
        mine = jnp.arange(copies) == lax.axis_index("dp") % copies
        rows = jnp.where(mine[None, :, None, None], rows[:, None], 0)
        rows = rows.reshape(experts_all * copies, -1, width)
    return exchange(rows, OWNERS).reshape(-1, width)


def send_back(rows, experts_all):
    width = rows.shape[-1]
    copies = copies_of_expert(experts_all)
    rows = exchange(rows.reshape(experts_all * copies, -1, width), OWNERS)
    if copies > 1:
        rows = rows.reshape(experts_all, copies, -1, width)
        rows = lax.dynamic_index_in_dim(rows, lax.axis_index("dp") % copies, 1, False)
    return rows.reshape(-1, width)


def row_halves(own, is_first):
    half = own.shape[1] // 2
    received = swapped(two_parts(own, lax.axis_index("section"), 1)[1])
    return (
        jnp.where(is_first, own[:, :half], received),
        jnp.where(is_first, received, own[:, half:]),
    )


def expert_in(rows):
    copies = lax.axis_size("dp") * lax.axis_size("section") // rows.shape[0]
    if copies > 1:
        rows = jnp.repeat(rows, copies, 0)
    return exchange(rows, LINE).reshape(-1, rows.shape[-1])


def expert_out(grad, experts):
    size = lax.axis_size("dp") * lax.axis_size("section")
    columns = grad.shape[1]
    pieces = exchange(grad.reshape(size, -1, columns), LINE)
    copies = size // experts
    if copies > 1:
        pieces = pieces.reshape(experts, copies, -1, columns).astype(F32)
        pieces = jnp.sum(pieces, 1).astype(BF)
    return pieces


def expert_home(homes, count=1):
    experts, rows, width = homes[0].shape
    columns = width // count

    def pick(k, where):
        section = where[0]
        used = [section, 2 + section]
        return [
            (jnp.where((used[0] == source) | (used[1] == source), k, 0), 0, 0)
            for source in range(4)
        ]

    def kernel(k, where, sources, outs):
        for core in range(2):
            used = source_of(where[0], core)
            for source in range(4):

                @pl.when(used == source)
                def _():
                    for part, out in enumerate(outs):
                        out[0, core * rows : (core + 1) * rows] = sources[source][
                            0, :, part * columns : (part + 1) * columns
                        ].astype(F32)

    shape = (experts, 2 * rows, columns)
    blocks = [(1, rows, width)] * 4
    return list(
        pick_blocks(homes, blocks, pick, experts, kernel, [shape] * count, [(1,) + shape[1:]] * count)
    )


def expert_rows(arrays, count, others, into=()):
    experts, rows, width = arrays[0].shape
    columns = width // count

    def pick(k, where):
        return [(jnp.where(where[0] == layer, k, 0), 0, 0) for layer in range(2)]

    def place(k, where):
        return (k, 1 - where[0] if others else where[0], 0)

    def kernel(k, where, sources, outs):
        for layer in range(2):

            @pl.when(where[0] == layer)
            def _():
                for part, out in enumerate(outs):
                    out[0] = sources[layer][0, :, part * columns : (part + 1) * columns].astype(F32)

    shape = (experts, 2 * rows, columns)
    return pick_blocks(
        arrays,
        [(1, rows, width)] * 2,
        pick,
        experts,
        kernel,
        [shape] * count,
        [(1, rows, columns)] * count,
        place,
        into,
    )


def routing(route_rows, turn_row, experts_all, capacity):
    expert_ids = jnp.arange(experts_all, dtype=jnp.int32)
    chosen = jnp.any(route_rows[:, :, None] == expert_ids[None, None, :], 1)
    earlier = (turn_row[None, :] < turn_row[:, None]).astype(BF)
    places = dot(earlier, chosen.astype(BF))
    place_of = jnp.where(chosen & (places < capacity), places, -1.0).astype(BF)
    slot_ids = jnp.arange(experts_all * capacity, dtype=jnp.int32)
    spread = (slot_ids[None, :] // capacity == expert_ids[:, None]).astype(BF)
    selected = dot(place_of, spread) == (slot_ids % capacity).astype(F32)[None, :]
    return chosen, selected, spread


def attention_forward(layer_in, visible, routed, dense_set, hook):
    attn_gain, w_query, w_key, w_value, w_out, ffn_gain, w_router = dense_set
    local_len = layer_in.shape[0]
    heads_kv = w_key.shape[1] // HEAD_SIZE
    normed, factor_one = normalize(layer_in, attn_gain)
    hidden_one = normed.astype(BF)
    key_rows = dot(hidden_one, w_key).astype(BF)
    value_rows = dot(hidden_one, w_value).astype(BF)
    kv_all = hook(gathered(jnp.concatenate([key_rows, value_rows], 1), 0))
    queries = dot(hidden_one, w_query).astype(BF)
    key_width = w_key.shape[1]
    key_all = kv_all[:, :key_width].reshape(-1, heads_kv, HEAD_SIZE)
    value_all = kv_all[:, key_width:].reshape(-1, heads_kv, HEAD_SIZE)
    grouped_query = queries.reshape(local_len, heads_kv, -1, HEAD_SIZE)
    raw = jnp.einsum("tkgd,skd->kgts", grouped_query, key_all, preferred_element_type=F32) * SCALE
    scores = jnp.where(visible[None, None], raw, masked_score)
    log_total = jax.nn.logsumexp(scores, -1, keepdims=True)
    attn_prob = jnp.exp(scores - log_total)
    attn_mix = jnp.einsum(
        "kgts,skd->tkgd", attn_prob.astype(BF), value_all, preferred_element_type=F32
    )
    attn_mix = attn_mix.reshape(local_len, -1).astype(BF)
    middle = layer_in + dot(attn_mix, w_out)
    normed_two, factor_two = normalize(middle, ffn_gain)
    hidden_two = normed_two.astype(BF)
    chosen, selected, spread = routed
    logits = dot(hidden_two, w_router)
    masked_logits = jnp.where(chosen, logits, masked_score)
    top = jnp.max(masked_logits, -1, keepdims=True)
    powers = jnp.where(chosen, jnp.exp(masked_logits - top), 0.0)
    gate_share = powers / jnp.sum(powers, -1, keepdims=True)
    weighting = jnp.where(selected, dot(gate_share.astype(BF), spread), 0.0).astype(BF)
    return SimpleNamespace(
        layer_in=layer_in,
        factor_one=factor_one,
        hidden_one=hidden_one,
        queries=queries,
        key_all=key_all,
        value_all=value_all,
        attn_prob=attn_prob,
        attn_mix=attn_mix,
        middle=middle,
        factor_two=factor_two,
        hidden_two=hidden_two,
        gate_share=gate_share,
        selected=selected,
        selector=selected.astype(BF),
        spread=spread,
        weighting=weighting,
    )


def expert_forward(arrived, w_gate, w_up):
    gate_pre = dot(arrived, w_gate)
    up_pre = dot(arrived, w_up)
    return gate_pre, up_pre, (jax.nn.silu(gate_pre) * up_pre).astype(BF)


def expert_backward(owed, gate_pre, up_pre, w_down):
    grad_inner = dot_t(owed, w_down)
    sigmoid_a = jax.nn.sigmoid(gate_pre)
    grad_gate_pre = grad_inner * up_pre * sigmoid_a * (1.0 + gate_pre * (1.0 - sigmoid_a))
    return jnp.concatenate([grad_gate_pre, grad_inner * gate_pre * sigmoid_a], 1).astype(BF)


def expert_input(grad_pre, w_gate, w_up):
    width = w_gate.shape[1]
    return dot_t(grad_pre[:, :width], w_gate) + dot_t(grad_pre[:, width:], w_up)


def router_backward(stored, grad_top, returned, w_router):
    match = jnp.where(stored.selected, dot_t(grad_top, returned), 0.0)
    grad_weighting = lax.dot_general(
        match,
        stored.spread.astype(F32),
        (((1,), (1,)), ((), ())),
        precision=lax.Precision.HIGHEST,
        preferred_element_type=F32,
    )
    gate_share = stored.gate_share
    grad_logits = (
        gate_share * (grad_weighting - jnp.sum(gate_share * grad_weighting, -1, keepdims=True))
    ).astype(BF)
    return t_dot(grad_logits, stored.hidden_two), dot_t(grad_logits, w_router)


def attention_backward(stored, grad_top, grad_router, grad_hidden, dense_set, hook):
    attn_gain, w_query, w_key, w_value, w_out, ffn_gain, w_router = dense_set
    local_len = grad_top.shape[0]
    grad_normed_two, grad_ffn_gain = norm_back(
        stored.middle, stored.factor_two, ffn_gain, grad_hidden
    )
    grad_middle = grad_top.astype(F32) + grad_normed_two
    grad_branch = hook("branch", grad_middle.astype(BF))
    grad_mix = dot_t(grad_branch, w_out).astype(BF)
    key_all = stored.key_all
    value_all = stored.value_all
    heads_kv = key_all.shape[1]
    attn_prob = stored.attn_prob
    grouped_grad = grad_mix.reshape(local_len, heads_kv, -1, HEAD_SIZE)
    grad_prob = jnp.einsum("tkgd,skd->kgts", grouped_grad, value_all, preferred_element_type=F32)
    centre = jnp.sum(attn_prob * grad_prob, -1, keepdims=True)
    grad_scores = (attn_prob * (grad_prob - centre)).astype(BF)
    grouped_query = stored.queries.reshape(local_len, heads_kv, -1, HEAD_SIZE)
    grad_keys_all = (
        jnp.einsum("kgts,tkgd->skd", grad_scores, grouped_query, preferred_element_type=F32) * SCALE
    )
    grad_values_all = jnp.einsum(
        "kgts,tkgd->skd", attn_prob.astype(BF), grouped_grad, preferred_element_type=F32
    )
    tree_length = key_all.shape[0]
    grad_kv_all = jnp.concatenate(
        [grad_keys_all.reshape(tree_length, -1), grad_values_all.reshape(tree_length, -1)], 1
    ).astype(BF)
    grad_kv_all = hook("kv_all", grad_kv_all)
    grad_kv = hook("kv", sum_to_owner(grad_kv_all, 0).astype(BF))
    grad_queries = (
        jnp.einsum("kgts,skd->tkgd", grad_scores, key_all, preferred_element_type=F32) * SCALE
    )
    grad_queries = grad_queries.reshape(local_len, -1).astype(BF)
    key_width = w_key.shape[1]
    grad_keys, grad_values = grad_kv[:, :key_width], grad_kv[:, key_width:]
    grad_hidden_one = dot_t(grad_queries, w_query)
    grad_hidden_one = grad_hidden_one + dot_t(grad_keys, w_key)
    grad_hidden_one = grad_hidden_one + dot_t(grad_values, w_value)
    grad_normed_one, grad_attn_gain = norm_back(
        stored.layer_in, stored.factor_one, attn_gain, grad_hidden_one
    )
    grad_input = grad_middle + grad_normed_one
    small = jnp.concatenate([grad_router, grad_attn_gain[None], grad_ffn_gain[None]], 0)
    return SimpleNamespace(
        input=grad_input,
        branch=grad_branch,
        qkv=jnp.concatenate([grad_queries, grad_kv], 1),
        small=jnp.pad(small, ((0, -small.shape[0] % 16), (0, 0))),
    )


def local(
    edge_in,
    seg_lengths,
    routes,
    turns,
    attn_gain,
    w_query,
    w_key,
    w_value,
    w_out,
    ffn_gain,
    w_router,
    w_gate,
    w_up,
    w_down,
):
    edge_rows = edge_in[0, :, 0]
    local_len = edge_rows.shape[1]
    lengths_all = seg_lengths[:, 0]
    is_first = lax.axis_index("section") == 0

    def both_layers(own, received):
        return (jnp.where(is_first, own, received), jnp.where(is_first, received, own))

    def of_micro(pair):
        mine = jnp.where(is_first, pair[0], pair[1])
        others = jnp.where(is_first, pair[1], pair[0])
        return both_layers(mine, swapped(others))

    layer_rows, cotangent = of_micro(edge_rows)
    dense_own = (attn_gain[0], w_query[0], w_key[0], w_value[0], w_out[0], ffn_gain[0], w_router[0])
    dense_pairs = [both_layers(a, swapped(a)) for a in dense_own]
    dense_sets = [tuple(p[i] for p in dense_pairs) for i in range(2)]
    lengths_row = jnp.where(is_first, lengths_all[0], lengths_all[1])
    visible = tree_mask(lengths_row, local_len)
    experts_all, experts = w_router.shape[2], w_gate.shape[1]
    picks = routes.shape[4]
    capacity = local_len * picks // experts_all
    orders = of_micro(
        jnp.concatenate([jnp.swapaxes(routes[0, :, 0], 1, 2), turns[0, :, 0]], 1)
    )
    routed = [routing(o[:picks].T, o[picks], experts_all, capacity) for o in orders]
    gates, ups, downs = (row_halves(a[0], is_first) for a in (w_gate, w_up, w_down))

    gate_first, up_first = expert_in(gates[0]), expert_in(ups[0])
    first = attention_forward(
        layer_rows.astype(F32), visible, routed[0], dense_sets[0], lambda value: value
    )
    outgoing = t_dot(first.selector, first.hidden_two).astype(BF)
    arrived_first = send_out(outgoing, experts_all)
    down_first = expert_in(downs[0])
    gate_pre, up_pre, inner_first = expert_forward(arrived_first, gate_first, up_first)
    pres_first = (gate_pre, up_pre)
    returned_first = send_back(dot(inner_first, down_first).astype(BF), experts_all)
    early = jnp.concatenate([first.hidden_one, first.attn_mix], 0)
    early, returned_first = tie(early, returned_first)
    kept = SimpleNamespace(early=early_operand(early))

    def end(name, value):
        got, value = tie(getattr(kept, name), value)
        setattr(kept, name, got)
        return value

    state = (first.middle + dot(first.weighting, returned_first)).astype(BF)
    gate_second, up_second = expert_in(gates[1]), expert_in(ups[1])
    second = attention_forward(
        state.astype(F32), visible, routed[1], dense_sets[1], lambda value: end("early", value)
    )
    early_first = kept.early
    outgoing = jnp.concatenate(
        [t_dot(second.selector, second.hidden_two), t_dot(second.weighting, cotangent)], 1
    ).astype(BF)
    outgoing = send_out(outgoing, experts_all)
    early = jnp.concatenate([second.hidden_one, second.attn_mix], 0)
    early, outgoing = tie(early, outgoing)
    early_second = early_operand(early)
    arrived_second, owed_second = jnp.split(outgoing, 2, 1)
    down_second = expert_in(downs[1])
    gate_pre, up_pre, inner_second = expert_forward(arrived_second, gate_second, up_second)
    grad_pre = expert_backward(owed_second, gate_pre, up_pre, down_second)
    early_second, grad_pre = tie(early_second, grad_pre)
    produced = jnp.concatenate(
        [dot(inner_second, down_second), expert_input(grad_pre, gate_second, up_second)], 1
    ).astype(BF)
    produced = send_back(produced, experts_all)
    gate_up_grad = t_dot(arrived_second, grad_pre).astype(BF)
    down_grad = t_dot(inner_second, owed_second).astype(BF)
    produced, gate_up_grad, down_grad = tie(produced, gate_up_grad, down_grad)
    kept.down1 = expert_out(down_grad, experts)
    returned_second, sent_second = jnp.split(produced, 2, 1)
    top = second.middle + dot(second.weighting, returned_second)
    top_other = lax.ppermute(top, "section", UP)

    grad_router, grad_hidden = router_backward(
        second, cotangent, returned_second, dense_sets[1][6]
    )
    grad_hidden = grad_hidden + dot(second.selector, sent_second)
    later = attention_backward(
        second,
        cotangent,
        grad_router,
        grad_hidden,
        dense_sets[1],
        lambda name, value: end("down1", value) if name == "kv_all" else value,
    )
    grad = later.input.astype(BF)
    branch, qkv, grad = tie(later.branch, later.qkv, grad)
    late = late_operands([branch, qkv])
    width = late[0].shape[1]
    owed_first = send_out(t_dot(first.weighting, grad).astype(BF), experts_all)
    late, owed_first = tie(late, owed_first)
    hidden_early, mix_early = early_second
    kept.dense = dense_rows(dense_partial([mix_early, hidden_early], late))
    grad_pre = expert_backward(owed_first, *pres_first, down_first)
    grad_arrived = expert_input(grad_pre, gate_first, up_first).astype(BF)
    first_grads = [t_dot(arrived_first, grad_pre).astype(BF)]
    first_grads.append(t_dot(inner_first, owed_first).astype(BF))
    sent_first = send_back(end("dense", grad_arrived), experts_all)
    kept.dense, sent_first = tie(kept.dense, sent_first)
    kept.dense, gate_up_grad = tie(dense_line(kept.dense), gate_up_grad)
    kept.gate_up1 = expert_out(gate_up_grad, experts)
    grad_router, grad_hidden = router_backward(first, grad, returned_first, dense_sets[0][6])
    grad_hidden = grad_hidden + dot(first.selector, sent_first)

    def hook(name, value):
        if name == "branch":
            kept.late = late_operands([value])
        if name == "kv_all":
            value = end("late", value)
            kept.out = dense_partial([early_first[1]], kept.late)
            kept.dense = dense_groups(kept.dense)
            value = end("dense", end("out", end("gate_up1", value)))
        if name == "kv":
            kept.out = dense_rows_step(kept.out, flips("dp")[0])
            down_grad, value, kept.out = tie(first_grads[1], value, kept.out)
            kept.down0 = expert_out(down_grad, experts)
        return value

    earlier = attention_backward(
        first, grad, grad_router, grad_hidden, dense_sets[0], hook
    )
    smalls = small_sum(
        jnp.where(is_first, earlier.small, later.small),
        jnp.where(is_first, later.small, earlier.small),
    )
    qkv_total = dense_partial([early_first[0]], late_operands([earlier.qkv]))
    qkv_total, smalls, down_part, out_total = tie(qkv_total, smalls, kept.down0, kept.out)
    small_rows, small_columns = smalls.shape
    qkv_total = with_small(qkv_total, smalls)
    steps = [(dense_rows_step, flip) for flip in flips("dp")]
    steps += [(dense_line_step, flip) for flip in reversed(flips("dp"))]
    turning = len(flips("dp"))
    for index in range(len(steps)):
        if index + 1 < len(steps):
            step, flip = steps[index + 1]
            out_total = out_total.astype(BF) if index + 1 >= turning else out_total
            out_total = step(out_total, flip)
        step, flip = steps[index]
        qkv_total = step(qkv_total.astype(BF) if index >= turning else qkv_total, flip)
        qkv_total, out_total = tie(qkv_total, out_total)
    qkv_total, out_total, gate_up_grad = tie(qkv_total, out_total, first_grads[0])
    gate_up_part = expert_out(gate_up_grad, experts)
    second_total = kept.dense
    second_other = lax.ppermute(second_total, "section", UP)
    down_total = expert_home(two_homes(down_part, kept.down1))
    out_total = dense_groups(out_total)
    out_other = lax.ppermute(out_total, "section", DOWN)
    homes = (out_total, second_total, out_other, second_other)
    out = dense_home(homes, [0] * 4, width, [w_out.shape[2]])[0]
    qkv_total = dense_groups(qkv_total)
    small = small_of(qkv_total, small_rows, small_columns)
    qkv_other = lax.ppermute(qkv_total, "section", DOWN)
    homes = (qkv_total, second_total, qkv_other, second_other)
    query, key, value = dense_home(
        homes,
        [0, width, 0, width],
        qkv_total.shape[3],
        [w_query.shape[2], w_key.shape[2], w_value.shape[2]],
    )
    grad = earlier.input
    grad_other = lax.ppermute(grad, "section", DOWN)
    edge_out = jnp.where(
        is_first, jnp.stack([grad, grad_other]), jnp.stack([top_other, top])
    )[None, :, None]
    gate_up_part, down_total, out, query, key, value, edge_out, small = tie(
        gate_up_part, down_total, out, query, key, value, edge_out, small
    )
    pair = (gate_up_part, kept.gate_up1)
    received = two_homes(*pair)[2:]
    expert_total = list(expert_rows(received, 2, True, expert_rows(pair, 2, False))) + down_total
    dense_out = (
        small[experts_all],
        query,
        key,
        value,
        out,
        small[experts_all + 1],
        small[:experts_all].T,
    )
    return (
        (edge_out,)
        + tuple((piece[None] for piece in dense_out))
        + tuple((piece[None] for piece in expert_total))
    )


def solution(mesh):
    section, expert, dp = "section", "expert", "dp"
    tokens = P(section, None, expert, dp, None)
    vector, matrix = P(section, None), P(section, None, None)
    rows = P(section, expert, dp, None)
    dense = (vector, matrix, matrix, matrix, matrix, vector, matrix)
    return jax.shard_map(
        local,
        mesh=mesh,
        in_specs=(tokens, P(None, expert, None), tokens, tokens) + dense + (rows, rows, rows),
        out_specs=(tokens,) + dense + (rows, rows, rows),
        check_vma=False,
    )
```

```python
from types import SimpleNamespace

import jax
import jax.numpy as jnp
import numpy as np
from jax import lax
from jax.experimental import pallas as pl
from jax.experimental.pallas import tpu as pltpu
from jax.sharding import PartitionSpec as P

HEAD_SIZE = 128
SCALE = HEAD_SIZE ** (-0.5)
epsilon = 1e-06
masked_score = -1e30
BF = jnp.bfloat16
F32 = jnp.float32

SWAP = [(0, 1), (1, 0)]
UP = [(0, 1)]
DOWN = [(1, 0)]
OWNERS = ("expert", "dp", "section")
LINE = ("dp", "section")


def ancestry():
    parents = [-1]
    for branch_index in range(4):
        parents += [0, 1 + 3 * branch_index, 1 + 3 * branch_index]
    lineage = np.zeros((13, 13), np.float32)
    for segment in range(13):
        current = segment
        while current >= 0:
            lineage[current, segment] = 1.0
            current = parents[current]
    return lineage


def dot(left, right):
    return jnp.dot(left, right, preferred_element_type=F32)


def dot_t(left, right):
    return lax.dot_general(left, right, (((1,), (1,)), ((), ())), preferred_element_type=F32)


def t_dot(left, right):
    return lax.dot_general(left, right, (((0,), (0,)), ((), ())), preferred_element_type=F32)


def t_dot_t(left, right):
    return lax.dot_general(left, right, (((0,), (1,)), ((), ())), preferred_element_type=F32)


def normalize(values, gain_vec):
    factor = lax.rsqrt(jnp.mean(values * values, -1, keepdims=True) + epsilon)
    return (values * factor * gain_vec, factor)


def norm_back(values, factor, gain_vec, upstream):
    scaled = upstream * gain_vec
    grad_gain = jnp.sum(upstream * values * factor, 0)
    inner_mean = jnp.mean(scaled * values, -1, keepdims=True)
    return (scaled * factor - values * factor * factor * factor * inner_mean, grad_gain)


def tree_mask(lengths_row, local_len):
    own = lax.axis_index("dp")
    first_row = own * local_len
    seg_ends = jnp.cumsum(lengths_row)
    blocks = own ^ jnp.asarray(block_order(), jnp.int32)
    key_spots = (
        blocks[:, None] * local_len + jnp.arange(local_len, dtype=jnp.int32)[None, :]
    ).reshape(-1)
    query_spots = first_row + jnp.arange(local_len, dtype=jnp.int32)
    seg_ids = jnp.arange(13, dtype=jnp.int32)
    key_seg = jnp.sum((key_spots[:, None] >= seg_ends[None, :]).astype(jnp.int32), 1)
    query_seg = jnp.sum((query_spots[:, None] >= seg_ends[None, :]).astype(jnp.int32), 1)
    key_hot = (key_seg[:, None] == seg_ids[None, :]).astype(BF)
    query_hot = (query_seg[:, None] == seg_ids[None, :]).astype(BF)
    allowed = dot(query_hot, jnp.asarray(ancestry(), BF)).astype(BF)
    linked = dot_t(allowed, key_hot) > 0.5
    return linked & (key_spots[None, :] <= query_spots[:, None])


def tie(*values):
    return lax.optimization_barrier(values)


def swapped(shard):
    return lax.ppermute(shard, "section", SWAP)


def partners(axis, flip):
    return [(i, i ^ flip) for i in range(lax.axis_size(axis))]


def flips(axis):
    found = [1]
    while 2 * found[-1] < lax.axis_size(axis):
        found.append(2 * found[-1])
    return found


def block_order():
    order = [0]
    for flip in reversed(flips("dp")):
        order = order + [k ^ flip for k in order]
    return order


def gathered(shard, axis, over="dp"):
    for flip in reversed(flips(over)):
        shard = jnp.concatenate([shard, lax.ppermute(shard, over, partners(over, flip))], axis)
    return shard


def sum_to_owner(partial, axis):
    sent_as = partial.dtype
    for flip in flips("dp"):
        kept, sent = jnp.split(partial, 2, axis)
        sent = lax.ppermute(sent.astype(sent_as), "dp", partners("dp", flip))
        partial = kept.astype(F32) + sent.astype(F32)
    return partial


def pick_blocks(sources, blocks, pick, count, kernel, out_shapes, out_blocks, place=None, into=()):
    where = jnp.stack([lax.axis_index(axis) for axis in ("section", "dp")]).astype(jnp.int32)

    def spec(at):
        def index(k, where):
            return pick(k, where)[at]

        return pl.BlockSpec(blocks[at], index)

    def body(where, *refs):
        kernel(pl.program_id(0), where, refs[: len(sources)], refs[len(sources) + len(into) :])

    return pl.pallas_call(
        body,
        grid_spec=pltpu.PrefetchScalarGridSpec(
            num_scalar_prefetch=1,
            grid=(count,),
            in_specs=[spec(at) for at in range(len(sources))]
            + [pl.BlockSpec(memory_space=pl.ANY)] * len(into),
            out_specs=[
                pl.BlockSpec(shape, place or (lambda k, where: (k,) + (0,) * (len(shape) - 1)))
                for shape in out_blocks
            ],
        ),
        out_shape=[jax.ShapeDtypeStruct(shape, F32) for shape in out_shapes],
        input_output_aliases={1 + len(sources) + at: at for at in range(len(into))},
        compiler_params=pltpu.CompilerParams(vmem_limit_bytes=48 * 1024 * 1024),
    )(where, *sources, *into)


def two_homes(first, second):
    return (
        first,
        second,
        lax.ppermute(first, "section", DOWN),
        lax.ppermute(second, "section", UP),
    )


def source_of(section, core):
    return jnp.where(core == section, section, 2 + section)


def dense_home(homes, offsets, width, out_widths):
    parts, groups, rows, _ = homes[1].shape
    block = rows // 2

    def pick(k, where):
        used = source_of(where[0], k // (2 * parts))
        return [
            (jnp.where(used == source, k // 2 % parts, 0), 0, jnp.where(used == source, k % 2, 0), 0)
            for source in range(4)
        ]

    def kernel(k, where, sources, outs):
        used = source_of(where[0], k // (2 * parts))
        for source in range(4):

            @pl.when(used == source)
            def _():
                out, at = 0, 0
                for group in range(groups):
                    start = offsets[source]
                    stop = start + width
                    while start < stop:
                        piece = min(stop - start, out_widths[out] - at)
                        outs[out][:, at : at + piece] = sources[source][
                            0, group, :, start : start + piece
                        ].astype(F32)
                        start, at = start + piece, at + piece
                        if at == out_widths[out]:
                            out, at = out + 1, 0

    count = 4 * parts
    shapes = [(count * block, w) for w in out_widths]
    blocks = [(1, groups, block, home.shape[3]) for home in homes]
    return pick_blocks(
        homes, blocks, pick, count, kernel, shapes, [(block, w) for w in out_widths]
    )


def two_parts(array, index, axis=0):
    half = array.shape[axis] // 2
    return (
        lax.dynamic_slice_in_dim(array, index * half, half, axis),
        lax.dynamic_slice_in_dim(array, (1 - index) * half, half, axis),
    )


def in_order(mine, others, index, axis):
    first = index == 0
    return jnp.concatenate(
        [jnp.where(first, mine, others), jnp.where(first, others, mine)], axis
    )


def early_operand(rows):
    mine, others = two_parts(rows, lax.axis_index("section"), 1)
    half = mine.shape[1]
    joined = jnp.stack([mine.reshape(2, -1, half), swapped(others).reshape(2, -1, half)], 1)
    joined = joined[:, None]
    for flip in reversed(flips("expert")):
        others = lax.ppermute(joined, "expert", partners("expert", flip))
        if flip == 1:
            return joined, others
        joined = jnp.concatenate([joined, others], 1)


def early_join(pair):
    joined = jnp.concatenate(pair, 1)
    return joined.reshape(2, -1, joined.shape[-1])


def late_operands(operands):
    groups = lax.axis_size("expert")
    own = lax.axis_index("expert")
    blocks = []
    order = [0]
    for flip in reversed(flips("expert")):
        order = order + [k ^ flip for k in order]
    for flip in order:
        shares = []
        for rows in operands:
            share = rows.shape[1] // groups
            shares.append(lax.dynamic_slice_in_dim(rows, (own ^ flip) * share, share, 1))
        block = jnp.concatenate(shares, 1)
        if flip > 0:
            block = lax.ppermute(block, "expert", partners("expert", flip))
        blocks.append(block)
    joined = jnp.stack(blocks)
    joined = jnp.stack([joined, swapped(joined)], 1)
    joined = joined.reshape(-1, joined.shape[-1])
    return jnp.split(joined, np.cumsum([a.shape[1] // groups for a in operands])[:-1], 1)


def dense_partial(early, late):
    return jnp.concatenate([t_dot(e, p) for e, p in zip(early, late, strict=True)], 1)


def dense_rows(partial):
    for flip in flips("dp"):
        partial = dense_rows_step(partial, flip)
    return partial.astype(BF)


def dense_rows_step(partial, flip):
    own = lax.axis_index("dp")
    kept, sent = two_parts(partial, jnp.where((own & flip) == 0, 0, 1))
    sent = lax.ppermute(sent.astype(BF), "dp", partners("dp", flip))
    return kept.astype(F32) + sent.astype(F32)


def dense_line(total):
    for flip in reversed(flips("dp")):
        total = dense_line_step(total, flip)
    return total


def dense_line_step(total, flip):
    others = lax.ppermute(total, "dp", partners("dp", flip))
    return in_order(total, others, lax.axis_index("dp") & flip, 0)


def group_parts(total):
    axes = (1,) * len(flips("expert"))
    return [part.reshape(axes + part.shape) for part in jnp.split(total, 2, 0)]


def group_step(parts, index):
    own = lax.axis_index("expert")
    order = flips("expert")
    stepped = []
    for part, way in zip(parts, (order, order[::-1]), strict=True):
        flip = way[index]
        others = lax.ppermute(part, "expert", partners("expert", flip))
        axis = len(order) - 1 - order.index(flip)
        stepped.append(in_order(part, others, own & flip, axis))
    return stepped


def group_join(parts):
    return jnp.stack([part.reshape((-1,) + part.shape[-2:]) for part in parts])


def dense_groups(total):
    parts = group_parts(total)
    for index in range(len(flips("expert"))):
        parts = group_step(parts, index)
    return group_join(parts)


def small_sum(mine, others):
    total = mine + swapped(others.astype(BF)).astype(F32)
    for flip in flips("expert"):
        total = total + lax.ppermute(
            total.astype(BF), "expert", partners("expert", flip)
        ).astype(F32)
    return total


def with_small(partial, small):
    width = small.shape[1] // lax.axis_size("expert")
    share = lax.dynamic_slice_in_dim(small, lax.axis_index("expert") * width, width, 1)
    share = jnp.pad(share, ((0, -small.shape[0] % 64), (0, partial.shape[1] - width)))
    halves = [jnp.split(a, 2, 0) for a in (partial, share)]
    return jnp.concatenate([a[k] for k in range(2) for a in halves], 0)


def small_of(total, rows, columns):
    first = total.shape[2] - (rows + -rows % 64) // 2
    part = jnp.transpose(total[:, :, first:, : columns // total.shape[1]], (0, 2, 1, 3))
    return part.reshape(-1, part.shape[2] * part.shape[3])[:rows].astype(F32)


def exchange(rows, axes):
    return lax.all_to_all(rows, axes, split_axis=0, concat_axis=0, tiled=True)


def copies_of_expert(experts_all):
    owners = lax.axis_size("expert") * lax.axis_size("dp") * lax.axis_size("section")
    return owners // experts_all


def send_out(slot_rows, experts_all):
    width = slot_rows.shape[-1]
    copies = copies_of_expert(experts_all)
    rows = slot_rows.reshape(experts_all, -1, width)
    if copies > 1:
        mine = jnp.arange(copies) == lax.axis_index("dp") % copies
        rows = jnp.where(mine[None, :, None, None], rows[:, None], 0)
        rows = rows.reshape(experts_all * copies, -1, width)
    return exchange(rows, OWNERS).reshape(-1, width)


def send_back(rows, experts_all):
    width = rows.shape[-1]
    copies = copies_of_expert(experts_all)
    rows = exchange(rows.reshape(experts_all * copies, -1, width), OWNERS)
    if copies > 1:
        rows = rows.reshape(experts_all, copies, -1, width)
        rows = lax.dynamic_index_in_dim(rows, lax.axis_index("dp") % copies, 1, False)
    return rows.reshape(-1, width)


def row_halves(own, is_first):
    half = own.shape[1] // 2
    received = swapped(two_parts(own, lax.axis_index("section"), 1)[1])
    return (
        jnp.where(is_first, own[:, :half], received),
        jnp.where(is_first, received, own[:, half:]),
    )


def expert_in(rows):
    copies = lax.axis_size("dp") * lax.axis_size("section") // rows.shape[0]
    if copies > 1:
        rows = jnp.repeat(rows, copies, 0)
    return exchange(rows, LINE).reshape(-1, rows.shape[-1])


def expert_out(grad, experts):
    size = lax.axis_size("dp") * lax.axis_size("section")
    columns = grad.shape[1]
    pieces = exchange(grad.reshape(size, -1, columns), LINE)
    copies = size // experts
    if copies > 1:
        pieces = pieces.reshape(experts, copies, -1, columns).astype(F32)
        pieces = jnp.sum(pieces, 1).astype(BF)
    return pieces


def expert_home(homes, count=1):
    experts, rows, width = homes[0].shape
    columns = width // count

    def pick(k, where):
        section = where[0]
        used = [section, 2 + section]
        return [
            (jnp.where((used[0] == source) | (used[1] == source), k, 0), 0, 0)
            for source in range(4)
        ]

    def kernel(k, where, sources, outs):
        for core in range(2):
            used = source_of(where[0], core)
            for source in range(4):

                @pl.when(used == source)
                def _():
                    for part, out in enumerate(outs):
                        out[0, core * rows : (core + 1) * rows] = sources[source][
                            0, :, part * columns : (part + 1) * columns
                        ].astype(F32)

    shape = (experts, 2 * rows, columns)
    blocks = [(1, rows, width)] * 4
    return list(
        pick_blocks(homes, blocks, pick, experts, kernel, [shape] * count, [(1,) + shape[1:]] * count)
    )


def expert_rows(arrays, count, others, into=()):
    experts, rows, width = arrays[0].shape
    columns = width // count

    def pick(k, where):
        return [(jnp.where(where[0] == layer, k, 0), 0, 0) for layer in range(2)]

    def place(k, where):
        return (k, 1 - where[0] if others else where[0], 0)

    def kernel(k, where, sources, outs):
        for layer in range(2):

            @pl.when(where[0] == layer)
            def _():
                for part, out in enumerate(outs):
                    out[0] = sources[layer][0, :, part * columns : (part + 1) * columns].astype(F32)

    shape = (experts, 2 * rows, columns)
    return pick_blocks(
        arrays,
        [(1, rows, width)] * 2,
        pick,
        experts,
        kernel,
        [shape] * count,
        [(1, rows, columns)] * count,
        place,
        into,
    )


def routing(route_rows, turn_row, experts_all, capacity):
    expert_ids = jnp.arange(experts_all, dtype=jnp.int32)
    chosen = jnp.any(route_rows[:, :, None] == expert_ids[None, None, :], 1)
    earlier = (turn_row[None, :] < turn_row[:, None]).astype(BF)
    places = dot(earlier, chosen.astype(BF))
    place_of = jnp.where(chosen & (places < capacity), places, -1.0).astype(BF)
    slot_ids = jnp.arange(experts_all * capacity, dtype=jnp.int32)
    spread = (slot_ids[None, :] // capacity == expert_ids[:, None]).astype(BF)
    selected = dot(place_of, spread) == (slot_ids % capacity).astype(F32)[None, :]
    return chosen, selected, spread


def attention_forward(layer_in, visible, routed, dense_set, hook):
    attn_gain, w_query, w_key, w_value, w_out, ffn_gain, w_router = dense_set
    local_len = layer_in.shape[0]
    heads_kv = w_key.shape[1] // HEAD_SIZE
    normed, factor_one = normalize(layer_in, attn_gain)
    hidden_one = normed.astype(BF)
    key_rows = dot(hidden_one, w_key).astype(BF)
    value_rows = dot(hidden_one, w_value).astype(BF)
    kv_all = hook(gathered(jnp.concatenate([key_rows, value_rows], 1), 0))
    queries = dot(hidden_one, w_query).astype(BF)
    key_width = w_key.shape[1]
    key_all = kv_all[:, :key_width].reshape(-1, heads_kv, HEAD_SIZE)
    value_all = kv_all[:, key_width:].reshape(-1, heads_kv, HEAD_SIZE)
    grouped_query = queries.reshape(local_len, heads_kv, -1, HEAD_SIZE)
    raw = jnp.einsum("tkgd,skd->kgts", grouped_query, key_all, preferred_element_type=F32) * SCALE
    scores = jnp.where(visible[None, None], raw, masked_score)
    log_total = jax.nn.logsumexp(scores, -1, keepdims=True)
    attn_prob = jnp.exp(scores - log_total)
    attn_mix = jnp.einsum(
        "kgts,skd->tkgd", attn_prob.astype(BF), value_all, preferred_element_type=F32
    )
    attn_mix = attn_mix.reshape(local_len, -1).astype(BF)
    middle = layer_in + dot(attn_mix, w_out)
    normed_two, factor_two = normalize(middle, ffn_gain)
    hidden_two = normed_two.astype(BF)
    chosen, selected, spread = routed
    logits = dot(hidden_two, w_router)
    masked_logits = jnp.where(chosen, logits, masked_score)
    top = jnp.max(masked_logits, -1, keepdims=True)
    powers = jnp.where(chosen, jnp.exp(masked_logits - top), 0.0)
    gate_share = powers / jnp.sum(powers, -1, keepdims=True)
    weighting = jnp.where(selected, dot(gate_share.astype(BF), spread), 0.0).astype(BF)
    return SimpleNamespace(
        layer_in=layer_in,
        factor_one=factor_one,
        hidden_one=hidden_one,
        queries=queries,
        key_all=key_all,
        value_all=value_all,
        attn_prob=attn_prob,
        attn_mix=attn_mix,
        middle=middle,
        factor_two=factor_two,
        hidden_two=hidden_two,
        gate_share=gate_share,
        selected=selected,
        selector=selected.astype(BF),
        spread=spread,
        weighting=weighting,
    )


def expert_forward(arrived, w_gate, w_up):
    gate_pre = dot(arrived, w_gate)
    up_pre = dot(arrived, w_up)
    return gate_pre, up_pre, (jax.nn.silu(gate_pre) * up_pre).astype(BF)


def expert_backward(owed, gate_pre, up_pre, w_down):
    grad_inner = dot_t(owed, w_down)
    sigmoid_a = jax.nn.sigmoid(gate_pre)
    grad_gate_pre = grad_inner * up_pre * sigmoid_a * (1.0 + gate_pre * (1.0 - sigmoid_a))
    return jnp.concatenate([grad_gate_pre, grad_inner * gate_pre * sigmoid_a], 1).astype(BF)


def expert_input(grad_pre, w_gate, w_up):
    width = w_gate.shape[1]
    return dot_t(grad_pre[:, :width], w_gate) + dot_t(grad_pre[:, width:], w_up)


def router_backward(stored, grad_top, returned, w_router):
    match = jnp.where(stored.selected, dot_t(grad_top, returned), 0.0)
    grad_weighting = lax.dot_general(
        match,
        stored.spread.astype(F32),
        (((1,), (1,)), ((), ())),
        precision=lax.Precision.HIGHEST,
        preferred_element_type=F32,
    )
    gate_share = stored.gate_share
    grad_logits = (
        gate_share * (grad_weighting - jnp.sum(gate_share * grad_weighting, -1, keepdims=True))
    ).astype(BF)
    return t_dot(grad_logits, stored.hidden_two), dot_t(grad_logits, w_router)


def attention_backward(stored, grad_top, grad_router, grad_hidden, dense_set, hook):
    attn_gain, w_query, w_key, w_value, w_out, ffn_gain, w_router = dense_set
    local_len = grad_top.shape[0]
    grad_normed_two, grad_ffn_gain = norm_back(
        stored.middle, stored.factor_two, ffn_gain, grad_hidden
    )
    grad_middle = grad_top.astype(F32) + grad_normed_two
    grad_branch = hook("branch", grad_middle.astype(BF))
    grad_mix = dot_t(grad_branch, w_out).astype(BF)
    key_all = stored.key_all
    value_all = stored.value_all
    heads_kv = key_all.shape[1]
    attn_prob = stored.attn_prob
    grouped_grad = grad_mix.reshape(local_len, heads_kv, -1, HEAD_SIZE)
    grad_prob = jnp.einsum("tkgd,skd->kgts", grouped_grad, value_all, preferred_element_type=F32)
    centre = jnp.sum(attn_prob * grad_prob, -1, keepdims=True)
    grad_scores = (attn_prob * (grad_prob - centre)).astype(BF)
    grouped_query = stored.queries.reshape(local_len, heads_kv, -1, HEAD_SIZE)
    grad_keys_all = (
        jnp.einsum("kgts,tkgd->skd", grad_scores, grouped_query, preferred_element_type=F32) * SCALE
    )
    grad_values_all = jnp.einsum(
        "kgts,tkgd->skd", attn_prob.astype(BF), grouped_grad, preferred_element_type=F32
    )
    tree_length = key_all.shape[0]
    grad_kv_all = jnp.concatenate(
        [grad_keys_all.reshape(tree_length, -1), grad_values_all.reshape(tree_length, -1)], 1
    ).astype(BF)
    grad_kv_all = hook("kv_all", grad_kv_all)
    grad_kv = hook("kv", sum_to_owner(grad_kv_all, 0).astype(BF))
    grad_queries = (
        jnp.einsum("kgts,skd->tkgd", grad_scores, key_all, preferred_element_type=F32) * SCALE
    )
    grad_queries = grad_queries.reshape(local_len, -1).astype(BF)
    key_width = w_key.shape[1]
    grad_keys, grad_values = grad_kv[:, :key_width], grad_kv[:, key_width:]
    grad_hidden_one = dot_t(grad_queries, w_query)
    grad_hidden_one = grad_hidden_one + dot_t(grad_keys, w_key)
    grad_hidden_one = grad_hidden_one + dot_t(grad_values, w_value)
    grad_normed_one, grad_attn_gain = norm_back(
        stored.layer_in, stored.factor_one, attn_gain, grad_hidden_one
    )
    grad_input = grad_middle + grad_normed_one
    small = jnp.concatenate([grad_router, grad_attn_gain[None], grad_ffn_gain[None]], 0)
    return SimpleNamespace(
        input=grad_input,
        branch=grad_branch,
        qkv=jnp.concatenate([grad_queries, grad_kv], 1),
        small=jnp.pad(small, ((0, -small.shape[0] % 16), (0, 0))),
    )


def local(
    edge_in,
    seg_lengths,
    routes,
    turns,
    attn_gain,
    w_query,
    w_key,
    w_value,
    w_out,
    ffn_gain,
    w_router,
    w_gate,
    w_up,
    w_down,
):
    edge_rows = edge_in[0, :, 0]
    local_len = edge_rows.shape[1]
    lengths_all = seg_lengths[:, 0]
    is_first = lax.axis_index("section") == 0

    def both_layers(own, received):
        return (jnp.where(is_first, own, received), jnp.where(is_first, received, own))

    def of_micro(pair):
        mine = jnp.where(is_first, pair[0], pair[1])
        others = jnp.where(is_first, pair[1], pair[0])
        return both_layers(mine, swapped(others))

    layer_rows, cotangent = of_micro(edge_rows)
    dense_own = (attn_gain[0], w_query[0], w_key[0], w_value[0], w_out[0], ffn_gain[0], w_router[0])
    dense_pairs = [both_layers(a, swapped(a)) for a in dense_own]
    dense_sets = [tuple(p[i] for p in dense_pairs) for i in range(2)]
    lengths_row = jnp.where(is_first, lengths_all[0], lengths_all[1])
    visible = tree_mask(lengths_row, local_len)
    experts_all, experts = w_router.shape[2], w_gate.shape[1]
    picks = routes.shape[4]
    capacity = local_len * picks // experts_all
    orders = of_micro(
        jnp.concatenate([jnp.swapaxes(routes[0, :, 0], 1, 2), turns[0, :, 0]], 1)
    )
    routed = [routing(o[:picks].T, o[picks], experts_all, capacity) for o in orders]
    gates, ups, downs = (row_halves(a[0], is_first) for a in (w_gate, w_up, w_down))

    gate_first, up_first = expert_in(gates[0]), expert_in(ups[0])
    first = attention_forward(
        layer_rows.astype(F32), visible, routed[0], dense_sets[0], lambda value: value
    )
    outgoing = t_dot(first.selector, first.hidden_two).astype(BF)
    arrived_first = send_out(outgoing, experts_all)
    down_first = expert_in(downs[0])
    gate_pre, up_pre, inner_first = expert_forward(arrived_first, gate_first, up_first)
    pres_first = (gate_pre, up_pre)
    returned_first = send_back(dot(inner_first, down_first).astype(BF), experts_all)
    early = jnp.concatenate([first.hidden_one, first.attn_mix], 0)
    early, returned_first = tie(early, returned_first)
    kept = SimpleNamespace(early=early_operand(early))

    def end(name, value):
        got, value = tie(getattr(kept, name), value)
        setattr(kept, name, got)
        return value

    state = (first.middle + dot(first.weighting, returned_first)).astype(BF)
    gate_second, up_second = expert_in(gates[1]), expert_in(ups[1])
    second = attention_forward(
        state.astype(F32), visible, routed[1], dense_sets[1], lambda value: end("early", value)
    )
    early_first = early_join(kept.early)
    outgoing = jnp.concatenate(
        [t_dot(second.selector, second.hidden_two), t_dot(second.weighting, cotangent)], 1
    ).astype(BF)
    outgoing = send_out(outgoing, experts_all)
    early = jnp.concatenate([second.hidden_one, second.attn_mix], 0)
    early, outgoing = tie(early, outgoing)
    early_second = early_operand(early)
    arrived_second, owed_second = jnp.split(outgoing, 2, 1)
    down_second = expert_in(downs[1])
    gate_pre, up_pre, inner_second = expert_forward(arrived_second, gate_second, up_second)
    grad_pre = expert_backward(owed_second, gate_pre, up_pre, down_second)
    early_second, grad_pre = tie(early_second, grad_pre)
    produced = jnp.concatenate(
        [dot(inner_second, down_second), expert_input(grad_pre, gate_second, up_second)], 1
    ).astype(BF)
    produced = send_back(produced, experts_all)
    gate_up_grad = t_dot(arrived_second, grad_pre).astype(BF)
    down_grad = t_dot(inner_second, owed_second).astype(BF)
    produced, gate_up_grad, down_grad = tie(produced, gate_up_grad, down_grad)
    kept.down1 = expert_out(down_grad, experts)
    returned_second, sent_second = jnp.split(produced, 2, 1)
    top = second.middle + dot(second.weighting, returned_second)
    top_other = lax.ppermute(top, "section", UP)

    grad_router, grad_hidden = router_backward(
        second, cotangent, returned_second, dense_sets[1][6]
    )
    grad_hidden = grad_hidden + dot(second.selector, sent_second)
    later = attention_backward(
        second,
        cotangent,
        grad_router,
        grad_hidden,
        dense_sets[1],
        lambda name, value: value,
    )
    grad = later.input.astype(BF)
    branch, qkv, grad = tie(later.branch, later.qkv, grad)
    late = late_operands([branch, qkv])
    width = late[0].shape[1]
    outgoing = end("down1", t_dot(first.weighting, grad).astype(BF))
    owed_first = send_out(outgoing, experts_all)
    late, owed_first = tie(late, owed_first)
    hidden_early, mix_early = early_join(early_second)
    kept.dense = dense_partial([mix_early, hidden_early], late)
    for flip in flips("dp")[:-1]:
        kept.dense = dense_rows_step(kept.dense, flip)
    grad_pre = expert_backward(owed_first, *pres_first, down_first)
    grad_arrived = expert_input(grad_pre, gate_first, up_first).astype(BF)
    first_grads = [t_dot(arrived_first, grad_pre).astype(BF)]
    first_grads.append(t_dot(inner_first, owed_first).astype(BF))
    sent_first = send_back(end("dense", grad_arrived), experts_all)
    kept.dense = dense_rows_step(kept.dense, flips("dp")[-1]).astype(BF)
    kept.dense, sent_first = tie(kept.dense, sent_first)
    kept.dense, gate_up_grad = tie(dense_line(kept.dense), gate_up_grad)
    kept.gate_up1 = expert_out(gate_up_grad, experts)
    grad_router, grad_hidden = router_backward(first, grad, returned_first, dense_sets[0][6])
    grad_hidden = grad_hidden + dot(first.selector, sent_first)

    def hook(name, value):
        if name == "branch":
            kept.late = late_operands([value])
        if name == "kv_all":
            value = end("late", value)
            kept.out = dense_partial([early_first[1]], kept.late)
            kept.dense = dense_groups(kept.dense)
            value = end("dense", end("out", value))
        if name == "kv":
            value = end("gate_up1", value)
            kept.out = dense_rows_step(kept.out, flips("dp")[0])
            down_grad, value, kept.out = tie(first_grads[1], value, kept.out)
            kept.down0 = expert_out(down_grad, experts)
        return value

    earlier = attention_backward(
        first, grad, grad_router, grad_hidden, dense_sets[0], hook
    )
    smalls = small_sum(
        jnp.where(is_first, earlier.small, later.small),
        jnp.where(is_first, later.small, earlier.small),
    )
    qkv_total = dense_partial([early_first[0]], late_operands([earlier.qkv]))
    small_rows, small_columns = smalls.shape
    qkv_total = with_small(qkv_total, smalls)
    qkv_total, down_part, out_total = tie(qkv_total, kept.down0, kept.out)
    steps = [(dense_rows_step, flip) for flip in flips("dp")]
    steps += [(dense_line_step, flip) for flip in reversed(flips("dp"))]
    turning = len(flips("dp"))
    for index in range(len(steps)):
        if index + 1 < len(steps):
            step, flip = steps[index + 1]
            out_total = out_total.astype(BF) if index + 1 >= turning else out_total
            out_total = step(out_total, flip)
        step, flip = steps[index]
        qkv_total = step(qkv_total.astype(BF) if index >= turning else qkv_total, flip)
        qkv_total, out_total = tie(qkv_total, out_total)
    qkv_total, out_total, gate_up_grad = tie(qkv_total, out_total, first_grads[0])
    gate_up_part = expert_out(gate_up_grad, experts)
    second_total = kept.dense
    second_other = lax.ppermute(second_total, "section", UP)
    down_total = expert_home(two_homes(down_part, kept.down1))
    out_total = dense_groups(out_total)
    out_other = lax.ppermute(out_total, "section", DOWN)
    homes = (out_total, second_total, out_other, second_other)
    out = dense_home(homes, [0] * 4, width, [w_out.shape[2]])[0]
    qkv_total = dense_groups(qkv_total)
    small = small_of(qkv_total, small_rows, small_columns)
    qkv_other = lax.ppermute(qkv_total, "section", DOWN)
    homes = (qkv_total, second_total, qkv_other, second_other)
    query, key, value = dense_home(
        homes,
        [0, width, 0, width],
        qkv_total.shape[3],
        [w_query.shape[2], w_key.shape[2], w_value.shape[2]],
    )
    grad = earlier.input
    grad_other = lax.ppermute(grad, "section", DOWN)
    edge_out = jnp.where(
        is_first, jnp.stack([grad, grad_other]), jnp.stack([top_other, top])
    )[None, :, None]
    gate_up_part, down_total, out, query, key, value, edge_out, small = tie(
        gate_up_part, down_total, out, query, key, value, edge_out, small
    )
    pair = (gate_up_part, kept.gate_up1)
    received = two_homes(*pair)[2:]
    expert_total = list(expert_rows(received, 2, True, expert_rows(pair, 2, False))) + down_total
    dense_out = (
        small[experts_all],
        query,
        key,
        value,
        out,
        small[experts_all + 1],
        small[:experts_all].T,
    )
    return (
        (edge_out,)
        + tuple((piece[None] for piece in dense_out))
        + tuple((piece[None] for piece in expert_total))
    )


def solution(mesh):
    section, expert, dp = "section", "expert", "dp"
    tokens = P(section, None, expert, dp, None)
    vector, matrix = P(section, None), P(section, None, None)
    rows = P(section, expert, dp, None)
    dense = (vector, matrix, matrix, matrix, matrix, vector, matrix)
    return jax.shard_map(
        local,
        mesh=mesh,
        in_specs=(tokens, P(None, expert, None), tokens, tokens) + dense + (rows, rows, rows),
        out_specs=(tokens,) + dense + (rows, rows, rows),
        check_vma=False,
    )
```

```python
from types import SimpleNamespace

import jax
import jax.numpy as jnp
import numpy as np
from jax import lax
from jax.experimental import pallas as pl
from jax.experimental.pallas import tpu as pltpu
from jax.sharding import PartitionSpec as P

HEAD_SIZE = 128
SCALE = HEAD_SIZE ** (-0.5)
epsilon = 1e-06
masked_score = -1e30
BF = jnp.bfloat16
F32 = jnp.float32

SWAP = [(0, 1), (1, 0)]
UP = [(0, 1)]
DOWN = [(1, 0)]
OWNERS = ("expert", "dp", "section")
LINE = ("dp", "section")


def ancestry():
    parents = [-1]
    for branch_index in range(4):
        parents += [0, 1 + 3 * branch_index, 1 + 3 * branch_index]
    lineage = np.zeros((13, 13), np.float32)
    for segment in range(13):
        current = segment
        while current >= 0:
            lineage[current, segment] = 1.0
            current = parents[current]
    return lineage


def dot(left, right):
    return jnp.dot(left, right, preferred_element_type=F32)


def dot_t(left, right):
    return lax.dot_general(left, right, (((1,), (1,)), ((), ())), preferred_element_type=F32)


def t_dot(left, right):
    return lax.dot_general(left, right, (((0,), (0,)), ((), ())), preferred_element_type=F32)


def t_dot_t(left, right):
    return lax.dot_general(left, right, (((0,), (1,)), ((), ())), preferred_element_type=F32)


def normalize(values, gain_vec):
    factor = lax.rsqrt(jnp.mean(values * values, -1, keepdims=True) + epsilon)
    return (values * factor * gain_vec, factor)


def norm_back(values, factor, gain_vec, upstream):
    scaled = upstream * gain_vec
    grad_gain = jnp.sum(upstream * values * factor, 0)
    inner_mean = jnp.mean(scaled * values, -1, keepdims=True)
    return (scaled * factor - values * factor * factor * factor * inner_mean, grad_gain)


def tree_mask(lengths_row, local_len):
    own = lax.axis_index("dp")
    first_row = own * local_len
    seg_ends = jnp.cumsum(lengths_row)
    blocks = own ^ jnp.asarray(block_order(), jnp.int32)
    key_spots = (
        blocks[:, None] * local_len + jnp.arange(local_len, dtype=jnp.int32)[None, :]
    ).reshape(-1)
    query_spots = first_row + jnp.arange(local_len, dtype=jnp.int32)
    seg_ids = jnp.arange(13, dtype=jnp.int32)
    key_seg = jnp.sum((key_spots[:, None] >= seg_ends[None, :]).astype(jnp.int32), 1)
    query_seg = jnp.sum((query_spots[:, None] >= seg_ends[None, :]).astype(jnp.int32), 1)
    key_hot = (key_seg[:, None] == seg_ids[None, :]).astype(BF)
    query_hot = (query_seg[:, None] == seg_ids[None, :]).astype(BF)
    allowed = dot(query_hot, jnp.asarray(ancestry(), BF)).astype(BF)
    linked = dot_t(allowed, key_hot) > 0.5
    return linked & (key_spots[None, :] <= query_spots[:, None])


def tie(*values):
    return lax.optimization_barrier(values)


def swapped(shard):
    return lax.ppermute(shard, "section", SWAP)


def partners(axis, flip):
    return [(i, i ^ flip) for i in range(lax.axis_size(axis))]


def flips(axis):
    found = [1]
    while 2 * found[-1] < lax.axis_size(axis):
        found.append(2 * found[-1])
    return found


def block_order():
    order = [0]
    for flip in reversed(flips("dp")):
        order = order + [k ^ flip for k in order]
    return order


def gathered(shard, axis, over="dp"):
    for flip in reversed(flips(over)):
        shard = jnp.concatenate([shard, lax.ppermute(shard, over, partners(over, flip))], axis)
    return shard


def sum_to_owner(partial, axis):
    sent_as = partial.dtype
    for flip in flips("dp"):
        kept, sent = jnp.split(partial, 2, axis)
        sent = lax.ppermute(sent.astype(sent_as), "dp", partners("dp", flip))
        partial = kept.astype(F32) + sent.astype(F32)
    return partial


def pick_blocks(sources, blocks, pick, count, kernel, out_shapes, out_blocks, place=None, into=()):
    where = jnp.stack([lax.axis_index(axis) for axis in ("section", "dp")]).astype(jnp.int32)

    def spec(at):
        def index(k, where):
            return pick(k, where)[at]

        return pl.BlockSpec(blocks[at], index)

    def body(where, *refs):
        kernel(pl.program_id(0), where, refs[: len(sources)], refs[len(sources) + len(into) :])

    return pl.pallas_call(
        body,
        grid_spec=pltpu.PrefetchScalarGridSpec(
            num_scalar_prefetch=1,
            grid=(count,),
            in_specs=[spec(at) for at in range(len(sources))]
            + [pl.BlockSpec(memory_space=pl.ANY)] * len(into),
            out_specs=[
                pl.BlockSpec(shape, place or (lambda k, where: (k,) + (0,) * (len(shape) - 1)))
                for shape in out_blocks
            ],
        ),
        out_shape=[jax.ShapeDtypeStruct(shape, F32) for shape in out_shapes],
        input_output_aliases={1 + len(sources) + at: at for at in range(len(into))},
        compiler_params=pltpu.CompilerParams(vmem_limit_bytes=48 * 1024 * 1024),
    )(where, *sources, *into)


def two_homes(first, second):
    return (
        first,
        second,
        lax.ppermute(first, "section", DOWN),
        lax.ppermute(second, "section", UP),
    )


def source_of(section, core):
    return jnp.where(core == section, section, 2 + section)


def dense_home(homes, offsets, width, out_widths):
    parts, groups, rows, _ = homes[1].shape
    block = rows // 2

    def pick(k, where):
        used = source_of(where[0], k // (2 * parts))
        return [
            (jnp.where(used == source, k // 2 % parts, 0), 0, jnp.where(used == source, k % 2, 0), 0)
            for source in range(4)
        ]

    def kernel(k, where, sources, outs):
        used = source_of(where[0], k // (2 * parts))
        for source in range(4):

            @pl.when(used == source)
            def _():
                out, at = 0, 0
                for group in range(groups):
                    start = offsets[source]
                    stop = start + width
                    while start < stop:
                        piece = min(stop - start, out_widths[out] - at)
                        outs[out][:, at : at + piece] = sources[source][
                            0, group, :, start : start + piece
                        ].astype(F32)
                        start, at = start + piece, at + piece
                        if at == out_widths[out]:
                            out, at = out + 1, 0

    count = 4 * parts
    shapes = [(count * block, w) for w in out_widths]
    blocks = [(1, groups, block, home.shape[3]) for home in homes]
    return pick_blocks(
        homes, blocks, pick, count, kernel, shapes, [(block, w) for w in out_widths]
    )


def two_parts(array, index, axis=0):
    half = array.shape[axis] // 2
    return (
        lax.dynamic_slice_in_dim(array, index * half, half, axis),
        lax.dynamic_slice_in_dim(array, (1 - index) * half, half, axis),
    )


def in_order(mine, others, index, axis):
    first = index == 0
    return jnp.concatenate(
        [jnp.where(first, mine, others), jnp.where(first, others, mine)], axis
    )


def early_operand(rows):
    mine, others = two_parts(rows, lax.axis_index("section"), 1)
    half = mine.shape[1]
    joined = jnp.stack([mine.reshape(2, -1, half), swapped(others).reshape(2, -1, half)], 1)
    joined = joined[:, None]
    for flip in reversed(flips("expert")):
        others = lax.ppermute(joined, "expert", partners("expert", flip))
        if flip == 1:
            return joined, others
        joined = jnp.concatenate([joined, others], 1)


def early_join(pair):
    joined = jnp.concatenate(pair, 1)
    return joined.reshape(2, -1, joined.shape[-1])


def late_operands(operands):
    groups = lax.axis_size("expert")
    own = lax.axis_index("expert")
    blocks = []
    order = [0]
    for flip in reversed(flips("expert")):
        order = order + [k ^ flip for k in order]
    for flip in order:
        shares = []
        for rows in operands:
            share = rows.shape[1] // groups
            shares.append(lax.dynamic_slice_in_dim(rows, (own ^ flip) * share, share, 1))
        block = jnp.concatenate(shares, 1)
        if flip > 0:
            block = lax.ppermute(block, "expert", partners("expert", flip))
        blocks.append(block)
    joined = jnp.stack(blocks)
    joined = jnp.stack([joined, swapped(joined)], 1)
    joined = joined.reshape(-1, joined.shape[-1])
    return jnp.split(joined, np.cumsum([a.shape[1] // groups for a in operands])[:-1], 1)


def dense_partial(early, late):
    return jnp.concatenate([t_dot(e, p) for e, p in zip(early, late, strict=True)], 1)


def dense_rows(partial):
    for flip in flips("dp"):
        partial = dense_rows_step(partial, flip)
    return partial.astype(BF)


def dense_rows_step(partial, flip):
    own = lax.axis_index("dp")
    kept, sent = two_parts(partial, jnp.where((own & flip) == 0, 0, 1))
    sent = lax.ppermute(sent.astype(BF), "dp", partners("dp", flip))
    return kept.astype(F32) + sent.astype(F32)


def dense_line(total):
    for flip in reversed(flips("dp")):
        total = dense_line_step(total, flip)
    return total


def dense_line_step(total, flip):
    others = lax.ppermute(total, "dp", partners("dp", flip))
    return in_order(total, others, lax.axis_index("dp") & flip, 0)


def group_parts(total):
    axes = (1,) * len(flips("expert"))
    return [part.reshape(axes + part.shape) for part in jnp.split(total, 2, 0)]


def group_step(parts, index):
    own = lax.axis_index("expert")
    order = flips("expert")
    stepped = []
    for part, way in zip(parts, (order, order[::-1]), strict=True):
        flip = way[index]
        others = lax.ppermute(part, "expert", partners("expert", flip))
        axis = len(order) - 1 - order.index(flip)
        stepped.append(in_order(part, others, own & flip, axis))
    return stepped


def group_join(parts):
    return jnp.stack([part.reshape((-1,) + part.shape[-2:]) for part in parts])


def dense_groups(total):
    parts = group_parts(total)
    for index in range(len(flips("expert"))):
        parts = group_step(parts, index)
    return group_join(parts)


def small_sum(mine, others):
    total = mine + swapped(others.astype(BF)).astype(F32)
    for flip in flips("expert"):
        total = total + lax.ppermute(
            total.astype(BF), "expert", partners("expert", flip)
        ).astype(F32)
    return total


def with_small(partial, small):
    width = small.shape[1] // lax.axis_size("expert")
    share = lax.dynamic_slice_in_dim(small, lax.axis_index("expert") * width, width, 1)
    share = jnp.pad(share, ((0, -small.shape[0] % 64), (0, partial.shape[1] - width)))
    halves = [jnp.split(a, 2, 0) for a in (partial, share)]
    return jnp.concatenate([a[k] for k in range(2) for a in halves], 0)


def small_of(total, rows, columns):
    first = total.shape[2] - (rows + -rows % 64) // 2
    part = jnp.transpose(total[:, :, first:, : columns // total.shape[1]], (0, 2, 1, 3))
    return part.reshape(-1, part.shape[2] * part.shape[3])[:rows].astype(F32)


def exchange(rows, axes):
    return lax.all_to_all(rows, axes, split_axis=0, concat_axis=0, tiled=True)


def copies_of_expert(experts_all):
    owners = lax.axis_size("expert") * lax.axis_size("dp") * lax.axis_size("section")
    return owners // experts_all


def send_out(slot_rows, experts_all):
    width = slot_rows.shape[-1]
    copies = copies_of_expert(experts_all)
    rows = slot_rows.reshape(experts_all, -1, width)
    if copies > 1:
        mine = jnp.arange(copies) == lax.axis_index("dp") % copies
        rows = jnp.where(mine[None, :, None, None], rows[:, None], 0)
        rows = rows.reshape(experts_all * copies, -1, width)
    return exchange(rows, OWNERS).reshape(-1, width)


def send_back(rows, experts_all):
    width = rows.shape[-1]
    copies = copies_of_expert(experts_all)
    rows = exchange(rows.reshape(experts_all * copies, -1, width), OWNERS)
    if copies > 1:
        rows = rows.reshape(experts_all, copies, -1, width)
        rows = lax.dynamic_index_in_dim(rows, lax.axis_index("dp") % copies, 1, False)
    return rows.reshape(-1, width)


def row_halves(own, is_first):
    half = own.shape[1] // 2
    received = swapped(two_parts(own, lax.axis_index("section"), 1)[1])
    return (
        jnp.where(is_first, own[:, :half], received),
        jnp.where(is_first, received, own[:, half:]),
    )


def expert_in(rows):
    copies = lax.axis_size("dp") * lax.axis_size("section") // rows.shape[0]
    if copies > 1:
        rows = jnp.repeat(rows, copies, 0)
    return exchange(rows, LINE).reshape(-1, rows.shape[-1])


def expert_out(grad, experts):
    size = lax.axis_size("dp") * lax.axis_size("section")
    columns = grad.shape[1]
    pieces = exchange(grad.reshape(size, -1, columns), LINE)
    copies = size // experts
    if copies > 1:
        pieces = pieces.reshape(experts, copies, -1, columns).astype(F32)
        pieces = jnp.sum(pieces, 1).astype(BF)
    return pieces


def expert_home(homes, count=1):
    experts, rows, width = homes[0].shape
    columns = width // count

    def pick(k, where):
        section = where[0]
        used = [section, 2 + section]
        return [
            (jnp.where((used[0] == source) | (used[1] == source), k, 0), 0, 0)
            for source in range(4)
        ]

    def kernel(k, where, sources, outs):
        for core in range(2):
            used = source_of(where[0], core)
            for source in range(4):

                @pl.when(used == source)
                def _():
                    for part, out in enumerate(outs):
                        out[0, core * rows : (core + 1) * rows] = sources[source][
                            0, :, part * columns : (part + 1) * columns
                        ].astype(F32)

    shape = (experts, 2 * rows, columns)
    blocks = [(1, rows, width)] * 4
    return list(
        pick_blocks(homes, blocks, pick, experts, kernel, [shape] * count, [(1,) + shape[1:]] * count)
    )


def expert_rows(arrays, count, others, into=()):
    experts, rows, width = arrays[0].shape
    columns = width // count

    def pick(k, where):
        return [(jnp.where(where[0] == layer, k, 0), 0, 0) for layer in range(2)]

    def place(k, where):
        return (k, 1 - where[0] if others else where[0], 0)

    def kernel(k, where, sources, outs):
        for layer in range(2):

            @pl.when(where[0] == layer)
            def _():
                for part, out in enumerate(outs):
                    out[0] = sources[layer][0, :, part * columns : (part + 1) * columns].astype(F32)

    shape = (experts, 2 * rows, columns)
    return pick_blocks(
        arrays,
        [(1, rows, width)] * 2,
        pick,
        experts,
        kernel,
        [shape] * count,
        [(1, rows, columns)] * count,
        place,
        into,
    )


def routing(route_rows, turn_row, experts_all, capacity):
    expert_ids = jnp.arange(experts_all, dtype=jnp.int32)
    chosen = jnp.any(route_rows[:, :, None] == expert_ids[None, None, :], 1)
    earlier = (turn_row[None, :] < turn_row[:, None]).astype(BF)
    places = dot(earlier, chosen.astype(BF))
    place_of = jnp.where(chosen & (places < capacity), places, -1.0).astype(BF)
    slot_ids = jnp.arange(experts_all * capacity, dtype=jnp.int32)
    spread = (slot_ids[None, :] // capacity == expert_ids[:, None]).astype(BF)
    selected = dot(place_of, spread) == (slot_ids % capacity).astype(F32)[None, :]
    return chosen, selected, spread


def attention_forward(layer_in, visible, routed, dense_set, hook):
    attn_gain, w_query, w_key, w_value, w_out, ffn_gain, w_router = dense_set
    local_len = layer_in.shape[0]
    heads_kv = w_key.shape[1] // HEAD_SIZE
    normed, factor_one = normalize(layer_in, attn_gain)
    hidden_one = normed.astype(BF)
    key_rows = dot(hidden_one, w_key).astype(BF)
    value_rows = dot(hidden_one, w_value).astype(BF)
    queries = dot(hidden_one, w_query).astype(BF)
    queries, kv_rows = tie(queries, jnp.concatenate([key_rows, value_rows], 1))
    kv_all = hook(gathered(kv_rows, 0))
    key_width = w_key.shape[1]
    key_all = kv_all[:, :key_width].reshape(-1, heads_kv, HEAD_SIZE)
    value_all = kv_all[:, key_width:].reshape(-1, heads_kv, HEAD_SIZE)
    grouped_query = queries.reshape(local_len, heads_kv, -1, HEAD_SIZE)
    raw = jnp.einsum("tkgd,skd->kgts", grouped_query, key_all, preferred_element_type=F32) * SCALE
    scores = jnp.where(visible[None, None], raw, masked_score)
    log_total = jax.nn.logsumexp(scores, -1, keepdims=True)
    attn_prob = jnp.exp(scores - log_total)
    attn_mix = jnp.einsum(
        "kgts,skd->tkgd", attn_prob.astype(BF), value_all, preferred_element_type=F32
    )
    attn_mix = attn_mix.reshape(local_len, -1).astype(BF)
    middle = layer_in + dot(attn_mix, w_out)
    normed_two, factor_two = normalize(middle, ffn_gain)
    hidden_two = normed_two.astype(BF)
    chosen, selected, spread = routed
    logits = dot(hidden_two, w_router)
    masked_logits = jnp.where(chosen, logits, masked_score)
    top = jnp.max(masked_logits, -1, keepdims=True)
    powers = jnp.where(chosen, jnp.exp(masked_logits - top), 0.0)
    gate_share = powers / jnp.sum(powers, -1, keepdims=True)
    weighting = jnp.where(selected, dot(gate_share.astype(BF), spread), 0.0).astype(BF)
    return SimpleNamespace(
        layer_in=layer_in,
        factor_one=factor_one,
        hidden_one=hidden_one,
        queries=queries,
        key_all=key_all,
        value_all=value_all,
        attn_prob=attn_prob,
        attn_mix=attn_mix,
        middle=middle,
        factor_two=factor_two,
        hidden_two=hidden_two,
        gate_share=gate_share,
        selected=selected,
        selector=selected.astype(BF),
        spread=spread,
        weighting=weighting,
    )


def expert_forward(arrived, w_gate, w_up):
    gate_pre = dot(arrived, w_gate)
    up_pre = dot(arrived, w_up)
    return gate_pre, up_pre, (jax.nn.silu(gate_pre) * up_pre).astype(BF)


def expert_backward(owed, gate_pre, up_pre, w_down):
    grad_inner = dot_t(owed, w_down)
    sigmoid_a = jax.nn.sigmoid(gate_pre)
    grad_gate_pre = grad_inner * up_pre * sigmoid_a * (1.0 + gate_pre * (1.0 - sigmoid_a))
    return jnp.concatenate([grad_gate_pre, grad_inner * gate_pre * sigmoid_a], 1).astype(BF)


def expert_input(grad_pre, w_gate, w_up):
    width = w_gate.shape[1]
    return dot_t(grad_pre[:, :width], w_gate) + dot_t(grad_pre[:, width:], w_up)


def router_backward(stored, grad_top, returned, w_router):
    match = jnp.where(stored.selected, dot_t(grad_top, returned), 0.0)
    grad_weighting = lax.dot_general(
        match,
        stored.spread.astype(F32),
        (((1,), (1,)), ((), ())),
        precision=lax.Precision.HIGHEST,
        preferred_element_type=F32,
    )
    gate_share = stored.gate_share
    grad_logits = (
        gate_share * (grad_weighting - jnp.sum(gate_share * grad_weighting, -1, keepdims=True))
    ).astype(BF)
    return t_dot(grad_logits, stored.hidden_two), dot_t(grad_logits, w_router)


def attention_backward(stored, grad_top, grad_router, grad_hidden, dense_set, hook):
    attn_gain, w_query, w_key, w_value, w_out, ffn_gain, w_router = dense_set
    local_len = grad_top.shape[0]
    grad_normed_two, grad_ffn_gain = norm_back(
        stored.middle, stored.factor_two, ffn_gain, grad_hidden
    )
    grad_middle = grad_top.astype(F32) + grad_normed_two
    grad_branch = hook("branch", grad_middle.astype(BF))
    grad_mix = dot_t(grad_branch, w_out).astype(BF)
    key_all = stored.key_all
    value_all = stored.value_all
    heads_kv = key_all.shape[1]
    attn_prob = stored.attn_prob
    grouped_grad = grad_mix.reshape(local_len, heads_kv, -1, HEAD_SIZE)
    grad_prob = jnp.einsum("tkgd,skd->kgts", grouped_grad, value_all, preferred_element_type=F32)
    centre = jnp.sum(attn_prob * grad_prob, -1, keepdims=True)
    grad_scores = (attn_prob * (grad_prob - centre)).astype(BF)
    grouped_query = stored.queries.reshape(local_len, heads_kv, -1, HEAD_SIZE)
    grad_keys_all = (
        jnp.einsum("kgts,tkgd->skd", grad_scores, grouped_query, preferred_element_type=F32) * SCALE
    )
    grad_values_all = jnp.einsum(
        "kgts,tkgd->skd", attn_prob.astype(BF), grouped_grad, preferred_element_type=F32
    )
    tree_length = key_all.shape[0]
    grad_kv_all = jnp.concatenate(
        [grad_keys_all.reshape(tree_length, -1), grad_values_all.reshape(tree_length, -1)], 1
    ).astype(BF)
    grad_kv_all = hook("kv_all", grad_kv_all)
    grad_kv = hook("kv", sum_to_owner(grad_kv_all, 0).astype(BF))
    grad_queries = (
        jnp.einsum("kgts,skd->tkgd", grad_scores, key_all, preferred_element_type=F32) * SCALE
    )
    grad_queries = grad_queries.reshape(local_len, -1).astype(BF)
    key_width = w_key.shape[1]
    grad_keys, grad_values = grad_kv[:, :key_width], grad_kv[:, key_width:]
    grad_hidden_one = dot_t(grad_queries, w_query)
    grad_hidden_one = grad_hidden_one + dot_t(grad_keys, w_key)
    grad_hidden_one = grad_hidden_one + dot_t(grad_values, w_value)
    grad_normed_one, grad_attn_gain = norm_back(
        stored.layer_in, stored.factor_one, attn_gain, grad_hidden_one
    )
    grad_input = grad_middle + grad_normed_one
    small = jnp.concatenate([grad_router, grad_attn_gain[None], grad_ffn_gain[None]], 0)
    return SimpleNamespace(
        input=grad_input,
        branch=grad_branch,
        qkv=jnp.concatenate([grad_queries, grad_kv], 1),
        small=jnp.pad(small, ((0, -small.shape[0] % 16), (0, 0))),
    )


def local(
    edge_in,
    seg_lengths,
    routes,
    turns,
    attn_gain,
    w_query,
    w_key,
    w_value,
    w_out,
    ffn_gain,
    w_router,
    w_gate,
    w_up,
    w_down,
):
    edge_rows = edge_in[0, :, 0]
    local_len = edge_rows.shape[1]
    lengths_all = seg_lengths[:, 0]
    is_first = lax.axis_index("section") == 0

    def both_layers(own, received):
        return (jnp.where(is_first, own, received), jnp.where(is_first, received, own))

    def of_micro(pair):
        mine = jnp.where(is_first, pair[0], pair[1])
        others = jnp.where(is_first, pair[1], pair[0])
        return both_layers(mine, swapped(others))

    layer_rows, cotangent = of_micro(edge_rows)
    dense_own = (attn_gain[0], w_query[0], w_key[0], w_value[0], w_out[0], ffn_gain[0], w_router[0])
    dense_pairs = [both_layers(a, swapped(a)) for a in dense_own]
    dense_sets = [tuple(p[i] for p in dense_pairs) for i in range(2)]
    lengths_row = jnp.where(is_first, lengths_all[0], lengths_all[1])
    visible = tree_mask(lengths_row, local_len)
    experts_all, experts = w_router.shape[2], w_gate.shape[1]
    picks = routes.shape[4]
    capacity = local_len * picks // experts_all
    orders = of_micro(
        jnp.concatenate([jnp.swapaxes(routes[0, :, 0], 1, 2), turns[0, :, 0]], 1)
    )
    routed = [routing(o[:picks].T, o[picks], experts_all, capacity) for o in orders]
    gates, ups, downs = (row_halves(a[0], is_first) for a in (w_gate, w_up, w_down))

    gate_first, up_first = expert_in(gates[0]), expert_in(ups[0])
    first = attention_forward(
        layer_rows.astype(F32), visible, routed[0], dense_sets[0], lambda value: value
    )
    outgoing = t_dot(first.selector, first.hidden_two).astype(BF)
    arrived_first = send_out(outgoing, experts_all)
    down_first = expert_in(downs[0])
    gate_pre, up_pre, inner_first = expert_forward(arrived_first, gate_first, up_first)
    pres_first = (gate_pre, up_pre)
    returned_first = send_back(dot(inner_first, down_first).astype(BF), experts_all)
    early = jnp.concatenate([first.hidden_one, first.attn_mix], 0)
    early, returned_first = tie(early, returned_first)
    kept = SimpleNamespace(early=early_operand(early))

    def end(name, value):
        got, value = tie(getattr(kept, name), value)
        setattr(kept, name, got)
        return value

    state = (first.middle + dot(first.weighting, returned_first)).astype(BF)
    gate_second, up_second = expert_in(gates[1]), expert_in(ups[1])
    second = attention_forward(
        state.astype(F32), visible, routed[1], dense_sets[1], lambda value: end("early", value)
    )
    early_first = early_join(kept.early)
    outgoing = jnp.concatenate(
        [t_dot(second.selector, second.hidden_two), t_dot(second.weighting, cotangent)], 1
    ).astype(BF)
    outgoing = send_out(outgoing, experts_all)
    early = jnp.concatenate([second.hidden_one, second.attn_mix], 0)
    early, outgoing = tie(early, outgoing)
    early_second = early_operand(early)
    arrived_second, owed_second = jnp.split(outgoing, 2, 1)
    down_second = expert_in(downs[1])
    gate_pre, up_pre, inner_second = expert_forward(arrived_second, gate_second, up_second)
    grad_pre = expert_backward(owed_second, gate_pre, up_pre, down_second)
    early_second, grad_pre = tie(early_second, grad_pre)
    produced = jnp.concatenate(
        [dot(inner_second, down_second), expert_input(grad_pre, gate_second, up_second)], 1
    ).astype(BF)
    produced = send_back(produced, experts_all)
    gate_up_grad = t_dot(arrived_second, grad_pre).astype(BF)
    down_grad = t_dot(inner_second, owed_second).astype(BF)
    produced, gate_up_grad, down_grad = tie(produced, gate_up_grad, down_grad)
    kept.down1 = expert_out(down_grad, experts)
    returned_second, sent_second = jnp.split(produced, 2, 1)
    top = second.middle + dot(second.weighting, returned_second)
    top_other = lax.ppermute(top, "section", UP)

    grad_router, grad_hidden = router_backward(
        second, cotangent, returned_second, dense_sets[1][6]
    )
    grad_hidden = grad_hidden + dot(second.selector, sent_second)
    later = attention_backward(
        second,
        cotangent,
        grad_router,
        grad_hidden,
        dense_sets[1],
        lambda name, value: value,
    )
    grad = later.input.astype(BF)
    branch, qkv, grad = tie(later.branch, later.qkv, grad)
    late = late_operands([branch, qkv])
    width = late[0].shape[1]
    outgoing = end("down1", t_dot(first.weighting, grad).astype(BF))
    owed_first = send_out(outgoing, experts_all)
    late, owed_first = tie(late, owed_first)
    hidden_early, mix_early = early_join(early_second)
    kept.dense = dense_partial([mix_early, hidden_early], late)
    for flip in flips("dp")[:-1]:
        kept.dense = dense_rows_step(kept.dense, flip)
    grad_pre = expert_backward(owed_first, *pres_first, down_first)
    grad_arrived = expert_input(grad_pre, gate_first, up_first).astype(BF)
    first_grads = [t_dot(arrived_first, grad_pre).astype(BF)]
    first_grads.append(t_dot(inner_first, owed_first).astype(BF))
    sent_first = send_back(end("dense", grad_arrived), experts_all)
    kept.dense = dense_rows_step(kept.dense, flips("dp")[-1]).astype(BF)
    kept.dense, sent_first = tie(kept.dense, sent_first)
    kept.dense, gate_up_grad = tie(dense_line(kept.dense), gate_up_grad)
    kept.gate_up1 = expert_out(gate_up_grad, experts)
    grad_router, grad_hidden = router_backward(first, grad, returned_first, dense_sets[0][6])
    grad_hidden = grad_hidden + dot(first.selector, sent_first)

    def hook(name, value):
        if name == "branch":
            kept.late = late_operands([value])
        if name == "kv_all":
            value = end("late", value)
            kept.out = dense_partial([early_first[1]], kept.late)
            kept.dense = dense_groups(kept.dense)
            value = end("dense", end("out", value))
        if name == "kv":
            value = end("gate_up1", value)
            kept.out = dense_rows_step(kept.out, flips("dp")[0])
            down_grad, value, kept.out = tie(first_grads[1], value, kept.out)
            kept.down0 = expert_out(down_grad, experts)
        return value

    earlier = attention_backward(
        first, grad, grad_router, grad_hidden, dense_sets[0], hook
    )
    smalls = small_sum(
        jnp.where(is_first, earlier.small, later.small),
        jnp.where(is_first, later.small, earlier.small),
    )
    qkv_total = dense_partial([early_first[0]], late_operands([earlier.qkv]))
    small_rows, small_columns = smalls.shape
    qkv_total = with_small(qkv_total, smalls)
    qkv_total, down_part, out_total = tie(qkv_total, kept.down0, kept.out)
    steps = [(dense_rows_step, flip) for flip in flips("dp")]
    steps += [(dense_line_step, flip) for flip in reversed(flips("dp"))]
    turning = len(flips("dp"))
    for index in range(len(steps)):
        if index + 1 < len(steps):
            step, flip = steps[index + 1]
            out_total = out_total.astype(BF) if index + 1 >= turning else out_total
            out_total = step(out_total, flip)
        step, flip = steps[index]
        qkv_total = step(qkv_total.astype(BF) if index >= turning else qkv_total, flip)
        qkv_total, out_total = tie(qkv_total, out_total)
    qkv_total, out_total, gate_up_grad = tie(qkv_total, out_total, first_grads[0])
    gate_up_part = expert_out(gate_up_grad, experts)
    second_total = kept.dense
    second_other = lax.ppermute(second_total, "section", UP)
    down_total = expert_home(two_homes(down_part, kept.down1))
    out_total = dense_groups(out_total)
    out_other = lax.ppermute(out_total, "section", DOWN)
    homes = (out_total, second_total, out_other, second_other)
    out = dense_home(homes, [0] * 4, width, [w_out.shape[2]])[0]
    qkv_total = dense_groups(qkv_total)
    small = small_of(qkv_total, small_rows, small_columns)
    qkv_other = lax.ppermute(qkv_total, "section", DOWN)
    homes = (qkv_total, second_total, qkv_other, second_other)
    query, key, value = dense_home(
        homes,
        [0, width, 0, width],
        qkv_total.shape[3],
        [w_query.shape[2], w_key.shape[2], w_value.shape[2]],
    )
    grad = earlier.input
    grad_other = lax.ppermute(grad, "section", DOWN)
    edge_out = jnp.where(
        is_first, jnp.stack([grad, grad_other]), jnp.stack([top_other, top])
    )[None, :, None]
    gate_up_part, down_total, out, query, key, value, edge_out, small = tie(
        gate_up_part, down_total, out, query, key, value, edge_out, small
    )
    pair = (gate_up_part, kept.gate_up1)
    received = two_homes(*pair)[2:]
    expert_total = list(expert_rows(received, 2, True, expert_rows(pair, 2, False))) + down_total
    dense_out = (
        small[experts_all],
        query,
        key,
        value,
        out,
        small[experts_all + 1],
        small[:experts_all].T,
    )
    return (
        (edge_out,)
        + tuple((piece[None] for piece in dense_out))
        + tuple((piece[None] for piece in expert_total))
    )


def solution(mesh):
    section, expert, dp = "section", "expert", "dp"
    tokens = P(section, None, expert, dp, None)
    vector, matrix = P(section, None), P(section, None, None)
    rows = P(section, expert, dp, None)
    dense = (vector, matrix, matrix, matrix, matrix, vector, matrix)
    return jax.shard_map(
        local,
        mesh=mesh,
        in_specs=(tokens, P(None, expert, None), tokens, tokens) + dense + (rows, rows, rows),
        out_specs=(tokens,) + dense + (rows, rows, rows),
        check_vma=False,
    )
```
